32 devices in a mesh: ctx: 2 (over x), tp: 4 (over y, core), rep: 4 (over z).
Axes of the slice: x: 2, y: 2, z: 4, core: 2. Of those that a mesh axis runs over, the one named last changes fastest.
Arguments:
- spikes: int32 [8, 512, 3584], P('rep', 'ctx'), may hold values from 0 to 4
- dec_spikes: int32 [4, 8, 3584], P(None, 'rep'), may hold values from 0 to 4
- thresholds: int32 [3584], replicated, may hold values from 1 to 3
- in_scale: float32 [3584], replicated, may hold values from 0.3 to 3
- qkv_weight: bfloat16 [3, 3584, 2048], P(None, ('ctx', 'rep'), 'tp'), may hold values from -0.09375 to 0.09375
- out_weight: bfloat16 [2048, 3584], P('tp', ('ctx', 'rep')), may hold values from -0.1875 to 0.1875
- head_gain: float32 [16, 128], P('tp'), may hold values from 0.5 to 2
- prior_state: float32 [8, 16, 128, 128], P('rep', 'tp'), may hold values from -256 to 256
- lengths: int32 [8], P('rep'), may hold values from 128 to 512, as said below
Outputs:
- block_out: bfloat16 [8, 512, 3584], P('rep', 'ctx', 'tp')
- decode_out: bfloat16 [4, 8, 3584], P(None, 'rep', 'tp')
The draws below stay inside these ranges and needn't reach their ends.
Inputs may be any that keep to these rules, and one draw needn't show every extreme that they name: `lengths`: one request in every draw has a full block of 512 prompt positions.
All inputs are finite; a program needn't handle non-finite values.
Results may differ from the reference program's by a relative error of at most 0.012.
Values may be sent and summed in bfloat16 or wider, within the bound.
No kernel may reach another device: no remote copies, remote signals or barrier semaphores. Data moves between devices by JAX's collectives and lax.ppermute only.
A program may use at most 128 MiB of HBM per device.

```python
import math
import jax
import jax.numpy as jnp
from jax import lax

D = 3584
HEAD = 128
BLK = 256
STEPS = 4
HEADS = 16
LEN = 512
REQS = 8
N_CTX = 2


def draw_lengths(key, part):
    first, second = jax.random.split(key)
    value_rows = jax.random.randint(first, (REQS,), LEN // 4, LEN + 1)
    which = jax.random.randint(second, (), 0, REQS)
    return jnp.where(jnp.arange(REQS) == which, LEN, value_rows).astype(jnp.int32)


def with_ends(drawn, rng, least, largest):
    longest = drawn.shape.index(max(drawn.shape))
    spots = []
    for shift in (0, 1):
        where = [jax.random.randint(jax.random.fold_in(rng, axis), (), 0, length) for axis, length in enumerate(drawn.shape)]
        where[longest] = (where[longest] + shift) % drawn.shape[longest]
        spots.append(tuple(where))
    return drawn.at[spots[0]].set(least).at[spots[1]].set(largest)


def strengthened(drawn, own_key, source, target, blocks, factor):
    owner, partner = [(jnp.arange(drawn.shape[position]) // (drawn.shape[position] // blocks)).reshape([-1 if axis == position else 1 for axis in range(drawn.ndim)]) for position in (source, target)]
    chosen = jax.random.permutation(own_key, blocks)[partner]
    strong = (owner == chosen) | (owner == (partner + blocks // 2) % blocks)
    return jnp.where(strong, factor * drawn, drawn)


def levels(key, extent, pieces, least, high):
    def one(dim, shards_of):
        heights = jax.random.uniform(jax.random.fold_in(jax.random.fold_in(key, 6), dim), (shards_of,), jnp.float32, least / len(pieces), high / len(pieces))
        return jnp.repeat(jnp.exp(heights), extent[dim] // shards_of).reshape((-1,) + (1,) * (len(extent) - dim - 1))

    level = one(*pieces[0])
    for cut in pieces[1:]:
        level = level * one(*cut)
    return level


def centred(own_key, dims, deviation, most, pieces=(), kind=jnp.bfloat16):
    entries = deviation * jax.random.normal(own_key, dims, jnp.float32)
    if pieces:
        entries = entries * levels(own_key, dims, pieces, -0.22, 0.18)
    return jnp.clip(entries, -most, most).astype(kind)


def gaussian_with(rng, dims, spread, most, shards, heavy, held_as=jnp.bfloat16):
    result = spread * jax.random.normal(rng, dims, jnp.float32)
    if shards:
        result = result * levels(rng, dims, shards, -0.22, 0.18)
    return jnp.clip(strengthened(result, jax.random.fold_in(rng, 3), *heavy), -most, most).astype(held_as)


def setup_inputs(seed: int = 0) -> dict:
    key_list = jax.random.split(jax.random.key(seed), 10)
    return {
        "spikes": with_ends(jax.random.randint(key_list[0], (REQS, LEN, D), 0, 5), jax.random.fold_in(key_list[0], 1), 0, 4).astype(jnp.int32),
        "dec_spikes": with_ends(jax.random.randint(key_list[1], (STEPS, REQS, D), 0, 5), jax.random.fold_in(key_list[1], 1), 0, 4).astype(jnp.int32),
        "thresholds": with_ends(jax.random.randint(key_list[2], (D,), 1, 4), jax.random.fold_in(key_list[2], 1), 1, 3).astype(jnp.int32),
        "in_scale": jnp.clip(jnp.exp(jax.random.uniform(key_list[3], (D,), jnp.float32, math.log(0.3), math.log(3.0))), 0.3, 3.0),
        "qkv_weight": centred(key_list[4], (3, D, HEADS * HEAD), D ** -0.5, 0.09375, ((1, 8), (2, 4))),
        "out_weight": gaussian_with(key_list[5], (HEADS * HEAD, D), (HEADS * HEAD) ** -0.5, 0.1875, ((0, 4), (1, 8)), (0, 1, 8, 2.0)),
        "head_gain": jnp.clip(jnp.exp(math.log(2.0) - 1.3862944 * jax.random.uniform(key_list[6], (HEADS, HEAD), jnp.float32) ** levels(key_list[6], (HEADS, HEAD), ((0, 4),), -0.2, 0.2)), 0.5, 2.0),
        "prior_state": centred(key_list[7], (REQS, HEADS, HEAD, HEAD), (2.0 * BLK ** 0.5), 256.0, ((0, 4), (1, 4)), jnp.float32),
        "lengths": draw_lengths(jax.random.fold_in(key_list[9], 71), 0),
    }


def normalize(value_rows, gain):
    mean = lax.optimization_barrier(jnp.mean(value_rows * value_rows, axis=-1, keepdims=True))
    return (value_rows * lax.rsqrt(mean + 1e-06) * gain).astype(jnp.bfloat16)

def reference(spikes, dec_spikes, thresholds, in_scale, qkv_weight, out_weight, head_gain, prior_state, lengths):
    heads = HEADS
    head = HEAD
    blocks = N_CTX
    block = LEN // blocks
    topmost_precision = lax.Precision.HIGHEST

    def embed(counts):
        gated = jnp.where(counts >= thresholds, counts, 0)
        return (gated.astype(jnp.float32) * in_scale).astype(jnp.bfloat16)

    def apply_projection(rows):
        parts = [jnp.dot(rows, qkv_weight[i], preferred_element_type=jnp.float32) for i in range(3)]
        return lax.optimization_barrier(jnp.stack(parts, 1).astype(jnp.bfloat16))

    def single(item):
        counts, dec_counts, prior, length = item
        tokens_x = embed(counts)
        dec_x = embed(dec_counts)
        proj = apply_projection(tokens_x).reshape(LEN, 3, heads, head)
        query = proj[:, 0]
        value_rows = proj[:, 2]
        live = jnp.arange(LEN) < length
        keys = jnp.where(live[:, None, None], proj[:, 1], jnp.zeros_like(proj[:, 1]))
        q_four = query.astype(jnp.float32).reshape(blocks, block, heads, head)
        k_four = keys.astype(jnp.float32).reshape(blocks, block, heads, head)
        v_four = value_rows.astype(jnp.float32).reshape(blocks, block, heads, head)
        block_state = jnp.einsum('bthk,bthv->bhkv', k_four, v_four)
        running = jnp.cumsum(block_state, axis=0)
        before = jnp.concatenate([jnp.zeros_like(block_state[:1]), running[:-1]], 0)
        carried = lax.optimization_barrier((prior[None] + before).astype(jnp.bfloat16)).astype(jnp.float32)
        inter = jnp.einsum('bthk,bhkv->bthv', q_four, carried)
        scores = jnp.einsum('bthk,bshk->bhts', q_four, k_four)
        causal = jnp.arange(block)[:, None] >= jnp.arange(block)[None, :]
        weights = lax.optimization_barrier(jnp.where(causal, scores, 0.0).astype(jnp.bfloat16)).astype(jnp.float32)
        intra = jnp.einsum('bhts,bshv->bthv', weights, v_four)
        hidden = normalize(inter + intra, head_gain).reshape(LEN, heads * head)
        memory_state = prior + lax.optimization_barrier(jnp.sum(block_state, axis=0))
        decode_projection_matrix = apply_projection(dec_x).reshape(STEPS, 3, heads, head).astype(jnp.float32)
        state_readouts = []
        for decode_step_body in range(STEPS):
            memory_state = memory_state + jnp.einsum('dl,dn->dln', decode_projection_matrix[decode_step_body, 1], decode_projection_matrix[decode_step_body, 2], precision=topmost_precision)
            state_readouts.append(jnp.einsum('jd,jdq->jq', decode_projection_matrix[decode_step_body, 0], memory_state, precision=topmost_precision))
        dec_hidden = normalize(jnp.stack(state_readouts), head_gain).reshape(STEPS, heads * head)
        block_out = (tokens_x.astype(jnp.float32) + jnp.dot(hidden, out_weight, preferred_element_type=jnp.float32)).astype(jnp.bfloat16)
        dec_out = (dec_x.astype(jnp.float32) + jnp.dot(dec_hidden, out_weight, preferred_element_type=jnp.float32)).astype(jnp.bfloat16)
        return (block_out, dec_out)
    block_out, dec_out = lax.map(single, (spikes, jnp.transpose(dec_spikes, (1, 0, 2)), prior_state, lengths))
    return (block_out, jnp.transpose(dec_out, (1, 0, 2)))
```

```python
import jax
import jax.numpy as jnp
from jax import lax
from jax.experimental import pallas as pl
from jax.experimental.pallas import tpu as pltpu
from jax.sharding import PartitionSpec as P


def carried_in(value, axis, combine, identity):
    peers, here = (lax.axis_size(axis), lax.axis_index(axis))
    everything = lax.all_gather(value, axis)
    start = jnp.broadcast_to(jnp.asarray(identity, value.dtype), value.shape)

    def turn(k, before):
        reached = k < here
        new = combine(before, everything[k])
        return jnp.where(reached, new, before)

    return lax.fori_loop(0, peers, turn, start)


def normalize(value_rows, gain):
    mean = jnp.mean(value_rows * value_rows, axis=-1, keepdims=True)
    return (value_rows * lax.rsqrt(mean + 1e-06) * gain).astype(jnp.bfloat16)


def local_any(
    spikes,
    dec_spikes,
    thresholds,
    in_scale,
    qkv_weight,
    out_weight,
    head_gain,
    prior_state,
    lengths,
):
    groups, block, width = spikes.shape
    steps = dec_spikes.shape[0]
    heads, head = head_gain.shape
    inner = heads * head
    prompt_rows = groups * block
    topmost_precision = lax.Precision.HIGHEST
    context_position = lax.axis_index("ctx")
    tokens_x = (jnp.where(spikes >= thresholds, spikes, 0).astype(jnp.float32) * in_scale).astype(
        jnp.bfloat16
    )
    dec_x = (
        jnp.where(dec_spikes >= thresholds, dec_spikes, 0).astype(jnp.float32) * in_scale
    ).astype(jnp.bfloat16)
    rows_all = jnp.concatenate(
        [tokens_x.reshape(prompt_rows, width), dec_x.reshape(steps * groups, width)], 0
    )
    full = lax.all_gather(qkv_weight, ("ctx", "rep"), axis=1, tiled=True)
    projected = jnp.einsum("rd,cde->rce", rows_all, full, preferred_element_type=jnp.float32)
    projected = projected.astype(jnp.bfloat16)
    prompt = projected[:prompt_rows].reshape(groups, block, 3, heads, head)
    decoded = projected[prompt_rows:].reshape(steps, groups, 3, heads, head)
    query = prompt[:, :, 0]
    value_rows = prompt[:, :, 2]
    positions = context_position * block + jnp.arange(block)
    live = positions[None, :] < lengths[:, None]
    keys = jnp.where(live[:, :, None, None], prompt[:, :, 1], jnp.zeros_like(prompt[:, :, 1]))
    block_state = jnp.einsum(
        "gthk,gthv->ghkv", keys, value_rows, preferred_element_type=jnp.float32
    )
    before = carried_in(
        block_state, "ctx", lambda earlier, later: earlier + later, jnp.zeros_like(block_state)
    )
    carried = (prior_state + before).astype(jnp.bfloat16)
    inter = jnp.einsum("gthk,ghkv->gthv", query, carried, preferred_element_type=jnp.float32)
    scores = jnp.einsum("gthk,gshk->ghts", query, keys, preferred_element_type=jnp.float32)
    causal = jnp.arange(block)[:, None] >= jnp.arange(block)[None, :]
    weights = jnp.where(causal, scores, 0.0).astype(jnp.bfloat16)
    intra = jnp.einsum("ghts,gshv->gthv", weights, value_rows, preferred_element_type=jnp.float32)
    hidden = normalize(inter + intra, head_gain).reshape(prompt_rows, inner)
    dec_query = decoded[:, :, 0].astype(jnp.float32)
    dec_keys = decoded[:, :, 1].astype(jnp.float32)
    dec_values = decoded[:, :, 2].astype(jnp.float32)
    state_readouts = []
    memory_state = prior_state + lax.psum(block_state, "ctx")
    for decode_step_body in range(steps):
        memory_state = memory_state + jnp.einsum(
            "ghk,ghv->ghkv",
            dec_keys[decode_step_body],
            dec_values[decode_step_body],
            precision=topmost_precision,
        )
        state_readouts.append(
            jnp.einsum(
                "ghk,ghkv->ghv",
                dec_query[decode_step_body],
                memory_state,
                precision=topmost_precision,
            )
        )
    dec_hidden = normalize(jnp.stack(state_readouts), head_gain).reshape(steps * groups, inner)
    hidden_all = jnp.concatenate([hidden, dec_hidden], 0)
    columns = width // lax.axis_size("tp")
    residual = lax.dynamic_slice_in_dim(rows_all, lax.axis_index("tp") * columns, columns, 1)
    terms = jnp.dot(
        hidden_all,
        lax.all_gather(out_weight, ("ctx", "rep"), axis=1, tiled=True),
        preferred_element_type=jnp.float32,
    )
    summed = lax.psum_scatter(terms, "tp", scatter_dimension=1, tiled=True)
    result = (residual.astype(jnp.float32) + summed).astype(jnp.bfloat16)
    block_out = result[:prompt_rows].reshape(groups, block, columns)
    decode_out = result[prompt_rows:].reshape(steps, groups, columns)
    return (block_out, decode_out)


AXES = ("ctx", "tp", "rep")
VMEM_LIMIT = 60 * 1024 * 1024
DEC_PAD = 16


def fits(mesh):
    shape = dict(mesh.shape)
    return (shape["ctx"], shape["tp"], shape["rep"]) == (2, 4, 4)


def move(value, target):
    sizes = [lax.axis_size(name) for name in AXES]
    pairs = []
    for c in range(sizes[0]):
        for t in range(sizes[1]):
            for r in range(sizes[2]):
                to = target(c, t, r)
                if to is not None:
                    at = (c * sizes[1] + t) * sizes[2] + r
                    pairs.append((at, (to[0] * sizes[1] + to[1]) * sizes[2] + to[2]))
    return lax.ppermute(value, AXES, pairs)


def to_ctx(c, t, r):
    return (1 - c, t, r)


def to_core(c, t, r):
    return (c, t ^ 1, r)


def to_y(c, t, r):
    return (c, t ^ 2, r)


def to_diagonal(c, t, r):
    return (1 - c, t ^ 2, r)


def to_pair(c, t, r):
    return (c, t, r ^ 1)


def mid_swap(c, t, r):
    return (c, t, 3 - r) if r in (1, 2) else None


def mid_to_end(c, t, r):
    return (c, t, r ^ 1) if r in (1, 2) else None


def params():
    return pltpu.CompilerParams(vmem_limit_bytes=VMEM_LIMIT)


def whole(shape):
    return pl.BlockSpec(shape, lambda *_: (0,) * len(shape))


def embed_kernel(parts, spikes_ref, thresholds_ref, scale_ref, out_ref):
    counts = spikes_ref[...]
    gated = jnp.where(counts >= thresholds_ref[...], counts, 0)
    x = (gated.astype(jnp.float32) * scale_ref[...]).astype(jnp.bfloat16)
    width = x.shape[1] // (2 * parts)
    for z in range(parts):
        first = x[:, z * width : (z + 1) * width]
        second = x[:, (parts + z) * width : (parts + z + 1) * width]
        out_ref[z] = jnp.concatenate([first, second], axis=1)


def embed(spikes, thresholds, scale, parts, tile):
    rows, width = spikes.shape
    return pl.pallas_call(
        lambda *refs: embed_kernel(parts, *refs),
        grid=(rows // tile,),
        in_specs=[
            pl.BlockSpec((tile, width), lambda i: (i, 0)),
            whole((1, width)),
            whole((1, width)),
        ],
        out_specs=pl.BlockSpec((parts, tile, width // parts), lambda i: (0, i, 0)),
        out_shape=jax.ShapeDtypeStruct((parts, rows, width // parts), jnp.bfloat16),
        compiler_params=params(),
        name="embed",
    )(spikes, thresholds[None], scale[None])


def weights_of(scalars, mine, other, index):
    if len(mine) == 2:
        flag = scalars[1] == 1
        own = jnp.where(flag, mine[1][index], mine[0][index])
        far = jnp.where(flag, other[1][index], other[0][index])
    else:
        own, far = mine[0][index], other[0][index]
    first = scalars[0] == 0
    return jnp.concatenate([jnp.where(first, own, far), jnp.where(first, far, own)], axis=0)


def row_blocks(x_refs):
    at = 0
    for ref in x_refs:
        rows = ref.shape[1]
        yield ref, at, rows
        at += rows


def project_kernel(candidates, has_sum, scalars, *refs):
    x_refs = refs[:4]
    mine = refs[4 : 4 + candidates]
    other = refs[4 + candidates : 4 + 2 * candidates]
    out_ref = refs[-1]
    sum_ref = refs[-2] if has_sum else None
    for index in range(3):
        weight = weights_of(scalars, mine, other, index)
        columns = slice(index * weight.shape[1], (index + 1) * weight.shape[1])
        for ref, at, rows in row_blocks(x_refs):
            term = jnp.dot(ref[0], weight, preferred_element_type=jnp.float32)
            if has_sum:
                term = sum_ref[at : at + rows, columns] + term
            out_ref[at : at + rows, columns] = term


def part_spec(array, step):
    block = (1,) + array.shape[1:]
    return pl.BlockSpec(block, lambda i, scalars: (scalars[3 + step], 0, 0))


def project(scalars, step, xs, mine, other, summed):
    rows = sum(x.shape[1] for x in xs)
    columns = 3 * mine[0].shape[2]
    operands = [*xs, *mine, *other]
    in_specs = [part_spec(x, step) for x in xs]
    in_specs += [whole(w.shape) for w in (*mine, *other)]
    if summed is not None:
        operands.append(summed)
        in_specs.append(whole(summed.shape))
    return pl.pallas_call(
        lambda *refs: project_kernel(len(mine), summed is not None, *refs),
        grid_spec=pltpu.PrefetchScalarGridSpec(
            num_scalar_prefetch=1,
            grid=(1,),
            in_specs=in_specs,
            out_specs=whole((rows, columns)),
        ),
        out_shape=jax.ShapeDtypeStruct((rows, columns), jnp.float32),
        compiler_params=params(),
        cost_estimate=pl.CostEstimate(
            flops=2 * rows * columns * xs[0].shape[2], bytes_accessed=8 * rows * columns, transcendentals=0
        ),
        name="project",
    )(scalars, *operands)


def attend_kernel(
    dims, scalars, own_x, first_x, second_x, dec_x, m0, m1, o0, o1, sum_ref, prior_ref, gain_ref, lengths, near_ref, far_ref, qkv
):
    groups, block, heads, head, steps = dims
    for index in range(3):
        weight = weights_of(scalars, (m0, m1), (o0, o1), index)
        columns = slice(index * weight.shape[1], (index + 1) * weight.shape[1])
        for ref, at, rows in row_blocks((own_x, first_x, second_x, dec_x)):
            term = jnp.dot(ref[0], weight, preferred_element_type=jnp.float32)
            qkv[at : at + rows, columns] = (sum_ref[at : at + rows, columns] + term).astype(jnp.bfloat16)
    here = scalars[0]
    parity = scalars[2]
    wide = heads * head
    prompt = 2 * groups * block
    causal = lax.broadcasted_iota(jnp.int32, (block, block), 0) >= lax.broadcasted_iota(jnp.int32, (block, block), 1)
    position = lax.broadcasted_iota(jnp.int32, (block, head), 0)
    row = lax.broadcasted_iota(jnp.int32, (DEC_PAD, DEC_PAD), 0)
    column = lax.broadcasted_iota(jnp.int32, (DEC_PAD, DEC_PAD), 1)
    reach = (row % groups == column % groups) & (column <= row)
    exact = lax.Precision.HIGHEST
    inner = (((0,), (0,)), ((), ()))
    across = (((1,), (1,)), ((), ()))

    def finish(value, gain):
        mean = jnp.mean(value * value, axis=-1, keepdims=True)
        return (value * lax.rsqrt(mean + 1e-06) * gain).astype(jnp.bfloat16)

    for h in range(heads):
        cols = [slice(i * wide + h * head, i * wide + (h + 1) * head) for i in range(3)]
        gain = gain_ref[h : h + 1, :]
        dq = qkv[prompt : prompt + DEC_PAD, cols[0]]
        dk = qkv[prompt : prompt + DEC_PAD, cols[1]]
        dv = qkv[prompt : prompt + DEC_PAD, cols[2]].astype(jnp.float32)
        dq32 = dq.astype(jnp.float32)
        pairs = lax.dot_general(dq, dk, across, preferred_element_type=jnp.float32)
        read = jnp.dot(jnp.where(reach, pairs, 0.0), dv, precision=exact, preferred_element_type=jnp.float32)
        dec_group = lax.broadcasted_iota(jnp.int32, (DEC_PAD, head), 0) % groups
        for r in range(groups):
            prior = prior_ref[r, h]
            starts = (r * block, groups * block + pl.multiple_of((r ^ parity) * block, block))
            run = (here, 1 - here)
            keys, values, states = [], [], []
            for start, b in zip(starts, run):
                k = qkv[pl.ds(start, block), cols[1]]
                live = b * block + position < lengths[r]
                k = jnp.where(live, k, jnp.zeros_like(k))
                v = qkv[pl.ds(start, block), cols[2]]
                keys.append(k)
                values.append(v)
                states.append(lax.dot_general(k, v, inner, preferred_element_type=jnp.float32))
            before = (jnp.where(here == 1, states[1], 0.0), jnp.where(here == 0, states[0], 0.0))
            for side, out_ref in enumerate((near_ref, far_ref)):
                q = qkv[pl.ds(starts[side], block), cols[0]]
                carried = (prior + before[side]).astype(jnp.bfloat16)
                scores = lax.dot_general(q, keys[side], across, preferred_element_type=jnp.float32)
                weights = jnp.where(causal, scores, 0.0).astype(jnp.bfloat16)
                attended = jnp.dot(q, carried, preferred_element_type=jnp.float32) + jnp.dot(
                    weights, values[side], preferred_element_type=jnp.float32
                )
                out_ref[r * block : (r + 1) * block, h * head : (h + 1) * head] = finish(attended, gain)
            state = prior + (states[0] + states[1])
            inter = jnp.dot(dq32, state, precision=exact, preferred_element_type=jnp.float32)
            read = read + jnp.where(dec_group == r, inter, 0.0)
        done = finish(read, gain)
        near_ref[groups * block :, h * head : (h + 1) * head] = done
        far_ref[groups * block :, h * head : (h + 1) * head] = done


def attend(scalars, xs, mine, other, summed, prior, gain, lengths, dims):
    groups, block, heads, head, _ = dims
    rows, columns = summed.shape
    shape = (groups * block + DEC_PAD, heads * head)
    in_specs = [part_spec(x, 3) for x in xs]
    in_specs += [whole(w.shape) for w in (*mine, *other, summed)]
    in_specs += [
        pl.BlockSpec((groups, heads, head, head), lambda i, s: (0, s[0], 0, 0)),
        whole(gain.shape),
        pl.BlockSpec(memory_space=pltpu.SMEM),
    ]
    out = jax.ShapeDtypeStruct(shape, jnp.bfloat16)
    return pl.pallas_call(
        lambda *refs: attend_kernel(dims, *refs),
        grid_spec=pltpu.PrefetchScalarGridSpec(
            num_scalar_prefetch=1,
            grid=(1,),
            in_specs=in_specs,
            out_specs=[whole(shape), whole(shape)],
            scratch_shapes=[pltpu.VMEM((rows, columns), jnp.bfloat16)],
        ),
        out_shape=[out, out],
        compiler_params=params(),
        cost_estimate=pl.CostEstimate(
            flops=2 * rows * columns * xs[0].shape[2] * 2, bytes_accessed=4 * rows * columns, transcendentals=0
        ),
        name="attend",
    )(scalars, *xs, *mine, *other, summed, prior, gain, lengths)


def combine_kernel(dims, scalars, *refs):
    prompt, dec = dims
    hidden, weights = refs[:8], refs[8:16]
    res_ref, dec_res_ref, out_ref, dec_ref = refs[16:]
    here_first = scalars[0] == 0
    same = scalars[1] == 1
    total = None
    for i in range(4):
        core, moved = i % 2, i // 2
        def piece(j):
            return jnp.where(same, hidden[core * 4 + j + 2 * moved][...], hidden[core * 4 + j + 2 * (1 - moved)][...])

        near, far = piece(0), piece(1)
        rows = jnp.concatenate([jnp.where(here_first, near, far), jnp.where(here_first, far, near)], axis=1)
        weight = jnp.concatenate([weights[2 * i][...], weights[2 * i + 1][...]], axis=1)
        term = jnp.dot(rows, weight, preferred_element_type=jnp.float32)
        total = term if total is None else total + term
    out_ref[...] = (res_ref[...].astype(jnp.float32) + total[:prompt]).astype(jnp.bfloat16)
    dec_ref[...] = (dec_res_ref[...].astype(jnp.float32) + total[prompt : prompt + dec]).astype(jnp.bfloat16)


def combine(scalars, hidden, weights, res, dec_res):
    operands = [*hidden, *weights, res, dec_res]
    return pl.pallas_call(
        lambda *refs: combine_kernel((res.shape[0], dec_res.shape[0]), *refs),
        grid_spec=pltpu.PrefetchScalarGridSpec(
            num_scalar_prefetch=1,
            grid=(1,),
            in_specs=[whole(a.shape) for a in operands],
            out_specs=[whole(res.shape), whole(dec_res.shape)],
        ),
        out_shape=[
            jax.ShapeDtypeStruct(res.shape, jnp.bfloat16),
            jax.ShapeDtypeStruct(dec_res.shape, jnp.bfloat16),
        ],
        compiler_params=params(),
        name="combine",
    )(scalars, *operands)


def spread(value, is_end):
    pair = move(value, to_pair)
    third_mid = move(value, mid_swap)
    fourth_mid = move(pair, mid_swap)
    third_end = move(third_mid, mid_to_end)
    fourth_end = move(fourth_mid, mid_to_end)
    return (value,), (pair,), (third_mid, third_end), (fourth_mid, fourth_end)


def local_grid(
    spikes, dec_spikes, thresholds, in_scale, qkv_weight, out_weight, head_gain, prior_state, lengths
):
    groups, block, width = spikes.shape
    steps = dec_spikes.shape[0]
    all_heads, head = head_gain.shape
    heads = all_heads // 2
    wide = heads * head
    planes = lax.axis_size("rep")
    c, t, z = (lax.axis_index(name) for name in AXES)
    parity = t % 2
    y = t // 2
    is_end = (z == 0) | (z == planes - 1)
    end = is_end.astype(jnp.int32)
    third = jnp.where(is_end, z ^ 2, z ^ 3)
    fourth = jnp.where(is_end, z ^ 3, z ^ 2)
    scalars = jnp.stack([c, end, parity, z, z ^ 1, third, fourth]).astype(jnp.int32)

    kept = lax.dynamic_slice_in_dim(qkv_weight, c * wide, wide, 2)
    given = lax.dynamic_slice_in_dim(qkv_weight, (1 - c) * wide, wide, 2)
    other = move(given, to_ctx)
    mine_parts = spread(kept, is_end)
    other_parts = spread(other, is_end)

    counts = spikes.reshape(groups * block, width)
    dec_counts = dec_spikes.reshape(steps * groups, width)
    dec_padded = jnp.pad(dec_counts, ((0, DEC_PAD - steps * groups), (0, 0)))
    own_x = embed(counts, thresholds, in_scale, planes, block // 2)
    dec_x = embed(dec_padded, thresholds, in_scale, planes, DEC_PAD)
    first_x = move(lax.dynamic_slice_in_dim(own_x, parity * block, block, 1), to_ctx)
    second_x = move(first_x, to_core)
    xs = (own_x, first_x, second_x, dec_x)

    def meet(c, t, r):
        return (c, t, r) if c == t // 2 else (1 - c, t ^ 2, r)

    out_block = move(out_weight, meet)
    (o_own,), (o_pair,), o_third, o_fourth = spread(out_block, is_end)
    o_third = jnp.where(is_end, o_third[1], o_third[0])
    o_fourth = jnp.where(is_end, o_fourth[1], o_fourth[0])
    z_even = z % 2 == 0
    low = z < 2
    near_half = (jnp.where(z_even, o_own, o_pair), jnp.where(z_even, o_pair, o_own))
    far_half = (jnp.where(low, o_third, o_fourth), jnp.where(low, o_fourth, o_third))
    near_mine = z // 2 == parity
    used = [jnp.where(near_mine, a, b) for a, b in zip(near_half, far_half)]
    passed = [jnp.where(near_mine, b, a) for a, b in zip(near_half, far_half)]
    sibling = [move(p, to_core) for p in passed]
    out_weights = used + sibling + [move(u, to_ctx) for u in used] + [move(s, to_ctx) for s in sibling]

    summed = None
    for step in range(3):
        summed = project(scalars, step, xs, mine_parts[step], other_parts[step], summed)
    gain = lax.dynamic_slice_in_dim(head_gain, c * heads, heads, 0)
    near, far = attend(
        scalars, xs, mine_parts[3], other_parts[3], summed, prior_state, gain, lengths, (groups, block, heads, head, steps)
    )
    mine = [near, move(far, to_ctx), move(near, to_y), move(far, to_diagonal)]
    hidden = mine + [move(m, to_core) for m in mine]

    columns = width // lax.axis_size("tp")

    def gate(rows):
        part = lax.dynamic_slice_in_dim(rows, t * columns, columns, 1)
        level = lax.dynamic_slice_in_dim(thresholds, t * columns, columns, 0)
        scale = lax.dynamic_slice_in_dim(in_scale, t * columns, columns, 0)
        return (jnp.where(part >= level, part, 0).astype(jnp.float32) * scale).astype(jnp.bfloat16)

    flags = jnp.stack([c, (c == y).astype(jnp.int32)]).astype(jnp.int32)
    out, dec_out = combine(flags, hidden, out_weights, gate(counts), gate(dec_counts))
    return out.reshape(groups, block, columns), dec_out.reshape(steps, groups, columns)


def solution(mesh):
    return jax.shard_map(
        local_grid if fits(mesh) else local_any,
        mesh=mesh,
        in_specs=(
            P("rep", "ctx", None),
            P(None, "rep", None),
            P(),
            P(),
            P(None, ("ctx", "rep"), "tp"),
            P("tp", ("ctx", "rep")),
            P("tp", None),
            P("rep", "tp", None, None),
            P("rep"),
        ),
        out_specs=(P("rep", "ctx", "tp"), P(None, "rep", "tp")),
        check_vma=False,
    )
```

```python
import jax
import jax.numpy as jnp
from jax import lax
from jax.experimental import pallas as pl
from jax.experimental.pallas import tpu as pltpu
from jax.sharding import PartitionSpec as P


def carried_in(value, axis, combine, identity):
    peers, here = (lax.axis_size(axis), lax.axis_index(axis))
    everything = lax.all_gather(value, axis)
    start = jnp.broadcast_to(jnp.asarray(identity, value.dtype), value.shape)

    def turn(k, before):
        reached = k < here
        new = combine(before, everything[k])
        return jnp.where(reached, new, before)

    return lax.fori_loop(0, peers, turn, start)


def normalize(value_rows, gain):
    mean = jnp.mean(value_rows * value_rows, axis=-1, keepdims=True)
    return (value_rows * lax.rsqrt(mean + 1e-06) * gain).astype(jnp.bfloat16)


def local_any(
    spikes,
    dec_spikes,
    thresholds,
    in_scale,
    qkv_weight,
    out_weight,
    head_gain,
    prior_state,
    lengths,
):
    groups, block, width = spikes.shape
    steps = dec_spikes.shape[0]
    heads, head = head_gain.shape
    inner = heads * head
    prompt_rows = groups * block
    topmost_precision = lax.Precision.HIGHEST
    context_position = lax.axis_index("ctx")
    tokens_x = (jnp.where(spikes >= thresholds, spikes, 0).astype(jnp.float32) * in_scale).astype(
        jnp.bfloat16
    )
    dec_x = (
        jnp.where(dec_spikes >= thresholds, dec_spikes, 0).astype(jnp.float32) * in_scale
    ).astype(jnp.bfloat16)
    rows_all = jnp.concatenate(
        [tokens_x.reshape(prompt_rows, width), dec_x.reshape(steps * groups, width)], 0
    )
    full = lax.all_gather(qkv_weight, ("ctx", "rep"), axis=1, tiled=True)
    projected = jnp.einsum("rd,cde->rce", rows_all, full, preferred_element_type=jnp.float32)
    projected = projected.astype(jnp.bfloat16)
    prompt = projected[:prompt_rows].reshape(groups, block, 3, heads, head)
    decoded = projected[prompt_rows:].reshape(steps, groups, 3, heads, head)
    query = prompt[:, :, 0]
    value_rows = prompt[:, :, 2]
    positions = context_position * block + jnp.arange(block)
    live = positions[None, :] < lengths[:, None]
    keys = jnp.where(live[:, :, None, None], prompt[:, :, 1], jnp.zeros_like(prompt[:, :, 1]))
    block_state = jnp.einsum(
        "gthk,gthv->ghkv", keys, value_rows, preferred_element_type=jnp.float32
    )
    before = carried_in(
        block_state, "ctx", lambda earlier, later: earlier + later, jnp.zeros_like(block_state)
    )
    carried = (prior_state + before).astype(jnp.bfloat16)
    inter = jnp.einsum("gthk,ghkv->gthv", query, carried, preferred_element_type=jnp.float32)
    scores = jnp.einsum("gthk,gshk->ghts", query, keys, preferred_element_type=jnp.float32)
    causal = jnp.arange(block)[:, None] >= jnp.arange(block)[None, :]
    weights = jnp.where(causal, scores, 0.0).astype(jnp.bfloat16)
    intra = jnp.einsum("ghts,gshv->gthv", weights, value_rows, preferred_element_type=jnp.float32)
    hidden = normalize(inter + intra, head_gain).reshape(prompt_rows, inner)
    dec_query = decoded[:, :, 0].astype(jnp.float32)
    dec_keys = decoded[:, :, 1].astype(jnp.float32)
    dec_values = decoded[:, :, 2].astype(jnp.float32)
    state_readouts = []
    memory_state = prior_state + lax.psum(block_state, "ctx")
    for decode_step_body in range(steps):
        memory_state = memory_state + jnp.einsum(
            "ghk,ghv->ghkv",
            dec_keys[decode_step_body],
            dec_values[decode_step_body],
            precision=topmost_precision,
        )
        state_readouts.append(
            jnp.einsum(
                "ghk,ghkv->ghv",
                dec_query[decode_step_body],
                memory_state,
                precision=topmost_precision,
            )
        )
    dec_hidden = normalize(jnp.stack(state_readouts), head_gain).reshape(steps * groups, inner)
    hidden_all = jnp.concatenate([hidden, dec_hidden], 0)
    columns = width // lax.axis_size("tp")
    residual = lax.dynamic_slice_in_dim(rows_all, lax.axis_index("tp") * columns, columns, 1)
    terms = jnp.dot(
        hidden_all,
        lax.all_gather(out_weight, ("ctx", "rep"), axis=1, tiled=True),
        preferred_element_type=jnp.float32,
    )
    summed = lax.psum_scatter(terms, "tp", scatter_dimension=1, tiled=True)
    result = (residual.astype(jnp.float32) + summed).astype(jnp.bfloat16)
    block_out = result[:prompt_rows].reshape(groups, block, columns)
    decode_out = result[prompt_rows:].reshape(steps, groups, columns)
    return (block_out, decode_out)


AXES = ("ctx", "tp", "rep")
VMEM_LIMIT = 60 * 1024 * 1024
DEC_PAD = 16


def fits(mesh):
    shape = dict(mesh.shape)
    return (shape["ctx"], shape["tp"], shape["rep"]) == (2, 4, 4)


def move(value, target, name="move"):
    sizes = [lax.axis_size(name) for name in AXES]
    pairs = []
    for c in range(sizes[0]):
        for t in range(sizes[1]):
            for r in range(sizes[2]):
                to = target(c, t, r)
                if to is not None:
                    at = (c * sizes[1] + t) * sizes[2] + r
                    pairs.append((at, (to[0] * sizes[1] + to[1]) * sizes[2] + to[2]))
    with jax.named_scope(name):
        return lax.ppermute(value, AXES, pairs)


def after(value, *earlier):
    return lax.optimization_barrier((value, *earlier))[0]


def to_ctx(c, t, r):
    return (1 - c, t, r)


def to_core(c, t, r):
    return (c, t ^ 1, r)


def to_y(c, t, r):
    return (c, t ^ 2, r)


def to_diagonal(c, t, r):
    return (1 - c, t ^ 2, r)


def to_pair(c, t, r):
    return (c, t, r ^ 1)


def mid_swap(c, t, r):
    return (c, t, 3 - r) if r in (1, 2) else None


def mid_to_end(c, t, r):
    return (c, t, r ^ 1) if r in (1, 2) else None


def params():
    return pltpu.CompilerParams(vmem_limit_bytes=VMEM_LIMIT)


def whole(shape):
    return pl.BlockSpec(shape, lambda *_: (0,) * len(shape))


def split_kernel(scalars, kept_in, given_in, out_in, kept_ref, given_ref):
    kinds = kept_in.shape[0]
    kept_ref[:kinds] = kept_in[...]
    given_ref[...] = given_in[...]
    wide = kept_ref.shape[2]
    for half in range(kept_ref.shape[0] - kinds):
        kept_ref[kinds + half] = out_in[:, half * wide : (half + 1) * wide]


def split(scalars, weight, out_weight):
    kinds, rows, columns = weight.shape
    wide = columns // 2
    half = (kinds, rows, wide)
    kept = (kinds + out_weight.shape[1] // wide, rows, wide)
    return pl.pallas_call(
        split_kernel,
        grid_spec=pltpu.PrefetchScalarGridSpec(
            num_scalar_prefetch=1,
            grid=(1,),
            in_specs=[
                pl.BlockSpec(half, lambda i, s: (0, 0, s[0])),
                pl.BlockSpec(half, lambda i, s: (0, 0, 1 - s[0])),
                whole(out_weight.shape),
            ],
            out_specs=[whole(kept), whole(half)],
        ),
        out_shape=[jax.ShapeDtypeStruct(kept, weight.dtype), jax.ShapeDtypeStruct(half, weight.dtype)],
        compiler_params=params(),
        name="split",
    )(scalars, weight, weight, out_weight)


def embed_kernel(parts, spikes_ref, thresholds_ref, scale_ref, out_ref):
    place(parts, spikes_ref[...], thresholds_ref, scale_ref, out_ref)


def embed_steps_kernel(parts, spikes_ref, thresholds_ref, scale_ref, out_ref):
    steps, groups, width = spikes_ref.shape
    rows = [spikes_ref[step] for step in range(steps)]
    rows.append(jnp.zeros((DEC_PAD - steps * groups, width), spikes_ref.dtype))
    place(parts, jnp.concatenate(rows, axis=0), thresholds_ref, scale_ref, out_ref)


def embed_steps(spikes, thresholds, scale, parts):
    width = spikes.shape[2]
    return pl.pallas_call(
        lambda *refs: embed_steps_kernel(parts, *refs),
        out_shape=jax.ShapeDtypeStruct((parts, DEC_PAD, width // parts), jnp.bfloat16),
        compiler_params=params(),
        name="embed_steps",
    )(spikes, thresholds, scale)


def place(parts, counts, thresholds_ref, scale_ref, out_ref):
    gated = jnp.where(counts >= thresholds_ref[...][None], counts, 0)
    x = (gated.astype(jnp.float32) * scale_ref[...][None]).astype(jnp.bfloat16)
    width = x.shape[1] // (2 * parts)
    for z in range(parts):
        first = x[:, z * width : (z + 1) * width]
        second = x[:, (parts + z) * width : (parts + z + 1) * width]
        out_ref[z] = jnp.concatenate([first, second], axis=1)


def embed(spikes, thresholds, scale, parts, tile):
    rows, width = spikes.shape
    return pl.pallas_call(
        lambda *refs: embed_kernel(parts, *refs),
        grid=(rows // tile,),
        in_specs=[
            pl.BlockSpec((tile, width), lambda i: (i, 0)),
            whole((width,)),
            whole((width,)),
        ],
        out_specs=pl.BlockSpec((parts, tile, width // parts), lambda i: (0, i, 0)),
        out_shape=jax.ShapeDtypeStruct((parts, rows, width // parts), jnp.bfloat16),
        compiler_params=params(),
        name="embed",
    )(spikes, thresholds, scale)


def weights_of(scalars, mine, other, index):
    def pick(refs):
        return refs[0][index] if len(refs) == 1 else jnp.where(scalars[1] == 1, refs[1][index], refs[0][index])

    own, far = pick(mine), pick(other)
    first = scalars[0] == 0
    return jnp.concatenate([jnp.where(first, own, far), jnp.where(first, far, own)], axis=0)


def row_blocks(x_refs):
    at = 0
    for ref in x_refs:
        rows = ref.shape[1]
        yield ref, at, rows
        at += rows


def project_kernel(steps, has_sum, scalars, *refs):
    x_refs, out_ref = refs[:4], refs[-1]
    mine, other = refs[4 : 4 + steps], refs[4 + steps : 4 + 2 * steps]
    for step in range(steps):

        @pl.when(pl.program_id(0) == step)
        def _(step=step):
            for index in range(3):
                weight = weights_of(scalars, mine[step : step + 1], other[step : step + 1], index)
                columns = slice(index * weight.shape[1], (index + 1) * weight.shape[1])
                for ref, at, rows in row_blocks(x_refs):
                    term = jnp.dot(ref[0], weight, preferred_element_type=jnp.float32)
                    if step or has_sum:
                        term = (out_ref if step else refs[-2])[at : at + rows, columns] + term
                    out_ref[at : at + rows, columns] = term


def part_spec(array, step):
    block = (1,) + array.shape[1:]
    return pl.BlockSpec(block, lambda i, scalars: (scalars[3 + step + i], 0, 0))


def project(scalars, first, xs, mine, other, summed):
    steps = len(mine)
    rows = sum(x.shape[1] for x in xs)
    columns = 3 * mine[0].shape[2]
    earlier = [] if summed is None else [summed]
    return pl.pallas_call(
        lambda *refs: project_kernel(steps, bool(earlier), *refs),
        grid_spec=pltpu.PrefetchScalarGridSpec(
            num_scalar_prefetch=1,
            grid=(steps,),
            in_specs=[part_spec(x, first) for x in xs]
            + [whole(other[0].shape) for _ in (*mine, *other)]
            + [whole(sums.shape) for sums in earlier],
            out_specs=whole((rows, columns)),
        ),
        out_shape=jax.ShapeDtypeStruct((rows, columns), jnp.float32),
        compiler_params=params(),
        name="project",
    )(scalars, *xs, *mine, *other, *earlier)


def attend_kernel(
    dims, scalars, own_x, first_x, second_x, dec_x, mine, other0, other1, sum_ref, prior_ref, gain_ref, lengths, near_ref, far_ref, qkv
):
    groups, block, heads, head, steps = dims
    for index in range(3):
        weight = weights_of(scalars, (mine,), (other0, other1), index)
        columns = slice(index * weight.shape[1], (index + 1) * weight.shape[1])
        for ref, at, rows in row_blocks((own_x, first_x, second_x, dec_x)):
            term = jnp.dot(ref[0], weight, preferred_element_type=jnp.float32)
            qkv[at : at + rows, columns] = (sum_ref[at : at + rows, columns] + term).astype(jnp.bfloat16)
    here = scalars[0]
    parity = scalars[2]
    wide = heads * head
    prompt = 2 * groups * block
    causal = lax.broadcasted_iota(jnp.int32, (block, block), 0) >= lax.broadcasted_iota(jnp.int32, (block, block), 1)
    position = lax.broadcasted_iota(jnp.int32, (block, head), 0)
    row = lax.broadcasted_iota(jnp.int32, (DEC_PAD, DEC_PAD), 0)
    column = lax.broadcasted_iota(jnp.int32, (DEC_PAD, DEC_PAD), 1)
    reach = (row % groups == column % groups) & (column <= row)
    exact = lax.Precision.HIGHEST
    inner = (((0,), (0,)), ((), ()))
    across = (((1,), (1,)), ((), ()))

    def finish(value, gain):
        mean = jnp.mean(value * value, axis=-1, keepdims=True)
        return (value * lax.rsqrt(mean + 1e-06) * gain).astype(jnp.bfloat16)

    for h in range(heads):
        cols = [slice(i * wide + h * head, i * wide + (h + 1) * head) for i in range(3)]
        gain = gain_ref[h : h + 1, :]
        dq = qkv[prompt : prompt + DEC_PAD, cols[0]]
        dk = qkv[prompt : prompt + DEC_PAD, cols[1]]
        dv = qkv[prompt : prompt + DEC_PAD, cols[2]].astype(jnp.float32)
        dq32 = dq.astype(jnp.float32)
        pairs = lax.dot_general(dq, dk, across, preferred_element_type=jnp.float32)
        read = jnp.dot(jnp.where(reach, pairs, 0.0), dv, precision=exact, preferred_element_type=jnp.float32)
        dec_group = lax.broadcasted_iota(jnp.int32, (DEC_PAD, head), 0) % groups
        for r in range(groups):
            prior = prior_ref[r, h]
            starts = (r * block, groups * block + pl.multiple_of((r ^ parity) * block, block))
            run = (here, 1 - here)
            keys, values, states = [], [], []
            for start, b in zip(starts, run):
                k = qkv[pl.ds(start, block), cols[1]]
                live = b * block + position < lengths[r]
                k = jnp.where(live, k, jnp.zeros_like(k))
                v = qkv[pl.ds(start, block), cols[2]]
                keys.append(k)
                values.append(v)
                states.append(lax.dot_general(k, v, inner, preferred_element_type=jnp.float32))
            before = (jnp.where(here == 1, states[1], 0.0), jnp.where(here == 0, states[0], 0.0))
            for side, out_ref in enumerate((near_ref, far_ref)):
                q = qkv[pl.ds(starts[side], block), cols[0]]
                carried = (prior + before[side]).astype(jnp.bfloat16)
                scores = lax.dot_general(q, keys[side], across, preferred_element_type=jnp.float32)
                weights = jnp.where(causal, scores, 0.0).astype(jnp.bfloat16)
                attended = jnp.dot(q, carried, preferred_element_type=jnp.float32) + jnp.dot(
                    weights, values[side], preferred_element_type=jnp.float32
                )
                out_ref[r * block : (r + 1) * block, h * head : (h + 1) * head] = finish(attended, gain)
            state = prior + (states[0] + states[1])
            inter = jnp.dot(dq32, state, precision=exact, preferred_element_type=jnp.float32)
            read = read + jnp.where(dec_group == r, inter, 0.0)
        done = finish(read, gain)
        near_ref[groups * block :, h * head : (h + 1) * head] = done
        far_ref[groups * block :, h * head : (h + 1) * head] = done


def attend(scalars, xs, mine, other, summed, prior, gain, lengths, dims):
    groups, block, heads, head, _ = dims
    rows, columns = summed.shape
    shape = (groups * block + DEC_PAD, heads * head)
    in_specs = [part_spec(x, 3) for x in xs]
    in_specs += [whole(other[0].shape) for _ in (*mine, *other)] + [whole(summed.shape)]
    in_specs += [
        pl.BlockSpec((groups, heads, head, head), lambda i, s: (0, s[0], 0, 0)),
        whole(gain.shape),
        pl.BlockSpec(memory_space=pltpu.SMEM),
    ]
    out = jax.ShapeDtypeStruct(shape, jnp.bfloat16)
    return pl.pallas_call(
        lambda *refs: attend_kernel(dims, *refs),
        grid_spec=pltpu.PrefetchScalarGridSpec(
            num_scalar_prefetch=1,
            grid=(1,),
            in_specs=in_specs,
            out_specs=[whole(shape), whole(shape)],
            scratch_shapes=[pltpu.VMEM((rows, columns), jnp.bfloat16)],
        ),
        out_shape=[out, out],
        compiler_params=params(),
        cost_estimate=pl.CostEstimate(
            flops=2 * rows * columns * xs[0].shape[2] * 2, bytes_accessed=4 * rows * columns, transcendentals=0
        ),
        name="attend",
    )(scalars, *xs, *mine, *other, summed, prior, gain, lengths)


def combine_kernel(scalars, *refs):
    hidden, blocks = refs[:8], refs[8:12]
    res_ref, dec_res_ref, out_ref, dec_ref, rows, weights, hidden_sems, weight_sems = refs[12:]
    wide = hidden[0].shape[1]

    def hidden_copy(i, j):
        part = scalars[0] if j == 0 else 1 - scalars[0]
        at = pl.ds(pl.multiple_of((2 * i + part) * wide, wide), wide)
        source = hidden[4 * (i % 2) + 2 * (i // 2) + j]
        return pltpu.make_async_copy(source, rows.at[:, at], hidden_sems.at[i, j])

    def weight_copy(i, slot, part, plane):
        source = blocks[2 * (plane // 2) + i % 2].at[i // 2, plane % 2, part]
        at = pl.ds((2 * i + part) * wide, wide)
        return pltpu.make_async_copy(source, weights.at[slot, :, at], weight_sems.at[i, slot, part])

    every = [(i, slot, part) for slot in range(2) for i in range(4) for part in range(2)]
    for i in range(4):
        for j in range(2):
            hidden_copy(i, j).start()
    for chosen, planes in enumerate(((0, 1), (1, 0), (2, 3), (3, 2))):

        @pl.when(scalars[1] == chosen)
        def _(planes=planes):
            for i, slot, part in every:
                weight_copy(i, slot, part, planes[slot]).start()

    for i in range(4):
        for j in range(2):
            hidden_copy(i, j).wait()
    total = []
    for slot in range(2):
        for i, at, part in every:
            if at == slot:
                weight_copy(i, slot, part, 0).wait()
        total.append(
            lax.dot_general(rows[...], weights[slot], (((1,), (1,)), ((), ())), preferred_element_type=jnp.float32)
        )
    total = jnp.concatenate(total, axis=1)
    groups, block = out_ref.shape[:2]
    for r in range(groups):
        out_ref[r] = (res_ref[r].astype(jnp.float32) + total[r * block : (r + 1) * block]).astype(jnp.bfloat16)
    for step in range(dec_ref.shape[0]):
        at = groups * block + step * groups
        dec_ref[step] = (dec_res_ref[step].astype(jnp.float32) + total[at : at + groups]).astype(jnp.bfloat16)


def combine(scalars, hidden, blocks, res, dec_res):
    anywhere = pl.BlockSpec(memory_space=pl.ANY)
    return pl.pallas_call(
        combine_kernel,
        grid_spec=pltpu.PrefetchScalarGridSpec(
            num_scalar_prefetch=1,
            grid=(1,),
            in_specs=[anywhere] * (len(hidden) + len(blocks))
            + [whole(res.shape), whole(dec_res.shape)],
            out_specs=[whole(res.shape), whole(dec_res.shape)],
            scratch_shapes=[
                pltpu.VMEM((hidden[0].shape[0], 8 * hidden[0].shape[1]), jnp.bfloat16),
                pltpu.VMEM((2, blocks[0].shape[3], 8 * blocks[0].shape[4]), jnp.bfloat16),
                pltpu.SemaphoreType.DMA((4, 2)),
                pltpu.SemaphoreType.DMA((4, 2, 2)),
            ],
        ),
        out_shape=[
            jax.ShapeDtypeStruct(res.shape, jnp.bfloat16),
            jax.ShapeDtypeStruct(dec_res.shape, jnp.bfloat16),
        ],
        compiler_params=params(),
        name="combine",
    )(scalars, *hidden, *blocks, res, dec_res)


def local_grid(
    spikes, dec_spikes, thresholds, in_scale, qkv_weight, out_weight, head_gain, prior_state, lengths
):
    groups, block, width = spikes.shape
    steps = dec_spikes.shape[0]
    all_heads, head = head_gain.shape
    heads = all_heads // 2
    planes = lax.axis_size("rep")
    c, t, z = (lax.axis_index(name) for name in AXES)
    parity = t & 1
    y = t >> 1
    is_end = (z == 0) | (z == planes - 1)
    end = is_end.astype(jnp.int32)
    third = jnp.where(is_end, z ^ 2, z ^ 3)
    fourth = jnp.where(is_end, z ^ 3, z ^ 2)
    scalars = jnp.stack([c, end, parity, z, z ^ 1, third, fourth]).astype(jnp.int32)

    def meet(c, t, r):
        return (1 - c, t, r) if c == t // 2 else (c, t ^ 2, r)

    def corner(c, t, r):
        return None if c == t // 2 else (1 - c, t ^ 2, r)

    def near_pass(c, t, r):
        return None if t % 2 == r // 2 else (c, t ^ 1, r)

    def far_pass(c, t, r):
        return (c, t ^ 1, r) if t % 2 == r // 2 else None

    kept, given = split(scalars, qkv_weight, out_weight.T)
    pair_kept = move(kept, to_pair, "pair_kept")
    mid1_kept = move(kept, mid_swap, "mid1_kept")
    other = move(given, to_ctx, "pre_w")

    counts = spikes.reshape(groups * block, width)
    own_x = embed(counts, thresholds, in_scale, planes, block // 4)
    given_x = lax.dynamic_slice_in_dim(own_x, parity * block, block, 1)

    first_x = move(after(given_x, other), to_ctx, "x_ctx")

    stage = (pair_kept, mid1_kept, other, given_x)
    mid2_kept = move(after(pair_kept, *stage), mid_swap, "mid2_kept")
    end1_kept = move(after(mid1_kept, *stage), mid_to_end, "end1_kept")
    pair_other = move(after(other, *stage), to_pair, "pair_other")
    mid1_other = move(after(other, *stage), mid_swap, "mid1_other")
    dec_x = embed_steps(after(dec_spikes, *stage), thresholds, in_scale, planes)

    columns = width // lax.axis_size("tp")

    def gate(rows):
        part = lax.dynamic_slice_in_dim(rows, t * columns, columns, 2)
        level = lax.dynamic_slice_in_dim(thresholds, t * columns, columns, 0)
        scale = lax.dynamic_slice_in_dim(in_scale, t * columns, columns, 0)
        return (jnp.where(part >= level, part, 0).astype(jnp.float32) * scale).astype(jnp.bfloat16)

    res, dec_res = gate(after(spikes, *stage)), gate(after(dec_spikes, *stage))
    near_blocks = jnp.stack([after(kept, *stage)[3:], pair_kept[3:]])

    stage = (mid2_kept, end1_kept, pair_other, mid1_other, first_x, near_blocks, dec_x, res, dec_res)
    end2_kept = move(after(mid2_kept, *stage), mid_to_end, "end2_kept")
    mid2_other = move(after(pair_other, *stage), mid_swap, "mid2_other")
    end1_other = move(after(mid1_other, *stage), mid_to_end, "end1_other")
    second_x = move(after(first_x, *stage), to_core, "x_core")
    xs = (own_x, first_x, second_x, dec_x)
    summed = project(scalars, 0, xs, (kept, pair_kept), (other, pair_other), None)

    def carry(blocks, name):
        return blocks, move(blocks, meet, name + "_meet"), move(blocks, corner, name + "_corner")

    def place_out(blocks, met, far, passing, name):
        own = jnp.where(c == y, jnp.stack([blocks, met]), jnp.stack([met, far]))
        return own, move(own, passing, name + "_core")

    third_kept = jnp.where(is_end, end1_kept, mid1_kept)
    near = carry(after(near_blocks, second_x, third_kept), "near")

    stage = (mid2_other, end1_other, summed)
    end2_other = move(after(mid2_other, *stage), mid_to_end, "end2_other")
    near = place_out(near[0], near[1], after(near[2], summed), near_pass, "near")
    third_other = jnp.where(is_end, after(end1_other, *stage), mid1_other)
    summed = project(scalars, 2, xs, (third_kept,), (third_other,), summed)
    fourth_kept = jnp.where(is_end, after(end2_kept, *stage), mid2_kept)
    far = carry(after(jnp.stack([third_kept[3:], fourth_kept[3:]]), near[0]), "far")
    gain = lax.dynamic_slice_in_dim(head_gain, c * heads, heads, 0)

    dims = (groups, block, heads, head, steps)
    own_rows, far_rows = attend(
        scalars, xs, (fourth_kept,), (mid2_other, end2_other), summed, prior_state, gain, lengths, dims
    )
    h_ctx = move(far_rows, to_ctx, "h_ctx")
    h_y = move(own_rows, to_y, "h_y")
    h_diag = move(far_rows, to_diagonal, "h_diag")
    mine = [own_rows, h_ctx, h_y, h_diag]
    far = place_out(far[0], far[1], after(far[2], h_ctx, h_y, h_diag), far_pass, "far")
    hidden = mine + [move(m, to_core, "h_core") for m in mine]

    near_first = z & 1
    far_first = 2 + (z >> 1)
    flags = jnp.stack([c, jnp.where((z >> 1) == parity, near_first, far_first)]).astype(jnp.int32)
    return combine(flags, hidden, near + far, res, dec_res)


def solution(mesh):
    return jax.shard_map(
        local_grid if fits(mesh) else local_any,
        mesh=mesh,
        in_specs=(
            P("rep", "ctx", None),
            P(None, "rep", None),
            P(),
            P(),
            P(None, ("ctx", "rep"), "tp"),
            P("tp", ("ctx", "rep")),
            P("tp", None),
            P("rep", "tp", None, None),
            P("rep"),
        ),
        out_specs=(P("rep", "ctx", "tp"), P(None, "rep", "tp")),
        check_vma=False,
    )
```

```python
import jax
import jax.numpy as jnp
from jax import lax
from jax.experimental import pallas as pl
from jax.experimental.pallas import tpu as pltpu
from jax.sharding import PartitionSpec as P


def carried_in(value, axis, combine, identity):
    peers, here = (lax.axis_size(axis), lax.axis_index(axis))
    everything = lax.all_gather(value, axis)
    start = jnp.broadcast_to(jnp.asarray(identity, value.dtype), value.shape)

    def turn(k, before):
        reached = k < here
        new = combine(before, everything[k])
        return jnp.where(reached, new, before)

    return lax.fori_loop(0, peers, turn, start)


def normalize(value_rows, gain):
    mean = jnp.mean(value_rows * value_rows, axis=-1, keepdims=True)
    return (value_rows * lax.rsqrt(mean + 1e-06) * gain).astype(jnp.bfloat16)


def local_any(
    spikes,
    dec_spikes,
    thresholds,
    in_scale,
    qkv_weight,
    out_weight,
    head_gain,
    prior_state,
    lengths,
):
    groups, block, width = spikes.shape
    steps = dec_spikes.shape[0]
    heads, head = head_gain.shape
    inner = heads * head
    prompt_rows = groups * block
    topmost_precision = lax.Precision.HIGHEST
    context_position = lax.axis_index("ctx")
    tokens_x = (jnp.where(spikes >= thresholds, spikes, 0).astype(jnp.float32) * in_scale).astype(
        jnp.bfloat16
    )
    dec_x = (
        jnp.where(dec_spikes >= thresholds, dec_spikes, 0).astype(jnp.float32) * in_scale
    ).astype(jnp.bfloat16)
    rows_all = jnp.concatenate(
        [tokens_x.reshape(prompt_rows, width), dec_x.reshape(steps * groups, width)], 0
    )
    full = lax.all_gather(qkv_weight, ("ctx", "rep"), axis=1, tiled=True)
    projected = jnp.einsum("rd,cde->rce", rows_all, full, preferred_element_type=jnp.float32)
    projected = projected.astype(jnp.bfloat16)
    prompt = projected[:prompt_rows].reshape(groups, block, 3, heads, head)
    decoded = projected[prompt_rows:].reshape(steps, groups, 3, heads, head)
    query = prompt[:, :, 0]
    value_rows = prompt[:, :, 2]
    positions = context_position * block + jnp.arange(block)
    live = positions[None, :] < lengths[:, None]
    keys = jnp.where(live[:, :, None, None], prompt[:, :, 1], jnp.zeros_like(prompt[:, :, 1]))
    block_state = jnp.einsum(
        "gthk,gthv->ghkv", keys, value_rows, preferred_element_type=jnp.float32
    )
    before = carried_in(
        block_state, "ctx", lambda earlier, later: earlier + later, jnp.zeros_like(block_state)
    )
    carried = (prior_state + before).astype(jnp.bfloat16)
    inter = jnp.einsum("gthk,ghkv->gthv", query, carried, preferred_element_type=jnp.float32)
    scores = jnp.einsum("gthk,gshk->ghts", query, keys, preferred_element_type=jnp.float32)
    causal = jnp.arange(block)[:, None] >= jnp.arange(block)[None, :]
    weights = jnp.where(causal, scores, 0.0).astype(jnp.bfloat16)
    intra = jnp.einsum("ghts,gshv->gthv", weights, value_rows, preferred_element_type=jnp.float32)
    hidden = normalize(inter + intra, head_gain).reshape(prompt_rows, inner)
    dec_query = decoded[:, :, 0].astype(jnp.float32)
    dec_keys = decoded[:, :, 1].astype(jnp.float32)
    dec_values = decoded[:, :, 2].astype(jnp.float32)
    state_readouts = []
    memory_state = prior_state + lax.psum(block_state, "ctx")
    for decode_step_body in range(steps):
        memory_state = memory_state + jnp.einsum(
            "ghk,ghv->ghkv",
            dec_keys[decode_step_body],
            dec_values[decode_step_body],
            precision=topmost_precision,
        )
        state_readouts.append(
            jnp.einsum(
                "ghk,ghkv->ghv",
                dec_query[decode_step_body],
                memory_state,
                precision=topmost_precision,
            )
        )
    dec_hidden = normalize(jnp.stack(state_readouts), head_gain).reshape(steps * groups, inner)
    hidden_all = jnp.concatenate([hidden, dec_hidden], 0)
    columns = width // lax.axis_size("tp")
    residual = lax.dynamic_slice_in_dim(rows_all, lax.axis_index("tp") * columns, columns, 1)
    terms = jnp.dot(
        hidden_all,
        lax.all_gather(out_weight, ("ctx", "rep"), axis=1, tiled=True),
        preferred_element_type=jnp.float32,
    )
    summed = lax.psum_scatter(terms, "tp", scatter_dimension=1, tiled=True)
    result = (residual.astype(jnp.float32) + summed).astype(jnp.bfloat16)
    block_out = result[:prompt_rows].reshape(groups, block, columns)
    decode_out = result[prompt_rows:].reshape(steps, groups, columns)
    return (block_out, decode_out)


AXES = ("ctx", "tp", "rep")
VMEM_LIMIT = 24 * 1024 * 1024
DEC_PAD = 16


def fits(mesh):
    shape = dict(mesh.shape)
    return (shape["ctx"], shape["tp"], shape["rep"]) == (2, 4, 4)


def move(value, target, name="move"):
    sizes = [lax.axis_size(name) for name in AXES]
    pairs = []
    for c in range(sizes[0]):
        for t in range(sizes[1]):
            for r in range(sizes[2]):
                to = target(c, t, r)
                if to is not None:
                    at = (c * sizes[1] + t) * sizes[2] + r
                    pairs.append((at, (to[0] * sizes[1] + to[1]) * sizes[2] + to[2]))
    with jax.named_scope(name):
        return lax.ppermute(value, AXES, pairs)


def after(value, *earlier):
    return lax.optimization_barrier((value, *earlier))[0]


def to_ctx(c, t, r):
    return (1 - c, t, r)


def to_core(c, t, r):
    return (c, t ^ 1, r)


def to_y(c, t, r):
    return (c, t ^ 2, r)


def to_diagonal(c, t, r):
    return (1 - c, t ^ 2, r)


def to_pair(c, t, r):
    return (c, t, r ^ 1)


def mid_swap(c, t, r):
    return (c, t, 3 - r) if r in (1, 2) else None


def mid_to_end(c, t, r):
    return (c, t, r ^ 1) if r in (1, 2) else None


def params():
    return pltpu.CompilerParams(vmem_limit_bytes=VMEM_LIMIT)


def whole(shape):
    return pl.BlockSpec(shape, lambda *_: (0,) * len(shape))


def split_kernel(scalars, kept_in, given_in, out_in, kept_ref, given_ref):
    kinds = kept_in.shape[0]
    kept_ref[:kinds] = kept_in[...]
    given_ref[...] = given_in[...]
    wide = kept_ref.shape[2]
    for half in range(kept_ref.shape[0] - kinds):
        kept_ref[kinds + half] = out_in[:, half * wide : (half + 1) * wide]


def split(scalars, weight, out_weight):
    kinds, rows, columns = weight.shape
    wide = columns // 2
    half = (kinds, rows, wide)
    kept = (kinds + out_weight.shape[1] // wide, rows, wide)
    return pl.pallas_call(
        split_kernel,
        grid_spec=pltpu.PrefetchScalarGridSpec(
            num_scalar_prefetch=1,
            grid=(1,),
            in_specs=[
                pl.BlockSpec(half, lambda i, s: (0, 0, s[0])),
                pl.BlockSpec(half, lambda i, s: (0, 0, 1 - s[0])),
                whole(out_weight.shape),
            ],
            out_specs=[whole(kept), whole(half)],
        ),
        out_shape=[jax.ShapeDtypeStruct(kept, weight.dtype), jax.ShapeDtypeStruct(half, weight.dtype)],
        compiler_params=params(),
        name="split",
    )(scalars, weight, weight, out_weight)


def embed_kernel(parts, spikes_ref, thresholds_ref, scale_ref, out_ref):
    place(parts, spikes_ref[...], thresholds_ref, scale_ref, out_ref)


def embed_steps_kernel(parts, spikes_ref, thresholds_ref, scale_ref, out_ref):
    steps, groups, width = spikes_ref.shape
    rows = [spikes_ref[step] for step in range(steps)]
    rows.append(jnp.zeros((DEC_PAD - steps * groups, width), spikes_ref.dtype))
    place(parts, jnp.concatenate(rows, axis=0), thresholds_ref, scale_ref, out_ref)


def embed_steps(spikes, thresholds, scale, parts):
    width = spikes.shape[2]
    return pl.pallas_call(
        lambda *refs: embed_steps_kernel(parts, *refs),
        out_shape=jax.ShapeDtypeStruct((parts, DEC_PAD, width // parts), jnp.bfloat16),
        compiler_params=params(),
        name="embed_steps",
    )(spikes, thresholds, scale)


def place(parts, counts, thresholds_ref, scale_ref, out_ref):
    gated = jnp.where(counts >= thresholds_ref[...][None], counts, 0)
    x = (gated.astype(jnp.float32) * scale_ref[...][None]).astype(jnp.bfloat16)
    width = x.shape[1] // (2 * parts)
    for z in range(parts):
        first = x[:, z * width : (z + 1) * width]
        second = x[:, (parts + z) * width : (parts + z + 1) * width]
        out_ref[z] = jnp.concatenate([first, second], axis=1)


def embed(spikes, thresholds, scale, parts, tile):
    rows, width = spikes.shape
    return pl.pallas_call(
        lambda *refs: embed_kernel(parts, *refs),
        grid=(rows // tile,),
        in_specs=[
            pl.BlockSpec((tile, width), lambda i: (i, 0)),
            whole((width,)),
            whole((width,)),
        ],
        out_specs=pl.BlockSpec((parts, tile, width // parts), lambda i: (0, i, 0)),
        out_shape=jax.ShapeDtypeStruct((parts, rows, width // parts), jnp.bfloat16),
        compiler_params=params(),
        name="embed",
    )(spikes, thresholds, scale)


def weights_of(scalars, mine, other, index):
    def pick(refs):
        return refs[0][index] if len(refs) == 1 else jnp.where(scalars[1] == 1, refs[1][index], refs[0][index])

    own, far = pick(mine), pick(other)
    first = scalars[0] == 0
    return jnp.concatenate([jnp.where(first, own, far), jnp.where(first, far, own)], axis=0)


def row_blocks(x_refs):
    at = 0
    for ref in x_refs:
        rows = ref.shape[1]
        yield ref, at, rows
        at += rows


def project_kernel(steps, has_sum, scalars, *refs):
    x_refs, out_ref = refs[:4], refs[-1]
    mine, other = refs[4 : 4 + steps], refs[4 + steps : 4 + 2 * steps]
    for step in range(steps):

        @pl.when(pl.program_id(0) == step)
        def _(step=step):
            for index in range(3):
                weight = weights_of(scalars, mine[step : step + 1], other[step : step + 1], index)
                columns = slice(index * weight.shape[1], (index + 1) * weight.shape[1])
                for ref, at, rows in row_blocks(x_refs):
                    term = jnp.dot(ref[0], weight, preferred_element_type=jnp.float32)
                    if step or has_sum:
                        term = (out_ref if step else refs[-2])[at : at + rows, columns] + term
                    out_ref[at : at + rows, columns] = term


def part_spec(array, step):
    block = (1,) + array.shape[1:]
    return pl.BlockSpec(block, lambda i, scalars: (scalars[3 + step + i], 0, 0))


def project(scalars, first, xs, mine, other, summed):
    steps = len(mine)
    rows = sum(x.shape[1] for x in xs)
    columns = 3 * mine[0].shape[2]
    earlier = [] if summed is None else [summed]
    return pl.pallas_call(
        lambda *refs: project_kernel(steps, bool(earlier), *refs),
        grid_spec=pltpu.PrefetchScalarGridSpec(
            num_scalar_prefetch=1,
            grid=(steps,),
            in_specs=[part_spec(x, first) for x in xs]
            + [whole(other[0].shape) for _ in (*mine, *other)]
            + [whole(sums.shape) for sums in earlier],
            out_specs=whole((rows, columns)),
        ),
        out_shape=jax.ShapeDtypeStruct((rows, columns), jnp.float32),
        compiler_params=params(),
        name="project",
    )(scalars, *xs, *mine, *other, *earlier)


def attend_kernel(
    dims, scalars, own_x, first_x, second_x, dec_x, mine, other0, other1, sum_ref, prior_ref, gain_ref, lengths, near_ref, far_ref, qkv
):
    groups, block, heads, head, steps = dims
    for index in range(3):
        weight = weights_of(scalars, (mine,), (other0, other1), index)
        columns = slice(index * weight.shape[1], (index + 1) * weight.shape[1])
        for ref, at, rows in row_blocks((own_x, first_x, second_x, dec_x)):
            term = jnp.dot(ref[0], weight, preferred_element_type=jnp.float32)
            qkv[at : at + rows, columns] = (sum_ref[at : at + rows, columns] + term).astype(jnp.bfloat16)
    here = scalars[0]
    parity = scalars[2]
    wide = heads * head
    prompt = 2 * groups * block
    causal = lax.broadcasted_iota(jnp.int32, (block, block), 0) >= lax.broadcasted_iota(jnp.int32, (block, block), 1)
    position = lax.broadcasted_iota(jnp.int32, (block, head), 0)
    row = lax.broadcasted_iota(jnp.int32, (DEC_PAD, DEC_PAD), 0)
    column = lax.broadcasted_iota(jnp.int32, (DEC_PAD, DEC_PAD), 1)
    reach = (row % groups == column % groups) & (column <= row)
    exact = lax.Precision.HIGHEST
    inner = (((0,), (0,)), ((), ()))
    across = (((1,), (1,)), ((), ()))

    def finish(value, gain):
        mean = jnp.mean(value * value, axis=-1, keepdims=True)
        return (value * lax.rsqrt(mean + 1e-06) * gain).astype(jnp.bfloat16)

    for h in range(heads):
        cols = [slice(i * wide + h * head, i * wide + (h + 1) * head) for i in range(3)]
        gain = gain_ref[h : h + 1, :]
        dq = qkv[prompt : prompt + DEC_PAD, cols[0]]
        dk = qkv[prompt : prompt + DEC_PAD, cols[1]]
        dv = qkv[prompt : prompt + DEC_PAD, cols[2]].astype(jnp.float32)
        dq32 = dq.astype(jnp.float32)
        pairs = lax.dot_general(dq, dk, across, preferred_element_type=jnp.float32)
        read = jnp.dot(jnp.where(reach, pairs, 0.0), dv, precision=exact, preferred_element_type=jnp.float32)
        dec_group = lax.broadcasted_iota(jnp.int32, (DEC_PAD, head), 0) % groups
        for r in range(groups):
            prior = prior_ref[r, h]
            starts = (r * block, groups * block + pl.multiple_of((r ^ parity) * block, block))
            run = (here, 1 - here)
            keys, values, states = [], [], []
            for start, b in zip(starts, run):
                k = qkv[pl.ds(start, block), cols[1]]
                live = b * block + position < lengths[r]
                k = jnp.where(live, k, jnp.zeros_like(k))
                v = qkv[pl.ds(start, block), cols[2]]
                keys.append(k)
                values.append(v)
                states.append(lax.dot_general(k, v, inner, preferred_element_type=jnp.float32))
            before = (jnp.where(here == 1, states[1], 0.0), jnp.where(here == 0, states[0], 0.0))
            for side, out_ref in enumerate((near_ref, far_ref)):
                q = qkv[pl.ds(starts[side], block), cols[0]]
                carried = (prior + before[side]).astype(jnp.bfloat16)
                scores = lax.dot_general(q, keys[side], across, preferred_element_type=jnp.float32)
                weights = jnp.where(causal, scores, 0.0).astype(jnp.bfloat16)
                attended = jnp.dot(q, carried, preferred_element_type=jnp.float32) + jnp.dot(
                    weights, values[side], preferred_element_type=jnp.float32
                )
                out_ref[r * block : (r + 1) * block, h * head : (h + 1) * head] = finish(attended, gain)
            state = prior + (states[0] + states[1])
            inter = jnp.dot(dq32, state, precision=exact, preferred_element_type=jnp.float32)
            read = read + jnp.where(dec_group == r, inter, 0.0)
        done = finish(read, gain)
        near_ref[groups * block :, h * head : (h + 1) * head] = done
        far_ref[groups * block :, h * head : (h + 1) * head] = done


def attend(scalars, xs, mine, other, summed, prior, gain, lengths, dims):
    groups, block, heads, head, _ = dims
    rows, columns = summed.shape
    shape = (groups * block + DEC_PAD, heads * head)
    in_specs = [part_spec(x, 3) for x in xs]
    in_specs += [whole(other[0].shape) for _ in (*mine, *other)] + [whole(summed.shape)]
    in_specs += [
        pl.BlockSpec((groups, heads, head, head), lambda i, s: (0, s[0], 0, 0)),
        whole(gain.shape),
        pl.BlockSpec(memory_space=pltpu.SMEM),
    ]
    out = jax.ShapeDtypeStruct(shape, jnp.bfloat16)
    return pl.pallas_call(
        lambda *refs: attend_kernel(dims, *refs),
        grid_spec=pltpu.PrefetchScalarGridSpec(
            num_scalar_prefetch=1,
            grid=(1,),
            in_specs=in_specs,
            out_specs=[whole(shape), whole(shape)],
            scratch_shapes=[pltpu.VMEM((rows, columns), jnp.bfloat16)],
        ),
        out_shape=[out, out],
        compiler_params=params(),
        cost_estimate=pl.CostEstimate(
            flops=2 * rows * columns * xs[0].shape[2] * 2, bytes_accessed=4 * rows * columns, transcendentals=0
        ),
        name="attend",
    )(scalars, *xs, *mine, *other, summed, prior, gain, lengths)


def arrange_kernel(scalars, *refs):
    groups, out_ref, sems = (refs[:3], refs[3:6]), refs[6], refs[7]

    def copy(half, source):
        return pltpu.make_async_copy(source, out_ref.at[half], sems.at[half])

    for near in range(2):
        for same in range(2):

            @pl.when((scalars[1] == near) & (scalars[2] == same))
            def _(near=near, same=same):
                for half in range(2):
                    copy(half, groups[near][half + 1 - same]).start()

    for half in range(2):
        copy(half, groups[0][0]).wait()


def arrange(scalars, *blocks):
    shape = (2, *blocks[0].shape)
    return pl.pallas_call(
        arrange_kernel,
        grid_spec=pltpu.PrefetchScalarGridSpec(
            num_scalar_prefetch=1,
            grid=(1,),
            in_specs=[pl.BlockSpec(memory_space=pl.ANY)] * 6,
            out_specs=whole(shape),
            scratch_shapes=[pltpu.SemaphoreType.DMA((2,))],
        ),
        out_shape=jax.ShapeDtypeStruct(shape, jnp.bfloat16),
        compiler_params=params(),
        name="arrange",
    )(scalars, *blocks)


def combine_kernel(scalars, *refs):
    hidden, groups, passed = refs[:8], (refs[8:11], refs[11:14]), refs[14]
    res_ref, dec_res_ref, out_ref, dec_ref, rows, weights, hidden_sems, weight_sems = refs[15:]
    wide = hidden[0].shape[1]

    def hidden_copy(i, j):
        part = scalars[0] if j == 0 else 1 - scalars[0]
        at = pl.ds(pl.multiple_of((2 * i + part) * wide, wide), wide)
        source = hidden[4 * (i % 2) + 2 * (i // 2) + j]
        return pltpu.make_async_copy(source, rows.at[:, at], hidden_sems.at[i, j])

    def weight_copy(i, slot, part, source):
        at = pl.ds((2 * i + part) * wide, wide)
        return pltpu.make_async_copy(source, weights.at[slot, :, at], weight_sems.at[i, slot, part])

    every = [(i, slot, part) for slot in range(2) for i in range(4) for part in range(2)]
    for i in range(4):
        for j in range(2):
            hidden_copy(i, j).start()
    for near in range(2):
        for same in range(2):

            @pl.when((scalars[1] == near) & (scalars[2] == same))
            def _(near=near, same=same):
                for i, slot, part in every:
                    source = passed.at[i // 2] if i % 2 else groups[1 - near][i // 2 + 1 - same]
                    plane = jnp.bitwise_xor(scalars[3], slot)
                    weight_copy(i, slot, part, source.at[plane, part]).start()

    for i in range(4):
        for j in range(2):
            hidden_copy(i, j).wait()
    total = []
    for slot in range(2):
        for i, at, part in every:
            if at == slot:
                weight_copy(i, slot, part, passed.at[0, 0, 0]).wait()
        total.append(
            lax.dot_general(rows[...], weights[slot], (((1,), (1,)), ((), ())), preferred_element_type=jnp.float32)
        )
    total = jnp.concatenate(total, axis=1)
    groups, block = out_ref.shape[:2]
    for r in range(groups):
        out_ref[r] = (res_ref[r].astype(jnp.float32) + total[r * block : (r + 1) * block]).astype(jnp.bfloat16)
    for step in range(dec_ref.shape[0]):
        at = groups * block + step * groups
        dec_ref[step] = (dec_res_ref[step].astype(jnp.float32) + total[at : at + groups]).astype(jnp.bfloat16)


def combine(scalars, hidden, blocks, res, dec_res):
    anywhere = pl.BlockSpec(memory_space=pl.ANY)
    return pl.pallas_call(
        combine_kernel,
        grid_spec=pltpu.PrefetchScalarGridSpec(
            num_scalar_prefetch=1,
            grid=(1,),
            in_specs=[anywhere] * (len(hidden) + len(blocks))
            + [whole(res.shape), whole(dec_res.shape)],
            out_specs=[whole(res.shape), whole(dec_res.shape)],
            scratch_shapes=[
                pltpu.VMEM((hidden[0].shape[0], 8 * hidden[0].shape[1]), jnp.bfloat16),
                pltpu.VMEM((2, blocks[0].shape[2], 8 * blocks[0].shape[3]), jnp.bfloat16),
                pltpu.SemaphoreType.DMA((4, 2)),
                pltpu.SemaphoreType.DMA((4, 2, 2)),
            ],
        ),
        out_shape=[
            jax.ShapeDtypeStruct(res.shape, jnp.bfloat16),
            jax.ShapeDtypeStruct(dec_res.shape, jnp.bfloat16),
        ],
        compiler_params=params(),
        name="combine",
    )(scalars, *hidden, *blocks, res, dec_res)


def local_grid(
    spikes, dec_spikes, thresholds, in_scale, qkv_weight, out_weight, head_gain, prior_state, lengths
):
    groups, block, width = spikes.shape
    steps = dec_spikes.shape[0]
    all_heads, head = head_gain.shape
    heads = all_heads // 2
    planes = lax.axis_size("rep")
    c, t, z = (lax.axis_index(name) for name in AXES)
    parity = t & 1
    y = t >> 1
    is_end = (z == 0) | (z == planes - 1)
    end = is_end.astype(jnp.int32)
    third = jnp.where(is_end, z ^ 2, z ^ 3)
    fourth = jnp.where(is_end, z ^ 3, z ^ 2)
    scalars = jnp.stack([c, end, parity, z, z ^ 1, third, fourth]).astype(jnp.int32)

    def meet(c, t, r):
        return (1 - c, t, r) if c == t // 2 else (c, t ^ 2, r)

    def corner(c, t, r):
        return None if c == t // 2 else (1 - c, t ^ 2, r)

    kept, given = split(scalars, qkv_weight, out_weight.T)
    pair_kept = move(kept, to_pair, "pair_kept")
    mid1_kept = move(kept, mid_swap, "mid1_kept")
    other = move(given, to_ctx, "pre_w")

    counts = spikes.reshape(groups * block, width)
    own_x = embed(counts, thresholds, in_scale, planes, block // 4)
    given_x = lax.dynamic_slice_in_dim(own_x, parity * block, block, 1)

    first_x = move(after(given_x, other), to_ctx, "x_ctx")

    stage = (pair_kept, mid1_kept, other, given_x)
    mid2_kept = move(after(pair_kept, *stage), mid_swap, "mid2_kept")
    end1_kept = move(after(mid1_kept, *stage), mid_to_end, "end1_kept")
    pair_other = move(after(other, *stage), to_pair, "pair_other")
    mid1_other = move(after(other, *stage), mid_swap, "mid1_other")
    dec_x = embed_steps(after(dec_spikes, *stage), thresholds, in_scale, planes)

    near_blocks = jnp.stack([after(kept, *stage)[3:], pair_kept[3:]])

    stage = (mid2_kept, end1_kept, pair_other, mid1_other, first_x, near_blocks, dec_x)
    end2_kept = move(after(mid2_kept, *stage), mid_to_end, "end2_kept")
    mid2_other = move(after(pair_other, *stage), mid_swap, "mid2_other")
    end1_other = move(after(mid1_other, *stage), mid_to_end, "end1_other")
    second_x = move(after(first_x, *stage), to_core, "x_core")
    xs = (own_x, first_x, second_x, dec_x)
    summed = project(scalars, 0, xs, (kept, pair_kept), (other, pair_other), None)

    def carry(blocks, name):
        return blocks, move(blocks, meet, name + "_meet"), move(blocks, corner, name + "_corner")

    third_kept = jnp.where(is_end, end1_kept, mid1_kept)
    near = carry(after(near_blocks, second_x, third_kept), "near")

    columns = width // lax.axis_size("tp")

    def gate(rows):
        part = lax.dynamic_slice_in_dim(rows, t * columns, columns, 2)
        level = lax.dynamic_slice_in_dim(thresholds, t * columns, columns, 0)
        scale = lax.dynamic_slice_in_dim(in_scale, t * columns, columns, 0)
        return (jnp.where(part >= level, part, 0).astype(jnp.float32) * scale).astype(jnp.bfloat16)

    res, dec_res = gate(after(spikes, second_x)), gate(after(dec_spikes, second_x))
    stage = (mid2_other, end1_other, summed, res, dec_res)
    end2_other = move(after(mid2_other, *stage), mid_to_end, "end2_other")
    third_other = jnp.where(is_end, after(end1_other, *stage), mid1_other)
    summed = project(scalars, 2, xs, (third_kept,), (third_other,), summed)
    fourth_kept = jnp.where(is_end, after(end2_kept, *stage), mid2_kept)
    far = carry(after(jnp.stack([third_kept[3:], fourth_kept[3:]]), near[1], near[2]), "far")
    gain = lax.dynamic_slice_in_dim(head_gain, c * heads, heads, 0)

    dims = (groups, block, heads, head, steps)
    own_rows, far_rows = attend(
        scalars, xs, (fourth_kept,), (mid2_other, end2_other), summed, prior_state, gain, lengths, dims
    )
    h_ctx = move(far_rows, to_ctx, "h_ctx")
    h_y = move(own_rows, to_y, "h_y")
    h_diag = move(far_rows, to_diagonal, "h_diag")
    mine = [own_rows, h_ctx, h_y, h_diag]
    near_used = (z >> 1) == parity
    flags = jnp.stack([c, near_used, c == y, jnp.where(near_used, z & 1, z >> 1)]).astype(jnp.int32)
    passed = arrange(flags, *near, far[0], far[1], after(far[2], own_rows))
    blocks = (*near, *far, move(passed, to_core, "out_core"))
    hidden = mine + [move(m, to_core, "h_core") for m in (after(own_rows, h_ctx), h_ctx, h_y, h_diag)]

    return combine(flags, hidden, blocks, res, dec_res)


def solution(mesh):
    return jax.shard_map(
        local_grid if fits(mesh) else local_any,
        mesh=mesh,
        in_specs=(
            P("rep", "ctx", None),
            P(None, "rep", None),
            P(),
            P(),
            P(None, ("ctx", "rep"), "tp"),
            P("tp", ("ctx", "rep")),
            P("tp", None),
            P("rep", "tp", None, None),
            P("rep"),
        ),
        out_specs=(P("rep", "ctx", "tp"), P(None, "rep", "tp")),
        check_vma=False,
    )
```

```python
import jax
import jax.numpy as jnp
from jax import lax
from jax.experimental import pallas as pl
from jax.experimental.pallas import tpu as pltpu
from jax.sharding import PartitionSpec as P


def carried_in(value, axis, combine, identity):
    peers, here = (lax.axis_size(axis), lax.axis_index(axis))
    everything = lax.all_gather(value, axis)
    start = jnp.broadcast_to(jnp.asarray(identity, value.dtype), value.shape)

    def turn(k, before):
        reached = k < here
        new = combine(before, everything[k])
        return jnp.where(reached, new, before)

    return lax.fori_loop(0, peers, turn, start)


def normalize(value_rows, gain):
    mean = jnp.mean(value_rows * value_rows, axis=-1, keepdims=True)
    return (value_rows * lax.rsqrt(mean + 1e-06) * gain).astype(jnp.bfloat16)


def local_any(
    spikes,
    dec_spikes,
    thresholds,
    in_scale,
    qkv_weight,
    out_weight,
    head_gain,
    prior_state,
    lengths,
):
    groups, block, width = spikes.shape
    steps = dec_spikes.shape[0]
    heads, head = head_gain.shape
    inner = heads * head
    prompt_rows = groups * block
    topmost_precision = lax.Precision.HIGHEST
    context_position = lax.axis_index("ctx")
    tokens_x = (jnp.where(spikes >= thresholds, spikes, 0).astype(jnp.float32) * in_scale).astype(
        jnp.bfloat16
    )
    dec_x = (
        jnp.where(dec_spikes >= thresholds, dec_spikes, 0).astype(jnp.float32) * in_scale
    ).astype(jnp.bfloat16)
    rows_all = jnp.concatenate(
        [tokens_x.reshape(prompt_rows, width), dec_x.reshape(steps * groups, width)], 0
    )
    full = lax.all_gather(qkv_weight, ("ctx", "rep"), axis=1, tiled=True)
    projected = jnp.einsum("rd,cde->rce", rows_all, full, preferred_element_type=jnp.float32)
    projected = projected.astype(jnp.bfloat16)
    prompt = projected[:prompt_rows].reshape(groups, block, 3, heads, head)
    decoded = projected[prompt_rows:].reshape(steps, groups, 3, heads, head)
    query = prompt[:, :, 0]
    value_rows = prompt[:, :, 2]
    positions = context_position * block + jnp.arange(block)
    live = positions[None, :] < lengths[:, None]
    keys = jnp.where(live[:, :, None, None], prompt[:, :, 1], jnp.zeros_like(prompt[:, :, 1]))
    block_state = jnp.einsum(
        "gthk,gthv->ghkv", keys, value_rows, preferred_element_type=jnp.float32
    )
    before = carried_in(
        block_state, "ctx", lambda earlier, later: earlier + later, jnp.zeros_like(block_state)
    )
    carried = (prior_state + before).astype(jnp.bfloat16)
    inter = jnp.einsum("gthk,ghkv->gthv", query, carried, preferred_element_type=jnp.float32)
    scores = jnp.einsum("gthk,gshk->ghts", query, keys, preferred_element_type=jnp.float32)
    causal = jnp.arange(block)[:, None] >= jnp.arange(block)[None, :]
    weights = jnp.where(causal, scores, 0.0).astype(jnp.bfloat16)
    intra = jnp.einsum("ghts,gshv->gthv", weights, value_rows, preferred_element_type=jnp.float32)
    hidden = normalize(inter + intra, head_gain).reshape(prompt_rows, inner)
    dec_query = decoded[:, :, 0].astype(jnp.float32)
    dec_keys = decoded[:, :, 1].astype(jnp.float32)
    dec_values = decoded[:, :, 2].astype(jnp.float32)
    state_readouts = []
    memory_state = prior_state + lax.psum(block_state, "ctx")
    for decode_step_body in range(steps):
        memory_state = memory_state + jnp.einsum(
            "ghk,ghv->ghkv",
            dec_keys[decode_step_body],
            dec_values[decode_step_body],
            precision=topmost_precision,
        )
        state_readouts.append(
            jnp.einsum(
                "ghk,ghkv->ghv",
                dec_query[decode_step_body],
                memory_state,
                precision=topmost_precision,
            )
        )
    dec_hidden = normalize(jnp.stack(state_readouts), head_gain).reshape(steps * groups, inner)
    hidden_all = jnp.concatenate([hidden, dec_hidden], 0)
    columns = width // lax.axis_size("tp")
    residual = lax.dynamic_slice_in_dim(rows_all, lax.axis_index("tp") * columns, columns, 1)
    terms = jnp.dot(
        hidden_all,
        lax.all_gather(out_weight, ("ctx", "rep"), axis=1, tiled=True),
        preferred_element_type=jnp.float32,
    )
    summed = lax.psum_scatter(terms, "tp", scatter_dimension=1, tiled=True)
    result = (residual.astype(jnp.float32) + summed).astype(jnp.bfloat16)
    block_out = result[:prompt_rows].reshape(groups, block, columns)
    decode_out = result[prompt_rows:].reshape(steps, groups, columns)
    return (block_out, decode_out)


AXES = ("ctx", "tp", "rep")
VMEM_LIMIT = 24 * 1024 * 1024
DEC_PAD = 16


def fits(mesh):
    shape = dict(mesh.shape)
    return (shape["ctx"], shape["tp"], shape["rep"]) == (2, 4, 4)


def move(value, target, name="move"):
    sizes = [lax.axis_size(name) for name in AXES]
    pairs = []
    for c in range(sizes[0]):
        for t in range(sizes[1]):
            for r in range(sizes[2]):
                to = target(c, t, r)
                if to is not None:
                    at = (c * sizes[1] + t) * sizes[2] + r
                    pairs.append((at, (to[0] * sizes[1] + to[1]) * sizes[2] + to[2]))
    with jax.named_scope(name):
        return lax.ppermute(value, AXES, pairs)


def after(value, *earlier):
    return lax.optimization_barrier((value, *earlier))[0]


def after_all(values, *earlier):
    return lax.optimization_barrier((*values, *earlier))[: len(values)]


def to_ctx(c, t, r):
    return (1 - c, t, r)


def to_core(c, t, r):
    return (c, t ^ 1, r)


def to_y(c, t, r):
    return (c, t ^ 2, r)


def to_diagonal(c, t, r):
    return (1 - c, t ^ 2, r)


def to_pair(c, t, r):
    return (c, t, r ^ 1)


def mid_swap(c, t, r):
    return (c, t, 3 - r) if r in (1, 2) else None


def mid_to_end(c, t, r):
    return (c, t, r ^ 1) if r in (1, 2) else None


def params():
    return pltpu.CompilerParams(vmem_limit_bytes=VMEM_LIMIT)


def whole(shape):
    return pl.BlockSpec(shape, lambda *_: (0,) * len(shape))


def split_kernel(scalars, kept_in, given_in, out_in, kept_ref, given_ref):
    kinds = kept_in.shape[0]
    kept_ref[:kinds] = kept_in[...]
    given_ref[...] = given_in[...]
    wide = kept_ref.shape[2]
    for half in range(kept_ref.shape[0] - kinds):
        kept_ref[kinds + half] = out_in[:, half * wide : (half + 1) * wide]


def split(scalars, weight, out_weight):
    kinds, rows, columns = weight.shape
    wide = columns // 2
    half = (kinds, rows, wide)
    kept = (kinds + out_weight.shape[1] // wide, rows, wide)
    return pl.pallas_call(
        split_kernel,
        grid_spec=pltpu.PrefetchScalarGridSpec(
            num_scalar_prefetch=1,
            grid=(1,),
            in_specs=[
                pl.BlockSpec(half, lambda i, s: (0, 0, s[0])),
                pl.BlockSpec(half, lambda i, s: (0, 0, 1 - s[0])),
                whole(out_weight.shape),
            ],
            out_specs=[whole(kept), whole(half)],
        ),
        out_shape=[jax.ShapeDtypeStruct(kept, weight.dtype), jax.ShapeDtypeStruct(half, weight.dtype)],
        compiler_params=params(),
        name="split",
    )(scalars, weight, weight, out_weight)


def embed_kernel(parts, spikes_ref, thresholds_ref, scale_ref, out_ref):
    place(parts, spikes_ref[...], thresholds_ref, scale_ref, out_ref)


def embed_steps_kernel(parts, spikes_ref, thresholds_ref, scale_ref, out_ref):
    steps, groups, width = spikes_ref.shape
    rows = [spikes_ref[step] for step in range(steps)]
    rows.append(jnp.zeros((DEC_PAD - steps * groups, width), spikes_ref.dtype))
    place(parts, jnp.concatenate(rows, axis=0), thresholds_ref, scale_ref, out_ref)


def embed_steps(spikes, thresholds, scale, parts):
    width = spikes.shape[2]
    return pl.pallas_call(
        lambda *refs: embed_steps_kernel(parts, *refs),
        out_shape=jax.ShapeDtypeStruct((parts, DEC_PAD, width // parts), jnp.bfloat16),
        compiler_params=params(),
        name="embed_steps",
    )(spikes, thresholds, scale)


def place(parts, counts, thresholds_ref, scale_ref, out_ref):
    gated = jnp.where(counts >= thresholds_ref[...][None], counts, 0)
    x = (gated.astype(jnp.float32) * scale_ref[...][None]).astype(jnp.bfloat16)
    width = x.shape[1] // (2 * parts)
    for z in range(parts):
        first = x[:, z * width : (z + 1) * width]
        second = x[:, (parts + z) * width : (parts + z + 1) * width]
        out_ref[z] = jnp.concatenate([first, second], axis=1)


def embed(spikes, thresholds, scale, parts, tile):
    rows, width = spikes.shape
    return pl.pallas_call(
        lambda *refs: embed_kernel(parts, *refs),
        grid=(rows // tile,),
        in_specs=[
            pl.BlockSpec((tile, width), lambda i: (i, 0)),
            whole((width,)),
            whole((width,)),
        ],
        out_specs=pl.BlockSpec((parts, tile, width // parts), lambda i: (0, i, 0)),
        out_shape=jax.ShapeDtypeStruct((parts, rows, width // parts), jnp.bfloat16),
        compiler_params=params(),
        name="embed",
    )(spikes, thresholds, scale)


def weights_of(scalars, mine, other, index):
    def pick(refs):
        return refs[0][index] if len(refs) == 1 else jnp.where(scalars[1] == 1, refs[1][index], refs[0][index])

    own, far = pick(mine), pick(other)
    first = scalars[0] == 0
    return jnp.concatenate([jnp.where(first, own, far), jnp.where(first, far, own)], axis=0)


def row_blocks(x_refs):
    at = 0
    for ref in x_refs:
        rows = ref.shape[1]
        yield ref, at, rows
        at += rows


def project_kernel(steps, has_sum, scalars, *refs):
    x_refs, out_ref = refs[:4], refs[-1]
    mine, other = refs[4 : 4 + steps], refs[4 + steps : 4 + 2 * steps]
    for step in range(steps):

        @pl.when(pl.program_id(0) == step)
        def _(step=step):
            for index in range(3):
                weight = weights_of(scalars, mine[step : step + 1], other[step : step + 1], index)
                columns = slice(index * weight.shape[1], (index + 1) * weight.shape[1])
                for ref, at, rows in row_blocks(x_refs):
                    term = jnp.dot(ref[0], weight, preferred_element_type=jnp.float32)
                    if step or has_sum:
                        term = (out_ref if step else refs[-2])[at : at + rows, columns] + term
                    out_ref[at : at + rows, columns] = term


def part_spec(array, step):
    block = (1,) + array.shape[1:]
    return pl.BlockSpec(block, lambda i, scalars: (scalars[3 + step + i], 0, 0))


def project(scalars, first, xs, mine, other, summed):
    steps = len(mine)
    rows = sum(x.shape[1] for x in xs)
    columns = 3 * mine[0].shape[2]
    earlier = [] if summed is None else [summed]
    return pl.pallas_call(
        lambda *refs: project_kernel(steps, bool(earlier), *refs),
        grid_spec=pltpu.PrefetchScalarGridSpec(
            num_scalar_prefetch=1,
            grid=(steps,),
            in_specs=[part_spec(x, first) for x in xs]
            + [whole(other[0].shape) for _ in (*mine, *other)]
            + [whole(sums.shape) for sums in earlier],
            out_specs=whole((rows, columns)),
        ),
        out_shape=jax.ShapeDtypeStruct((rows, columns), jnp.float32),
        compiler_params=params(),
        name="project",
    )(scalars, *xs, *mine, *other, *earlier)


def attend_kernel(dims, scalars, *refs):
    own_x, first_x, second_x, dec_x, mine, other0, other1, sum_ref, prior_ref, gain_ref, lengths = refs[:11]
    sets, near_ref, far_ref, passed_ref, qkv, sems = (refs[11:14], refs[14:17]), *refs[17:]

    def copy(half, source):
        return pltpu.make_async_copy(source, passed_ref.at[half], sems.at[half])

    for near in range(2):
        for same in range(2):

            @pl.when((scalars[7] == near) & (scalars[8] == same))
            def _(near=near, same=same):
                for half in range(2):
                    copy(half, sets[near][half + 1 - same]).start()

    groups, block, heads, head, steps = dims
    for index in range(3):
        weight = weights_of(scalars, (mine,), (other0, other1), index)
        columns = slice(index * weight.shape[1], (index + 1) * weight.shape[1])
        for ref, at, rows in row_blocks((own_x, first_x, second_x, dec_x)):
            term = jnp.dot(ref[0], weight, preferred_element_type=jnp.float32)
            qkv[at : at + rows, columns] = (sum_ref[at : at + rows, columns] + term).astype(jnp.bfloat16)
    here = scalars[0]
    parity = scalars[2]
    wide = heads * head
    prompt = 2 * groups * block
    causal = lax.broadcasted_iota(jnp.int32, (block, block), 0) >= lax.broadcasted_iota(jnp.int32, (block, block), 1)
    position = lax.broadcasted_iota(jnp.int32, (block, head), 0)
    row = lax.broadcasted_iota(jnp.int32, (DEC_PAD, DEC_PAD), 0)
    column = lax.broadcasted_iota(jnp.int32, (DEC_PAD, DEC_PAD), 1)
    reach = (row % groups == column % groups) & (column <= row)
    exact = lax.Precision.HIGHEST
    inner = (((0,), (0,)), ((), ()))
    across = (((1,), (1,)), ((), ()))

    def finish(value, gain):
        mean = jnp.mean(value * value, axis=-1, keepdims=True)
        return (value * lax.rsqrt(mean + 1e-06) * gain).astype(jnp.bfloat16)

    for h in range(heads):
        cols = [slice(i * wide + h * head, i * wide + (h + 1) * head) for i in range(3)]
        gain = gain_ref[h : h + 1, :]
        dq = qkv[prompt : prompt + DEC_PAD, cols[0]]
        dk = qkv[prompt : prompt + DEC_PAD, cols[1]]
        dv = qkv[prompt : prompt + DEC_PAD, cols[2]].astype(jnp.float32)
        dq32 = dq.astype(jnp.float32)
        pairs = lax.dot_general(dq, dk, across, preferred_element_type=jnp.float32)
        read = jnp.dot(jnp.where(reach, pairs, 0.0), dv, precision=exact, preferred_element_type=jnp.float32)
        dec_group = lax.broadcasted_iota(jnp.int32, (DEC_PAD, head), 0) % groups
        for r in range(groups):
            prior = prior_ref[r, h]
            starts = (r * block, groups * block + pl.multiple_of((r ^ parity) * block, block))
            run = (here, 1 - here)
            keys, values, states = [], [], []
            for start, b in zip(starts, run):
                k = qkv[pl.ds(start, block), cols[1]]
                live = b * block + position < lengths[r]
                k = jnp.where(live, k, jnp.zeros_like(k))
                v = qkv[pl.ds(start, block), cols[2]]
                keys.append(k)
                values.append(v)
                states.append(lax.dot_general(k, v, inner, preferred_element_type=jnp.float32))
            before = (jnp.where(here == 1, states[1], 0.0), jnp.where(here == 0, states[0], 0.0))
            for side, out_ref in enumerate((near_ref, far_ref)):
                q = qkv[pl.ds(starts[side], block), cols[0]]
                carried = (prior + before[side]).astype(jnp.bfloat16)
                scores = lax.dot_general(q, keys[side], across, preferred_element_type=jnp.float32)
                weights = jnp.where(causal, scores, 0.0).astype(jnp.bfloat16)
                attended = jnp.dot(q, carried, preferred_element_type=jnp.float32) + jnp.dot(
                    weights, values[side], preferred_element_type=jnp.float32
                )
                out_ref[r * block : (r + 1) * block, h * head : (h + 1) * head] = finish(attended, gain)
            state = prior + (states[0] + states[1])
            inter = jnp.dot(dq32, state, precision=exact, preferred_element_type=jnp.float32)
            read = read + jnp.where(dec_group == r, inter, 0.0)
        done = finish(read, gain)
        near_ref[groups * block :, h * head : (h + 1) * head] = done
        far_ref[groups * block :, h * head : (h + 1) * head] = done
    for half in range(2):
        copy(half, sets[0][0]).wait()


def attend(scalars, xs, mine, other, summed, prior, gain, lengths, blocks, dims):
    groups, block, heads, head, _ = dims
    rows, columns = summed.shape
    shape = (groups * block + DEC_PAD, heads * head)
    in_specs = [part_spec(x, 3) for x in xs]
    in_specs += [whole(other[0].shape) for _ in (*mine, *other)] + [whole(summed.shape)]
    in_specs += [
        pl.BlockSpec((groups, heads, head, head), lambda i, s: (0, s[0], 0, 0)),
        whole(gain.shape),
        pl.BlockSpec(memory_space=pltpu.SMEM),
    ]
    in_specs += [pl.BlockSpec(memory_space=pl.ANY)] * len(blocks)
    passed = (2, *blocks[0].shape)
    out = jax.ShapeDtypeStruct(shape, jnp.bfloat16)
    return pl.pallas_call(
        lambda *refs: attend_kernel(dims, *refs),
        grid_spec=pltpu.PrefetchScalarGridSpec(
            num_scalar_prefetch=1,
            grid=(1,),
            in_specs=in_specs,
            out_specs=[whole(shape), whole(shape), whole(passed)],
            scratch_shapes=[pltpu.VMEM((rows, columns), jnp.bfloat16), pltpu.SemaphoreType.DMA((2,))],
        ),
        out_shape=[out, out, jax.ShapeDtypeStruct(passed, jnp.bfloat16)],
        compiler_params=params(),
        cost_estimate=pl.CostEstimate(
            flops=2 * rows * columns * xs[0].shape[2] * 2, bytes_accessed=4 * rows * columns, transcendentals=0
        ),
        name="attend",
    )(scalars, *xs, *mine, *other, summed, prior, gain, lengths, *blocks)


def lay_kernel(scalars, *refs):
    groups, passed, out_ref, sems = (refs[:3], refs[3:6]), refs[6], refs[7], refs[8]
    depth, wide = passed.shape[3:]

    def copy(i, slot, part, source):
        target = out_ref.at[pl.ds(slot * depth, depth), pl.ds((2 * i + part) * wide, wide)]
        return pltpu.make_async_copy(source, target, sems.at[i, slot, part])

    every = [(i, slot, part) for i in range(4) for slot in range(2) for part in range(2)]
    for near in range(2):
        for same in range(2):

            @pl.when((scalars[1] == near) & (scalars[2] == same))
            def _(near=near, same=same):
                for i, slot, part in every:
                    source = passed.at[i // 2] if i % 2 else groups[1 - near][i // 2 + 1 - same]
                    plane = jnp.bitwise_xor(scalars[3], slot)
                    copy(i, slot, part, source.at[plane, part]).start()

    for i, slot, part in every:
        copy(i, slot, part, passed.at[0, 0, 0]).wait()


def lay(scalars, *blocks):
    depth, wide = blocks[0].shape[2:]
    shape = (2 * depth, 8 * wide)
    return pl.pallas_call(
        lay_kernel,
        grid_spec=pltpu.PrefetchScalarGridSpec(
            num_scalar_prefetch=1,
            grid=(1,),
            in_specs=[pl.BlockSpec(memory_space=pl.ANY)] * len(blocks),
            out_specs=whole(shape),
            scratch_shapes=[pltpu.SemaphoreType.DMA((4, 2, 2))],
        ),
        out_shape=jax.ShapeDtypeStruct(shape, jnp.bfloat16),
        compiler_params=params(),
        name="lay",
    )(scalars, *blocks)


def combine_kernel(scalars, *refs):
    hidden = refs[:8]
    weights_ref, res_ref, dec_res_ref, out_ref, dec_ref, rows, sems = refs[8:]
    wide = hidden[0].shape[1]

    def copy(i, j):
        part = scalars[0] if j == 0 else 1 - scalars[0]
        at = pl.ds(pl.multiple_of((2 * i + part) * wide, wide), wide)
        source = hidden[4 * (i % 2) + 2 * (i // 2) + j]
        return pltpu.make_async_copy(source, rows.at[:, at], sems.at[i, j])

    every = [(i, j) for i in range(4) for j in range(2)]
    for i, j in every:
        copy(i, j).start()
    for i, j in every:
        copy(i, j).wait()
    total = lax.dot_general(
        rows[...], weights_ref[...], (((1,), (1,)), ((), ())), preferred_element_type=jnp.float32
    )
    groups, block = out_ref.shape[:2]
    for r in range(groups):
        out_ref[r] = (res_ref[r].astype(jnp.float32) + total[r * block : (r + 1) * block]).astype(jnp.bfloat16)
    for step in range(dec_ref.shape[0]):
        at = groups * block + step * groups
        dec_ref[step] = (dec_res_ref[step].astype(jnp.float32) + total[at : at + groups]).astype(jnp.bfloat16)


def combine(scalars, hidden, weights, res, dec_res):
    return pl.pallas_call(
        combine_kernel,
        grid_spec=pltpu.PrefetchScalarGridSpec(
            num_scalar_prefetch=1,
            grid=(1,),
            in_specs=[pl.BlockSpec(memory_space=pl.ANY)] * len(hidden)
            + [whole(weights.shape), whole(res.shape), whole(dec_res.shape)],
            out_specs=[whole(res.shape), whole(dec_res.shape)],
            scratch_shapes=[
                pltpu.VMEM((hidden[0].shape[0], weights.shape[1]), jnp.bfloat16),
                pltpu.SemaphoreType.DMA((4, 2)),
            ],
        ),
        out_shape=[
            jax.ShapeDtypeStruct(res.shape, jnp.bfloat16),
            jax.ShapeDtypeStruct(dec_res.shape, jnp.bfloat16),
        ],
        compiler_params=params(),
        name="combine",
    )(scalars, *hidden, weights, res, dec_res)


def local_grid(
    spikes, dec_spikes, thresholds, in_scale, qkv_weight, out_weight, head_gain, prior_state, lengths
):
    groups, block, width = spikes.shape
    steps = dec_spikes.shape[0]
    all_heads, head = head_gain.shape
    heads = all_heads // 2
    planes = lax.axis_size("rep")
    c, t, z = (lax.axis_index(name) for name in AXES)
    parity = t & 1
    y = t >> 1
    is_end = (z == 0) | (z == planes - 1)
    end = is_end.astype(jnp.int32)
    third = jnp.where(is_end, z ^ 2, z ^ 3)
    fourth = jnp.where(is_end, z ^ 3, z ^ 2)
    near_used = (z >> 1) == parity
    scalars = jnp.stack([c, end, parity, z, z ^ 1, third, fourth, near_used, c == y]).astype(jnp.int32)

    def meet(c, t, r):
        return (1 - c, t, r) if c == t // 2 else (c, t ^ 2, r)

    def corner(c, t, r):
        return None if c == t // 2 else (1 - c, t ^ 2, r)

    kept, given = split(scalars, qkv_weight, out_weight.T)
    pair_kept = move(kept, to_pair, "pair_kept")
    mid1_kept = move(kept, mid_swap, "mid1_kept")
    other = move(given, to_ctx, "pre_w")

    counts = spikes.reshape(groups * block, width)
    own_x = embed(counts, thresholds, in_scale, planes, block // 4)
    given_x = lax.dynamic_slice_in_dim(own_x, parity * block, block, 1)

    first_x = move(after(given_x, other), to_ctx, "x_ctx")

    stage = (pair_kept, mid1_kept, other, given_x)
    mid2_kept = move(after(pair_kept, *stage), mid_swap, "mid2_kept")
    end1_kept = move(after(mid1_kept, *stage), mid_to_end, "end1_kept")
    pair_other = move(after(other, *stage), to_pair, "pair_other")
    mid1_other = move(after(other, *stage), mid_swap, "mid1_other")
    dec_x = embed_steps(after(dec_spikes, *stage), thresholds, in_scale, planes)

    near_blocks = jnp.stack([after(kept, *stage)[3:], pair_kept[3:]])

    stage = (mid2_kept, end1_kept, pair_other, mid1_other, first_x, near_blocks, dec_x)
    end2_kept = move(after(mid2_kept, *stage), mid_to_end, "end2_kept")
    mid2_other = move(after(pair_other, *stage), mid_swap, "mid2_other")
    end1_other = move(after(mid1_other, mid2_other), mid_to_end, "end1_other")
    second_x = move(after(first_x, *stage), to_core, "x_core")
    xs = (own_x, first_x, second_x, dec_x)
    summed = project(scalars, 0, xs, (kept, pair_kept), (other, pair_other), None)

    def carry(blocks, name):
        return blocks, move(blocks, meet, name + "_meet"), move(blocks, corner, name + "_corner")

    third_kept = jnp.where(is_end, end1_kept, mid1_kept)
    near = carry(after(near_blocks, second_x, third_kept), "near")

    columns = width // lax.axis_size("tp")

    def gate(rows):
        part = lax.dynamic_slice_in_dim(rows, t * columns, columns, 2)
        level = lax.dynamic_slice_in_dim(thresholds, t * columns, columns, 0)
        scale = lax.dynamic_slice_in_dim(in_scale, t * columns, columns, 0)
        return (jnp.where(part >= level, part, 0).astype(jnp.float32) * scale).astype(jnp.bfloat16)

    res, dec_res = gate(after(spikes, second_x)), gate(after(dec_spikes, second_x))
    fourth_kept = jnp.where(is_end, after(end2_kept, summed), mid2_kept)
    far = carry(after(jnp.stack([third_kept[3:], fourth_kept[3:]]), near[1], near[2]), "far")
    stage = (mid2_other, end1_other, summed, res, dec_res)
    end2_other = move(after(mid2_other, *stage), mid_to_end, "end2_other")
    third_other = jnp.where(is_end, after(end1_other, *stage), mid1_other)
    summed = project(scalars, 2, xs, (third_kept,), (third_other,), summed)
    gain = lax.dynamic_slice_in_dim(head_gain, c * heads, heads, 0)

    flags = jnp.stack([c, near_used, c == y, jnp.where(near_used, z & 1, z >> 1)]).astype(jnp.int32)
    dims = (groups, block, heads, head, steps)
    own_rows, far_rows, passed = attend(
        scalars, xs, (fourth_kept,), (mid2_other, end2_other), summed, prior_state, gain, lengths, near + far, dims
    )
    h_ctx = move(far_rows, to_ctx, "h_ctx")
    h_y = move(own_rows, to_y, "h_y")
    h_diag = move(far_rows, to_diagonal, "h_diag")
    mine = [own_rows, h_ctx, h_y, h_diag]
    weights = lay(flags, *near, *far, move(passed, to_core, "out_core"))
    mine = [own_rows, h_ctx, h_y, h_diag]
    hidden = mine + [move(m, to_core, "h_core") for m in after_all(mine, weights)]
    return combine(flags, hidden, weights, res, dec_res)


def solution(mesh):
    return jax.shard_map(
        local_grid if fits(mesh) else local_any,
        mesh=mesh,
        in_specs=(
            P("rep", "ctx", None),
            P(None, "rep", None),
            P(),
            P(),
            P(None, ("ctx", "rep"), "tp"),
            P("tp", ("ctx", "rep")),
            P("tp", None),
            P("rep", "tp", None, None),
            P("rep"),
        ),
        out_specs=(P("rep", "ctx", "tp"), P(None, "rep", "tp")),
        check_vma=False,
    )
```

```python
import jax
import jax.numpy as jnp
from jax import lax
from jax.experimental import pallas as pl
from jax.experimental.pallas import tpu as pltpu
from jax.sharding import PartitionSpec as P


def carried_in(value, axis, combine, identity):
    peers, here = (lax.axis_size(axis), lax.axis_index(axis))
    everything = lax.all_gather(value, axis)
    start = jnp.broadcast_to(jnp.asarray(identity, value.dtype), value.shape)

    def turn(k, before):
        reached = k < here
        new = combine(before, everything[k])
        return jnp.where(reached, new, before)

    return lax.fori_loop(0, peers, turn, start)


def normalize(value_rows, gain):
    mean = jnp.mean(value_rows * value_rows, axis=-1, keepdims=True)
    return (value_rows * lax.rsqrt(mean + 1e-06) * gain).astype(jnp.bfloat16)


def local_any(
    spikes,
    dec_spikes,
    thresholds,
    in_scale,
    qkv_weight,
    out_weight,
    head_gain,
    prior_state,
    lengths,
):
    groups, block, width = spikes.shape
    steps = dec_spikes.shape[0]
    heads, head = head_gain.shape
    inner = heads * head
    prompt_rows = groups * block
    topmost_precision = lax.Precision.HIGHEST
    context_position = lax.axis_index("ctx")
    tokens_x = (jnp.where(spikes >= thresholds, spikes, 0).astype(jnp.float32) * in_scale).astype(
        jnp.bfloat16
    )
    dec_x = (
        jnp.where(dec_spikes >= thresholds, dec_spikes, 0).astype(jnp.float32) * in_scale
    ).astype(jnp.bfloat16)
    rows_all = jnp.concatenate(
        [tokens_x.reshape(prompt_rows, width), dec_x.reshape(steps * groups, width)], 0
    )
    full = lax.all_gather(qkv_weight, ("ctx", "rep"), axis=1, tiled=True)
    projected = jnp.einsum("rd,cde->rce", rows_all, full, preferred_element_type=jnp.float32)
    projected = projected.astype(jnp.bfloat16)
    prompt = projected[:prompt_rows].reshape(groups, block, 3, heads, head)
    decoded = projected[prompt_rows:].reshape(steps, groups, 3, heads, head)
    query = prompt[:, :, 0]
    value_rows = prompt[:, :, 2]
    positions = context_position * block + jnp.arange(block)
    live = positions[None, :] < lengths[:, None]
    keys = jnp.where(live[:, :, None, None], prompt[:, :, 1], jnp.zeros_like(prompt[:, :, 1]))
    block_state = jnp.einsum(
        "gthk,gthv->ghkv", keys, value_rows, preferred_element_type=jnp.float32
    )
    before = carried_in(
        block_state, "ctx", lambda earlier, later: earlier + later, jnp.zeros_like(block_state)
    )
    carried = (prior_state + before).astype(jnp.bfloat16)
    inter = jnp.einsum("gthk,ghkv->gthv", query, carried, preferred_element_type=jnp.float32)
    scores = jnp.einsum("gthk,gshk->ghts", query, keys, preferred_element_type=jnp.float32)
    causal = jnp.arange(block)[:, None] >= jnp.arange(block)[None, :]
    weights = jnp.where(causal, scores, 0.0).astype(jnp.bfloat16)
    intra = jnp.einsum("ghts,gshv->gthv", weights, value_rows, preferred_element_type=jnp.float32)
    hidden = normalize(inter + intra, head_gain).reshape(prompt_rows, inner)
    dec_query = decoded[:, :, 0].astype(jnp.float32)
    dec_keys = decoded[:, :, 1].astype(jnp.float32)
    dec_values = decoded[:, :, 2].astype(jnp.float32)
    state_readouts = []
    memory_state = prior_state + lax.psum(block_state, "ctx")
    for decode_step_body in range(steps):
        memory_state = memory_state + jnp.einsum(
            "ghk,ghv->ghkv",
            dec_keys[decode_step_body],
            dec_values[decode_step_body],
            precision=topmost_precision,
        )
        state_readouts.append(
            jnp.einsum(
                "ghk,ghkv->ghv",
                dec_query[decode_step_body],
                memory_state,
                precision=topmost_precision,
            )
        )
    dec_hidden = normalize(jnp.stack(state_readouts), head_gain).reshape(steps * groups, inner)
    hidden_all = jnp.concatenate([hidden, dec_hidden], 0)
    columns = width // lax.axis_size("tp")
    residual = lax.dynamic_slice_in_dim(rows_all, lax.axis_index("tp") * columns, columns, 1)
    terms = jnp.dot(
        hidden_all,
        lax.all_gather(out_weight, ("ctx", "rep"), axis=1, tiled=True),
        preferred_element_type=jnp.float32,
    )
    summed = lax.psum_scatter(terms, "tp", scatter_dimension=1, tiled=True)
    result = (residual.astype(jnp.float32) + summed).astype(jnp.bfloat16)
    block_out = result[:prompt_rows].reshape(groups, block, columns)
    decode_out = result[prompt_rows:].reshape(steps, groups, columns)
    return (block_out, decode_out)


AXES = ("ctx", "tp", "rep")
VMEM_LIMIT = 24 * 1024 * 1024
DEC_PAD = 16


def fits(mesh):
    shape = dict(mesh.shape)
    return (shape["ctx"], shape["tp"], shape["rep"]) == (2, 4, 4)


def move(value, target, name="move"):
    sizes = [lax.axis_size(name) for name in AXES]
    pairs = []
    for c in range(sizes[0]):
        for t in range(sizes[1]):
            for r in range(sizes[2]):
                to = target(c, t, r)
                if to is not None:
                    at = (c * sizes[1] + t) * sizes[2] + r
                    pairs.append((at, (to[0] * sizes[1] + to[1]) * sizes[2] + to[2]))
    with jax.named_scope(name):
        return lax.ppermute(value, AXES, pairs)


def after(value, *earlier):
    return lax.optimization_barrier((value, *earlier))[0]


def after_all(values, *earlier):
    return lax.optimization_barrier((*values, *earlier))[: len(values)]


def to_ctx(c, t, r):
    return (1 - c, t, r)


def to_core(c, t, r):
    return (c, t ^ 1, r)


def to_y(c, t, r):
    return (c, t ^ 2, r)


def to_diagonal(c, t, r):
    return (1 - c, t ^ 2, r)


def to_pair(c, t, r):
    return (c, t, r ^ 1)


def mid_swap(c, t, r):
    return (c, t, 3 - r) if r in (1, 2) else None


def mid_to_end(c, t, r):
    return (c, t, r ^ 1) if r in (1, 2) else None


def params():
    return pltpu.CompilerParams(vmem_limit_bytes=VMEM_LIMIT)


def whole(shape):
    return pl.BlockSpec(shape, lambda *_: (0,) * len(shape))


def split_kernel(scalars, kept_in, given_in, out_in, kept_ref, given_ref):
    kinds = kept_in.shape[0]
    kept_ref[:kinds] = kept_in[...]
    given_ref[...] = given_in[...]
    wide = kept_ref.shape[2]
    for half in range(kept_ref.shape[0] - kinds):
        kept_ref[kinds + half] = out_in[:, half * wide : (half + 1) * wide]


def split(scalars, weight, out_weight):
    kinds, rows, columns = weight.shape
    wide = columns // 2
    half = (kinds, rows, wide)
    kept = (kinds + out_weight.shape[1] // wide, rows, wide)
    return pl.pallas_call(
        split_kernel,
        grid_spec=pltpu.PrefetchScalarGridSpec(
            num_scalar_prefetch=1,
            grid=(1,),
            in_specs=[
                pl.BlockSpec(half, lambda i, s: (0, 0, s[0])),
                pl.BlockSpec(half, lambda i, s: (0, 0, 1 - s[0])),
                whole(out_weight.shape),
            ],
            out_specs=[whole(kept), whole(half)],
        ),
        out_shape=[jax.ShapeDtypeStruct(kept, weight.dtype), jax.ShapeDtypeStruct(half, weight.dtype)],
        compiler_params=params(),
        name="split",
    )(scalars, weight, weight, out_weight)


def embed_kernel(parts, spikes_ref, thresholds_ref, scale_ref, out_ref):
    place(parts, spikes_ref[...], thresholds_ref, scale_ref, out_ref)


def embed_steps_kernel(parts, spikes_ref, thresholds_ref, scale_ref, out_ref):
    steps, groups, width = spikes_ref.shape
    rows = [spikes_ref[step] for step in range(steps)]
    rows.append(jnp.zeros((DEC_PAD - steps * groups, width), spikes_ref.dtype))
    place(parts, jnp.concatenate(rows, axis=0), thresholds_ref, scale_ref, out_ref)


def embed_steps(spikes, thresholds, scale, parts):
    width = spikes.shape[2]
    return pl.pallas_call(
        lambda *refs: embed_steps_kernel(parts, *refs),
        out_shape=jax.ShapeDtypeStruct((parts, DEC_PAD, width // parts), jnp.bfloat16),
        compiler_params=params(),
        name="embed_steps",
    )(spikes, thresholds, scale)


def place(parts, counts, thresholds_ref, scale_ref, out_ref):
    gated = jnp.where(counts >= thresholds_ref[...][None], counts, 0)
    x = (gated.astype(jnp.float32) * scale_ref[...][None]).astype(jnp.bfloat16)
    width = x.shape[1] // (2 * parts)
    for z in range(parts):
        first = x[:, z * width : (z + 1) * width]
        second = x[:, (parts + z) * width : (parts + z + 1) * width]
        out_ref[z] = jnp.concatenate([first, second], axis=1)


def embed(spikes, thresholds, scale, parts, tile):
    rows, width = spikes.shape
    return pl.pallas_call(
        lambda *refs: embed_kernel(parts, *refs),
        grid=(rows // tile,),
        in_specs=[
            pl.BlockSpec((tile, width), lambda i: (i, 0)),
            whole((width,)),
            whole((width,)),
        ],
        out_specs=pl.BlockSpec((parts, tile, width // parts), lambda i: (0, i, 0)),
        out_shape=jax.ShapeDtypeStruct((parts, rows, width // parts), jnp.bfloat16),
        compiler_params=params(),
        name="embed",
    )(spikes, thresholds, scale)


def weights_of(scalars, mine, other, index):
    def pick(refs):
        return refs[0][index] if len(refs) == 1 else jnp.where(scalars[1] == 1, refs[1][index], refs[0][index])

    own, far = pick(mine), pick(other)
    first = scalars[0] == 0
    return jnp.concatenate([jnp.where(first, own, far), jnp.where(first, far, own)], axis=0)


def row_blocks(x_refs):
    at = 0
    for ref in x_refs:
        rows = ref.shape[1]
        yield ref, at, rows
        at += rows


def project_kernel(steps, has_sum, scalars, *refs):
    x_refs, out_ref = refs[:4], refs[-1]
    mine, other = refs[4 : 4 + steps], refs[4 + steps : 4 + 2 * steps]
    for step in range(steps):

        @pl.when(pl.program_id(0) == step)
        def _(step=step):
            for index in range(3):
                weight = weights_of(scalars, mine[step : step + 1], other[step : step + 1], index)
                columns = slice(index * weight.shape[1], (index + 1) * weight.shape[1])
                for ref, at, rows in row_blocks(x_refs):
                    term = jnp.dot(ref[0], weight, preferred_element_type=jnp.float32)
                    if step or has_sum:
                        term = (out_ref if step else refs[-2])[at : at + rows, columns] + term
                    out_ref[at : at + rows, columns] = term


def part_spec(array, step):
    block = (1,) + array.shape[1:]
    return pl.BlockSpec(block, lambda i, scalars: (scalars[3 + step + i], 0, 0))


def project(scalars, first, xs, mine, other, summed):
    steps = len(mine)
    rows = sum(x.shape[1] for x in xs)
    columns = 3 * mine[0].shape[2]
    earlier = [] if summed is None else [summed]
    return pl.pallas_call(
        lambda *refs: project_kernel(steps, bool(earlier), *refs),
        grid_spec=pltpu.PrefetchScalarGridSpec(
            num_scalar_prefetch=1,
            grid=(steps,),
            in_specs=[part_spec(x, first) for x in xs]
            + [whole(other[0].shape) for _ in (*mine, *other)]
            + [whole(sums.shape) for sums in earlier],
            out_specs=whole((rows, columns)),
        ),
        out_shape=jax.ShapeDtypeStruct((rows, columns), jnp.float32),
        compiler_params=params(),
        name="project",
    )(scalars, *xs, *mine, *other, *earlier)


def attend_kernel(dims, scalars, *refs):
    own_x, first_x, second_x, dec_x, mine, other0, other1, sum_ref, prior_ref, gain_ref, lengths = refs[:11]
    sets, near_ref, far_ref, passed_ref, qkv, held, sems = (refs[11:14], refs[14:17]), *refs[17:]

    def copy(half, source):
        return pltpu.make_async_copy(source, held.at[half], sems.at[half])

    for near in range(2):
        for same in range(2):

            @pl.when((scalars[7] == near) & (scalars[8] == same))
            def _(near=near, same=same):
                for half in range(2):
                    copy(half, sets[near][half + 1 - same]).start()

    groups, block, heads, head, steps = dims
    for index in range(3):
        weight = weights_of(scalars, (mine,), (other0, other1), index)
        columns = slice(index * weight.shape[1], (index + 1) * weight.shape[1])
        for ref, at, rows in row_blocks((own_x, first_x, second_x, dec_x)):
            term = jnp.dot(ref[0], weight, preferred_element_type=jnp.float32)
            qkv[at : at + rows, columns] = (sum_ref[at : at + rows, columns] + term).astype(jnp.bfloat16)
    for half in range(2):
        copy(half, sets[0][0]).wait()
    give = pltpu.make_async_copy(held, passed_ref, sems.at[2])
    give.start()
    here = scalars[0]
    parity = scalars[2]
    wide = heads * head
    prompt = 2 * groups * block
    causal = lax.broadcasted_iota(jnp.int32, (block, block), 0) >= lax.broadcasted_iota(jnp.int32, (block, block), 1)
    position = lax.broadcasted_iota(jnp.int32, (block, head), 0)
    row = lax.broadcasted_iota(jnp.int32, (DEC_PAD, DEC_PAD), 0)
    column = lax.broadcasted_iota(jnp.int32, (DEC_PAD, DEC_PAD), 1)
    reach = (row % groups == column % groups) & (column <= row)
    exact = lax.Precision.HIGHEST
    inner = (((0,), (0,)), ((), ()))
    across = (((1,), (1,)), ((), ()))

    def finish(value, gain):
        mean = jnp.mean(value * value, axis=-1, keepdims=True)
        return (value * lax.rsqrt(mean + 1e-06) * gain).astype(jnp.bfloat16)

    for h in range(heads):
        cols = [slice(i * wide + h * head, i * wide + (h + 1) * head) for i in range(3)]
        gain = gain_ref[h : h + 1, :]
        dq = qkv[prompt : prompt + DEC_PAD, cols[0]]
        dk = qkv[prompt : prompt + DEC_PAD, cols[1]]
        dv = qkv[prompt : prompt + DEC_PAD, cols[2]].astype(jnp.float32)
        dq32 = dq.astype(jnp.float32)
        pairs = lax.dot_general(dq, dk, across, preferred_element_type=jnp.float32)
        read = jnp.dot(jnp.where(reach, pairs, 0.0), dv, precision=exact, preferred_element_type=jnp.float32)
        dec_group = lax.broadcasted_iota(jnp.int32, (DEC_PAD, head), 0) % groups
        for r in range(groups):
            prior = prior_ref[r, h]
            starts = (r * block, groups * block + pl.multiple_of((r ^ parity) * block, block))
            run = (here, 1 - here)
            keys, values, states = [], [], []
            for start, b in zip(starts, run):
                k = qkv[pl.ds(start, block), cols[1]]
                live = b * block + position < lengths[r]
                k = jnp.where(live, k, jnp.zeros_like(k))
                v = qkv[pl.ds(start, block), cols[2]]
                keys.append(k)
                values.append(v)
                states.append(lax.dot_general(k, v, inner, preferred_element_type=jnp.float32))
            before = (jnp.where(here == 1, states[1], 0.0), jnp.where(here == 0, states[0], 0.0))
            for side, out_ref in enumerate((near_ref, far_ref)):
                q = qkv[pl.ds(starts[side], block), cols[0]]
                carried = (prior + before[side]).astype(jnp.bfloat16)
                scores = lax.dot_general(q, keys[side], across, preferred_element_type=jnp.float32)
                weights = jnp.where(causal, scores, 0.0).astype(jnp.bfloat16)
                attended = jnp.dot(q, carried, preferred_element_type=jnp.float32) + jnp.dot(
                    weights, values[side], preferred_element_type=jnp.float32
                )
                out_ref[r * block : (r + 1) * block, h * head : (h + 1) * head] = finish(attended, gain)
            state = prior + (states[0] + states[1])
            inter = jnp.dot(dq32, state, precision=exact, preferred_element_type=jnp.float32)
            read = read + jnp.where(dec_group == r, inter, 0.0)
        done = finish(read, gain)
        near_ref[groups * block :, h * head : (h + 1) * head] = done
        far_ref[groups * block :, h * head : (h + 1) * head] = done
    give.wait()


def attend(scalars, xs, mine, other, summed, prior, gain, lengths, blocks, dims):
    groups, block, heads, head, _ = dims
    rows, columns = summed.shape
    shape = (groups * block + DEC_PAD, heads * head)
    in_specs = [part_spec(x, 3) for x in xs]
    in_specs += [whole(other[0].shape) for _ in (*mine, *other)] + [whole(summed.shape)]
    in_specs += [
        pl.BlockSpec((groups, heads, head, head), lambda i, s: (0, s[0], 0, 0)),
        whole(gain.shape),
        pl.BlockSpec(memory_space=pltpu.SMEM),
    ]
    in_specs += [pl.BlockSpec(memory_space=pl.ANY)] * len(blocks)
    passed = (2, *blocks[0].shape)
    out = jax.ShapeDtypeStruct(shape, jnp.bfloat16)
    return pl.pallas_call(
        lambda *refs: attend_kernel(dims, *refs),
        grid_spec=pltpu.PrefetchScalarGridSpec(
            num_scalar_prefetch=1,
            grid=(1,),
            in_specs=in_specs,
            out_specs=[whole(shape), whole(shape), pl.BlockSpec(memory_space=pl.ANY)],
            scratch_shapes=[
                pltpu.VMEM((rows, columns), jnp.bfloat16),
                pltpu.VMEM(passed, jnp.bfloat16),
                pltpu.SemaphoreType.DMA((3,)),
            ],
        ),
        out_shape=[out, out, jax.ShapeDtypeStruct(passed, jnp.bfloat16)],
        compiler_params=params(),
        cost_estimate=pl.CostEstimate(
            flops=2 * rows * columns * xs[0].shape[2] * 2, bytes_accessed=4 * rows * columns, transcendentals=0
        ),
        name="attend",
    )(scalars, *xs, *mine, *other, summed, prior, gain, lengths, *blocks)


def lay_kernel(scalars, *refs):
    groups, passed, out_ref, sems = (refs[:3], refs[3:6]), refs[6], refs[7], refs[8]
    depth, wide = passed.shape[3:]

    def copy(i, slot, part, source):
        target = out_ref.at[pl.ds(slot * depth, depth), pl.ds((2 * i + part) * wide, wide)]
        return pltpu.make_async_copy(source, target, sems.at[i, slot, part])

    every = [(i, slot, part) for i in range(4) for slot in range(2) for part in range(2)]
    for near in range(2):
        for same in range(2):

            @pl.when((scalars[1] == near) & (scalars[2] == same))
            def _(near=near, same=same):
                for i, slot, part in every:
                    source = passed.at[i // 2] if i % 2 else groups[1 - near][i // 2 + 1 - same]
                    plane = jnp.bitwise_xor(scalars[3], slot)
                    copy(i, slot, part, source.at[plane, part]).start()

    for i, slot, part in every:
        copy(i, slot, part, passed.at[0, 0, 0]).wait()


def lay(scalars, *blocks):
    depth, wide = blocks[0].shape[2:]
    shape = (2 * depth, 8 * wide)
    return pl.pallas_call(
        lay_kernel,
        grid_spec=pltpu.PrefetchScalarGridSpec(
            num_scalar_prefetch=1,
            grid=(1,),
            in_specs=[pl.BlockSpec(memory_space=pl.ANY)] * len(blocks),
            out_specs=whole(shape),
            scratch_shapes=[pltpu.SemaphoreType.DMA((4, 2, 2))],
        ),
        out_shape=jax.ShapeDtypeStruct(shape, jnp.bfloat16),
        compiler_params=params(),
        name="lay",
    )(scalars, *blocks)


def combine_kernel(scalars, *refs):
    hidden = refs[:8]
    weights_ref, res_ref, dec_res_ref, out_ref, dec_ref, rows, sems = refs[8:]
    wide = hidden[0].shape[1]

    def copy(i, j):
        part = scalars[0] if j == 0 else 1 - scalars[0]
        at = pl.ds(pl.multiple_of((2 * i + part) * wide, wide), wide)
        source = hidden[4 * (i % 2) + 2 * (i // 2) + j]
        return pltpu.make_async_copy(source, rows.at[:, at], sems.at[i, j])

    every = [(i, j) for i in range(4) for j in range(2)]
    for i, j in every:
        copy(i, j).start()
    for i, j in every:
        copy(i, j).wait()
    total = lax.dot_general(
        rows[...], weights_ref[...], (((1,), (1,)), ((), ())), preferred_element_type=jnp.float32
    )
    groups, block = out_ref.shape[:2]
    for r in range(groups):
        out_ref[r] = (res_ref[r].astype(jnp.float32) + total[r * block : (r + 1) * block]).astype(jnp.bfloat16)
    for step in range(dec_ref.shape[0]):
        at = groups * block + step * groups
        dec_ref[step] = (dec_res_ref[step].astype(jnp.float32) + total[at : at + groups]).astype(jnp.bfloat16)


def combine(scalars, hidden, weights, res, dec_res):
    return pl.pallas_call(
        combine_kernel,
        grid_spec=pltpu.PrefetchScalarGridSpec(
            num_scalar_prefetch=1,
            grid=(1,),
            in_specs=[pl.BlockSpec(memory_space=pl.ANY)] * len(hidden)
            + [whole(weights.shape), whole(res.shape), whole(dec_res.shape)],
            out_specs=[whole(res.shape), whole(dec_res.shape)],
            scratch_shapes=[
                pltpu.VMEM((hidden[0].shape[0], weights.shape[1]), jnp.bfloat16),
                pltpu.SemaphoreType.DMA((4, 2)),
            ],
        ),
        out_shape=[
            jax.ShapeDtypeStruct(res.shape, jnp.bfloat16),
            jax.ShapeDtypeStruct(dec_res.shape, jnp.bfloat16),
        ],
        compiler_params=params(),
        name="combine",
    )(scalars, *hidden, weights, res, dec_res)


def local_grid(
    spikes, dec_spikes, thresholds, in_scale, qkv_weight, out_weight, head_gain, prior_state, lengths
):
    groups, block, width = spikes.shape
    steps = dec_spikes.shape[0]
    all_heads, head = head_gain.shape
    heads = all_heads // 2
    planes = lax.axis_size("rep")
    c, t, z = (lax.axis_index(name) for name in AXES)
    parity = t & 1
    y = t >> 1
    is_end = (z == 0) | (z == planes - 1)
    end = is_end.astype(jnp.int32)
    third = jnp.where(is_end, z ^ 2, z ^ 3)
    fourth = jnp.where(is_end, z ^ 3, z ^ 2)
    near_used = (z >> 1) == parity
    scalars = jnp.stack([c, end, parity, z, z ^ 1, third, fourth, near_used, c == y]).astype(jnp.int32)

    def meet(c, t, r):
        return (1 - c, t, r) if c == t // 2 else (c, t ^ 2, r)

    def corner(c, t, r):
        return None if c == t // 2 else (1 - c, t ^ 2, r)

    kept, given = split(scalars, qkv_weight, out_weight.T)
    pair_kept = move(kept, to_pair, "pair_kept")
    mid1_kept = move(kept, mid_swap, "mid1_kept")
    other = move(given, to_ctx, "pre_w")

    counts = spikes.reshape(groups * block, width)
    own_x = embed(counts, thresholds, in_scale, planes, block // 4)
    given_x = lax.dynamic_slice_in_dim(own_x, parity * block, block, 1)

    first_x = move(after(given_x, other), to_ctx, "x_ctx")

    pair_other = move(after(other, given_x), to_pair, "pair_other")
    mid1_other = move(after(other, given_x), mid_swap, "mid1_other")
    stage = (pair_kept, mid1_kept, other, given_x)
    mid2_kept = move(after(pair_kept, mid1_other, *stage), mid_swap, "mid2_kept")
    end1_kept = move(after(mid1_kept, pair_other, *stage), mid_to_end, "end1_kept")
    dec_x = embed_steps(after(dec_spikes, *stage), thresholds, in_scale, planes)

    near_blocks = jnp.stack([after(kept, *stage)[3:], pair_kept[3:]])

    stage = (mid2_kept, end1_kept, pair_other, mid1_other, first_x, near_blocks, dec_x)
    end2_kept = move(after(mid2_kept, *stage), mid_to_end, "end2_kept")
    mid2_other = move(after(pair_other, *stage), mid_swap, "mid2_other")
    end1_other = move(after(mid1_other, mid2_other), mid_to_end, "end1_other")
    second_x = move(after(first_x, *stage), to_core, "x_core")
    xs = (own_x, first_x, second_x, dec_x)
    summed = project(scalars, 0, xs, (kept, pair_kept), (other, pair_other), None)

    def carry(blocks, name):
        return blocks, move(blocks, meet, name + "_meet"), move(blocks, corner, name + "_corner")

    third_kept = jnp.where(is_end, end1_kept, mid1_kept)
    near = carry(after(near_blocks, second_x, third_kept), "near")

    columns = width // lax.axis_size("tp")

    def gate(rows):
        part = lax.dynamic_slice_in_dim(rows, t * columns, columns, 2)
        level = lax.dynamic_slice_in_dim(thresholds, t * columns, columns, 0)
        scale = lax.dynamic_slice_in_dim(in_scale, t * columns, columns, 0)
        return (jnp.where(part >= level, part, 0).astype(jnp.float32) * scale).astype(jnp.bfloat16)

    res, dec_res = gate(after(spikes, second_x)), gate(after(dec_spikes, second_x))
    fourth_kept = jnp.where(is_end, after(end2_kept, summed), mid2_kept)
    far = carry(after(jnp.stack([third_kept[3:], fourth_kept[3:]]), near[1], near[2]), "far")
    stage = (mid2_other, end1_other, summed, res, dec_res)
    end2_other = move(after(mid2_other, fourth_kept), mid_to_end, "end2_other")
    third_other = jnp.where(is_end, after(end1_other, *stage), mid1_other)
    summed = project(scalars, 2, xs, (third_kept,), (third_other,), summed)
    gain = lax.dynamic_slice_in_dim(head_gain, c * heads, heads, 0)

    flags = jnp.stack([c, near_used, c == y, jnp.where(near_used, z & 1, z >> 1)]).astype(jnp.int32)
    dims = (groups, block, heads, head, steps)
    own_rows, far_rows, passed = attend(
        scalars, xs, (fourth_kept,), (mid2_other, end2_other), summed, prior_state, gain, lengths, near + far, dims
    )
    h_ctx = move(far_rows, to_ctx, "h_ctx")
    h_y = move(own_rows, to_y, "h_y")
    h_diag = move(far_rows, to_diagonal, "h_diag")
    mine = [own_rows, h_ctx, h_y, h_diag]
    weights = lay(flags, *near, *far, move(passed, to_core, "out_core"))
    mine = [own_rows, h_ctx, h_y, h_diag]
    hidden = mine + [move(m, to_core, "h_core") for m in after_all(mine, weights)]
    return combine(flags, hidden, weights, res, dec_res)


def solution(mesh):
    return jax.shard_map(
        local_grid if fits(mesh) else local_any,
        mesh=mesh,
        in_specs=(
            P("rep", "ctx", None),
            P(None, "rep", None),
            P(),
            P(),
            P(None, ("ctx", "rep"), "tp"),
            P("tp", ("ctx", "rep")),
            P("tp", None),
            P("rep", "tp", None, None),
            P("rep"),
        ),
        out_specs=(P("rep", "ctx", "tp"), P(None, "rep", "tp")),
        check_vma=False,
    )
```

```python
import jax
import jax.numpy as jnp
from jax import lax
from jax.experimental import pallas as pl
from jax.experimental.pallas import tpu as pltpu
from jax.sharding import PartitionSpec as P


def carried_in(value, axis, combine, identity):
    peers, here = (lax.axis_size(axis), lax.axis_index(axis))
    everything = lax.all_gather(value, axis)
    start = jnp.broadcast_to(jnp.asarray(identity, value.dtype), value.shape)

    def turn(k, before):
        reached = k < here
        new = combine(before, everything[k])
        return jnp.where(reached, new, before)

    return lax.fori_loop(0, peers, turn, start)


def normalize(value_rows, gain):
    mean = jnp.mean(value_rows * value_rows, axis=-1, keepdims=True)
    return (value_rows * lax.rsqrt(mean + 1e-06) * gain).astype(jnp.bfloat16)


def local_any(
    spikes,
    dec_spikes,
    thresholds,
    in_scale,
    qkv_weight,
    out_weight,
    head_gain,
    prior_state,
    lengths,
):
    groups, block, width = spikes.shape
    steps = dec_spikes.shape[0]
    heads, head = head_gain.shape
    inner = heads * head
    prompt_rows = groups * block
    topmost_precision = lax.Precision.HIGHEST
    context_position = lax.axis_index("ctx")
    tokens_x = (jnp.where(spikes >= thresholds, spikes, 0).astype(jnp.float32) * in_scale).astype(
        jnp.bfloat16
    )
    dec_x = (
        jnp.where(dec_spikes >= thresholds, dec_spikes, 0).astype(jnp.float32) * in_scale
    ).astype(jnp.bfloat16)
    rows_all = jnp.concatenate(
        [tokens_x.reshape(prompt_rows, width), dec_x.reshape(steps * groups, width)], 0
    )
    full = lax.all_gather(qkv_weight, ("ctx", "rep"), axis=1, tiled=True)
    projected = jnp.einsum("rd,cde->rce", rows_all, full, preferred_element_type=jnp.float32)
    projected = projected.astype(jnp.bfloat16)
    prompt = projected[:prompt_rows].reshape(groups, block, 3, heads, head)
    decoded = projected[prompt_rows:].reshape(steps, groups, 3, heads, head)
    query = prompt[:, :, 0]
    value_rows = prompt[:, :, 2]
    positions = context_position * block + jnp.arange(block)
    live = positions[None, :] < lengths[:, None]
    keys = jnp.where(live[:, :, None, None], prompt[:, :, 1], jnp.zeros_like(prompt[:, :, 1]))
    block_state = jnp.einsum(
        "gthk,gthv->ghkv", keys, value_rows, preferred_element_type=jnp.float32
    )
    before = carried_in(
        block_state, "ctx", lambda earlier, later: earlier + later, jnp.zeros_like(block_state)
    )
    carried = (prior_state + before).astype(jnp.bfloat16)
    inter = jnp.einsum("gthk,ghkv->gthv", query, carried, preferred_element_type=jnp.float32)
    scores = jnp.einsum("gthk,gshk->ghts", query, keys, preferred_element_type=jnp.float32)
    causal = jnp.arange(block)[:, None] >= jnp.arange(block)[None, :]
    weights = jnp.where(causal, scores, 0.0).astype(jnp.bfloat16)
    intra = jnp.einsum("ghts,gshv->gthv", weights, value_rows, preferred_element_type=jnp.float32)
    hidden = normalize(inter + intra, head_gain).reshape(prompt_rows, inner)
    dec_query = decoded[:, :, 0].astype(jnp.float32)
    dec_keys = decoded[:, :, 1].astype(jnp.float32)
    dec_values = decoded[:, :, 2].astype(jnp.float32)
    state_readouts = []
    memory_state = prior_state + lax.psum(block_state, "ctx")
    for decode_step_body in range(steps):
        memory_state = memory_state + jnp.einsum(
            "ghk,ghv->ghkv",
            dec_keys[decode_step_body],
            dec_values[decode_step_body],
            precision=topmost_precision,
        )
        state_readouts.append(
            jnp.einsum(
                "ghk,ghkv->ghv",
                dec_query[decode_step_body],
                memory_state,
                precision=topmost_precision,
            )
        )
    dec_hidden = normalize(jnp.stack(state_readouts), head_gain).reshape(steps * groups, inner)
    hidden_all = jnp.concatenate([hidden, dec_hidden], 0)
    columns = width // lax.axis_size("tp")
    residual = lax.dynamic_slice_in_dim(rows_all, lax.axis_index("tp") * columns, columns, 1)
    terms = jnp.dot(
        hidden_all,
        lax.all_gather(out_weight, ("ctx", "rep"), axis=1, tiled=True),
        preferred_element_type=jnp.float32,
    )
    summed = lax.psum_scatter(terms, "tp", scatter_dimension=1, tiled=True)
    result = (residual.astype(jnp.float32) + summed).astype(jnp.bfloat16)
    block_out = result[:prompt_rows].reshape(groups, block, columns)
    decode_out = result[prompt_rows:].reshape(steps, groups, columns)
    return (block_out, decode_out)


AXES = ("ctx", "tp", "rep")
VMEM_LIMIT = 24 * 1024 * 1024
DEC_PAD = 16


def fits(mesh):
    shape = dict(mesh.shape)
    return (shape["ctx"], shape["tp"], shape["rep"]) == (2, 4, 4)


def move(value, target, name="move"):
    sizes = [lax.axis_size(name) for name in AXES]
    pairs = []
    for c in range(sizes[0]):
        for t in range(sizes[1]):
            for r in range(sizes[2]):
                to = target(c, t, r)
                if to is not None:
                    at = (c * sizes[1] + t) * sizes[2] + r
                    pairs.append((at, (to[0] * sizes[1] + to[1]) * sizes[2] + to[2]))
    with jax.named_scope(name):
        return lax.ppermute(value, AXES, pairs)


def after(value, *earlier):
    return lax.optimization_barrier((value, *earlier))[0]


def after_all(values, *earlier):
    return lax.optimization_barrier((*values, *earlier))[: len(values)]


def to_ctx(c, t, r):
    return (1 - c, t, r)


def to_core(c, t, r):
    return (c, t ^ 1, r)


def to_y(c, t, r):
    return (c, t ^ 2, r)


def to_diagonal(c, t, r):
    return (1 - c, t ^ 2, r)


def to_pair(c, t, r):
    return (c, t, r ^ 1)


def mid_swap(c, t, r):
    return (c, t, 3 - r) if r in (1, 2) else None


def mid_to_end(c, t, r):
    return (c, t, r ^ 1) if r in (1, 2) else None


def params():
    return pltpu.CompilerParams(vmem_limit_bytes=VMEM_LIMIT)


def whole(shape):
    return pl.BlockSpec(shape, lambda *_: (0,) * len(shape))


def split_kernel(scalars, kept_in, given_in, out_in, kept_ref, given_ref):
    kinds = kept_in.shape[0]
    kept_ref[:kinds] = kept_in[...]
    given_ref[...] = given_in[...]
    wide = kept_ref.shape[2]
    for half in range(kept_ref.shape[0] - kinds):
        kept_ref[kinds + half] = out_in[:, half * wide : (half + 1) * wide]


def split(scalars, weight, out_weight):
    kinds, rows, columns = weight.shape
    wide = columns // 2
    half = (kinds, rows, wide)
    kept = (kinds + out_weight.shape[1] // wide, rows, wide)
    return pl.pallas_call(
        split_kernel,
        grid_spec=pltpu.PrefetchScalarGridSpec(
            num_scalar_prefetch=1,
            grid=(1,),
            in_specs=[
                pl.BlockSpec(half, lambda i, s: (0, 0, s[0])),
                pl.BlockSpec(half, lambda i, s: (0, 0, 1 - s[0])),
                whole(out_weight.shape),
            ],
            out_specs=[whole(kept), whole(half)],
        ),
        out_shape=[jax.ShapeDtypeStruct(kept, weight.dtype), jax.ShapeDtypeStruct(half, weight.dtype)],
        compiler_params=params(),
        name="split",
    )(scalars, weight, weight, out_weight)


def embed_kernel(parts, spikes_ref, thresholds_ref, scale_ref, out_ref):
    place(parts, spikes_ref[...], thresholds_ref, scale_ref, out_ref)


def embed_steps_kernel(parts, spikes_ref, thresholds_ref, scale_ref, out_ref):
    steps, groups, width = spikes_ref.shape
    rows = [spikes_ref[step] for step in range(steps)]
    rows.append(jnp.zeros((DEC_PAD - steps * groups, width), spikes_ref.dtype))
    place(parts, jnp.concatenate(rows, axis=0), thresholds_ref, scale_ref, out_ref)


def embed_steps(spikes, thresholds, scale, parts):
    width = spikes.shape[2]
    return pl.pallas_call(
        lambda *refs: embed_steps_kernel(parts, *refs),
        out_shape=jax.ShapeDtypeStruct((parts, DEC_PAD, width // parts), jnp.bfloat16),
        compiler_params=params(),
        name="embed_steps",
    )(spikes, thresholds, scale)


def place(parts, counts, thresholds_ref, scale_ref, out_ref):
    gated = jnp.where(counts >= thresholds_ref[...][None], counts, 0)
    x = (gated.astype(jnp.float32) * scale_ref[...][None]).astype(jnp.bfloat16)
    width = x.shape[1] // (2 * parts)
    for z in range(parts):
        first = x[:, z * width : (z + 1) * width]
        second = x[:, (parts + z) * width : (parts + z + 1) * width]
        out_ref[z] = jnp.concatenate([first, second], axis=1)


def embed(spikes, thresholds, scale, parts, tile):
    rows, width = spikes.shape
    return pl.pallas_call(
        lambda *refs: embed_kernel(parts, *refs),
        grid=(rows // tile,),
        in_specs=[
            pl.BlockSpec((tile, width), lambda i: (i, 0)),
            whole((width,)),
            whole((width,)),
        ],
        out_specs=pl.BlockSpec((parts, tile, width // parts), lambda i: (0, i, 0)),
        out_shape=jax.ShapeDtypeStruct((parts, rows, width // parts), jnp.bfloat16),
        compiler_params=params(),
        name="embed",
    )(spikes, thresholds, scale)


def weights_of(scalars, mine, other, index):
    def pick(refs):
        return refs[0][index] if len(refs) == 1 else jnp.where(scalars[1] == 1, refs[1][index], refs[0][index])

    own, far = pick(mine), pick(other)
    first = scalars[0] == 0
    return jnp.concatenate([jnp.where(first, own, far), jnp.where(first, far, own)], axis=0)


def row_blocks(x_refs):
    at = 0
    for ref in x_refs:
        rows = ref.shape[1]
        yield ref, at, rows
        at += rows


def project_kernel(steps, has_sum, scalars, *refs):
    x_refs, out_ref = refs[:4], refs[-1]
    mine, other = refs[4 : 4 + steps], refs[4 + steps : 4 + 2 * steps]
    for step in range(steps):

        @pl.when(pl.program_id(0) == step)
        def _(step=step):
            for index in range(3):
                weight = weights_of(scalars, mine[step : step + 1], other[step : step + 1], index)
                columns = slice(index * weight.shape[1], (index + 1) * weight.shape[1])
                for ref, at, rows in row_blocks(x_refs):
                    term = jnp.dot(ref[0], weight, preferred_element_type=jnp.float32)
                    if step or has_sum:
                        term = (out_ref if step else refs[-2])[at : at + rows, columns] + term
                    out_ref[at : at + rows, columns] = term


def part_spec(array, step):
    block = (1,) + array.shape[1:]
    return pl.BlockSpec(block, lambda i, scalars: (scalars[3 + step + i], 0, 0))


def project(scalars, first, xs, mine, other, summed):
    steps = len(mine)
    rows = sum(x.shape[1] for x in xs)
    columns = 3 * mine[0].shape[2]
    earlier = [] if summed is None else [summed]
    return pl.pallas_call(
        lambda *refs: project_kernel(steps, bool(earlier), *refs),
        grid_spec=pltpu.PrefetchScalarGridSpec(
            num_scalar_prefetch=1,
            grid=(steps,),
            in_specs=[part_spec(x, first) for x in xs]
            + [whole(other[0].shape) for _ in (*mine, *other)]
            + [whole(sums.shape) for sums in earlier],
            out_specs=whole((rows, columns)),
        ),
        out_shape=jax.ShapeDtypeStruct((rows, columns), jnp.float32),
        compiler_params=params(),
        name="project",
    )(scalars, *xs, *mine, *other, *earlier)


def attend_kernel(dims, scalars, *refs):
    own_x, first_x, second_x, dec_x, mine, other0, other1, sum_ref, prior_ref, gain_ref, lengths = refs[:11]
    sets, near_ref, far_ref, passed_ref, qkv, held, sems = (refs[11:14], refs[14:17]), *refs[17:]

    def copy(half, source):
        return pltpu.make_async_copy(source, held.at[half], sems.at[half])

    for near in range(2):
        for same in range(2):

            @pl.when((scalars[7] == near) & (scalars[8] == same))
            def _(near=near, same=same):
                for half in range(2):
                    copy(half, sets[near][half + 1 - same]).start()

    groups, block, heads, head, steps = dims
    for index in range(3):
        weight = weights_of(scalars, (mine,), (other0, other1), index)
        columns = slice(index * weight.shape[1], (index + 1) * weight.shape[1])
        for ref, at, rows in row_blocks((own_x, first_x, second_x, dec_x)):
            term = jnp.dot(ref[0], weight, preferred_element_type=jnp.float32)
            qkv[at : at + rows, columns] = (sum_ref[at : at + rows, columns] + term).astype(jnp.bfloat16)
    for half in range(2):
        copy(half, sets[0][0]).wait()
    give = pltpu.make_async_copy(held, passed_ref, sems.at[2])
    give.start()
    here = scalars[0]
    parity = scalars[2]
    wide = heads * head
    prompt = 2 * groups * block
    causal = lax.broadcasted_iota(jnp.int32, (block, block), 0) >= lax.broadcasted_iota(jnp.int32, (block, block), 1)
    position = lax.broadcasted_iota(jnp.int32, (block, head), 0)
    row = lax.broadcasted_iota(jnp.int32, (DEC_PAD, DEC_PAD), 0)
    column = lax.broadcasted_iota(jnp.int32, (DEC_PAD, DEC_PAD), 1)
    reach = (row % groups == column % groups) & (column <= row)
    exact = lax.Precision.HIGHEST
    inner = (((0,), (0,)), ((), ()))
    across = (((1,), (1,)), ((), ()))

    def finish(value, gain):
        mean = jnp.mean(value * value, axis=-1, keepdims=True)
        return (value * lax.rsqrt(mean + 1e-06) * gain).astype(jnp.bfloat16)

    for h in range(heads):
        cols = [slice(i * wide + h * head, i * wide + (h + 1) * head) for i in range(3)]
        gain = gain_ref[h : h + 1, :]
        dq = qkv[prompt : prompt + DEC_PAD, cols[0]]
        dk = qkv[prompt : prompt + DEC_PAD, cols[1]]
        dv = qkv[prompt : prompt + DEC_PAD, cols[2]].astype(jnp.float32)
        dq32 = dq.astype(jnp.float32)
        pairs = lax.dot_general(dq, dk, across, preferred_element_type=jnp.float32)
        read = jnp.dot(jnp.where(reach, pairs, 0.0), dv, precision=exact, preferred_element_type=jnp.float32)
        dec_group = lax.broadcasted_iota(jnp.int32, (DEC_PAD, head), 0) % groups
        for r in range(groups):
            prior = prior_ref[r, h]
            starts = (r * block, groups * block + pl.multiple_of((r ^ parity) * block, block))
            run = (here, 1 - here)
            keys, values, states = [], [], []
            for start, b in zip(starts, run):
                k = qkv[pl.ds(start, block), cols[1]]
                live = b * block + position < lengths[r]
                k = jnp.where(live, k, jnp.zeros_like(k))
                v = qkv[pl.ds(start, block), cols[2]]
                keys.append(k)
                values.append(v)
                states.append(lax.dot_general(k, v, inner, preferred_element_type=jnp.float32))
            before = (jnp.where(here == 1, states[1], 0.0), jnp.where(here == 0, states[0], 0.0))
            for side, out_ref in enumerate((near_ref, far_ref)):
                q = qkv[pl.ds(starts[side], block), cols[0]]
                carried = (prior + before[side]).astype(jnp.bfloat16)
                scores = lax.dot_general(q, keys[side], across, preferred_element_type=jnp.float32)
                weights = jnp.where(causal, scores, 0.0).astype(jnp.bfloat16)
                attended = jnp.dot(q, carried, preferred_element_type=jnp.float32) + jnp.dot(
                    weights, values[side], preferred_element_type=jnp.float32
                )
                out_ref[r * block : (r + 1) * block, h * head : (h + 1) * head] = finish(attended, gain)
            state = prior + (states[0] + states[1])
            inter = jnp.dot(dq32, state, precision=exact, preferred_element_type=jnp.float32)
            read = read + jnp.where(dec_group == r, inter, 0.0)
        done = finish(read, gain)
        near_ref[groups * block :, h * head : (h + 1) * head] = done
        far_ref[groups * block :, h * head : (h + 1) * head] = done
    give.wait()


def attend(scalars, xs, mine, other, summed, prior, gain, lengths, blocks, dims):
    groups, block, heads, head, _ = dims
    rows, columns = summed.shape
    shape = (groups * block + DEC_PAD, heads * head)
    in_specs = [part_spec(x, 3) for x in xs]
    in_specs += [whole(other[0].shape) for _ in (*mine, *other)] + [whole(summed.shape)]
    in_specs += [
        pl.BlockSpec((groups, heads, head, head), lambda i, s: (0, s[0], 0, 0)),
        whole(gain.shape),
        pl.BlockSpec(memory_space=pltpu.SMEM),
    ]
    in_specs += [pl.BlockSpec(memory_space=pl.ANY)] * len(blocks)
    passed = (2, *blocks[0].shape)
    out = jax.ShapeDtypeStruct(shape, jnp.bfloat16)
    return pl.pallas_call(
        lambda *refs: attend_kernel(dims, *refs),
        grid_spec=pltpu.PrefetchScalarGridSpec(
            num_scalar_prefetch=1,
            grid=(1,),
            in_specs=in_specs,
            out_specs=[whole(shape), whole(shape), pl.BlockSpec(memory_space=pl.ANY)],
            scratch_shapes=[
                pltpu.VMEM((rows, columns), jnp.bfloat16),
                pltpu.VMEM(passed, jnp.bfloat16),
                pltpu.SemaphoreType.DMA((3,)),
            ],
        ),
        out_shape=[out, out, jax.ShapeDtypeStruct(passed, jnp.bfloat16)],
        compiler_params=params(),
        cost_estimate=pl.CostEstimate(
            flops=2 * rows * columns * xs[0].shape[2] * 2, bytes_accessed=4 * rows * columns, transcendentals=0
        ),
        name="attend",
    )(scalars, *xs, *mine, *other, summed, prior, gain, lengths, *blocks)


def lay_kernel(scalars, *refs):
    groups, passed, out_ref, sems = (refs[:3], refs[3:6]), refs[6], refs[7], refs[8]
    depth, wide = passed.shape[3:]

    def copy(i, slot, part, source):
        at = 4 * (i % 2) + 2 * (i // 2) + part
        target = out_ref.at[pl.ds(slot * depth, depth), pl.ds(at * wide, wide)]
        return pltpu.make_async_copy(source, target, sems.at[i, slot, part])

    every = [(i, slot, part) for i in range(4) for slot in range(2) for part in range(2)]
    for near in range(2):
        for same in range(2):

            @pl.when((scalars[1] == near) & (scalars[2] == same))
            def _(near=near, same=same):
                for i, slot, part in every:
                    source = passed.at[i // 2] if i % 2 else groups[1 - near][i // 2 + 1 - same]
                    plane = jnp.bitwise_xor(scalars[3], slot)
                    copy(i, slot, part, source.at[plane, part]).start()

    for i, slot, part in every:
        copy(i, slot, part, passed.at[0, 0, 0]).wait()


def lay(scalars, *blocks):
    depth, wide = blocks[0].shape[2:]
    shape = (2 * depth, 8 * wide)
    return pl.pallas_call(
        lay_kernel,
        grid_spec=pltpu.PrefetchScalarGridSpec(
            num_scalar_prefetch=1,
            grid=(1,),
            in_specs=[pl.BlockSpec(memory_space=pl.ANY)] * len(blocks),
            out_specs=whole(shape),
            scratch_shapes=[pltpu.SemaphoreType.DMA((4, 2, 2))],
        ),
        out_shape=jax.ShapeDtypeStruct(shape, jnp.bfloat16),
        compiler_params=params(),
        name="lay",
    )(scalars, *blocks)


def combine_kernel(last, scalars, *refs):
    hidden, weights_ref, refs = refs[:4], refs[4], refs[5:]
    rows, sems = refs[-2:]
    wide = hidden[0].shape[1]

    def copy(i, j):
        part = scalars[0] if j == 0 else 1 - scalars[0]
        at = pl.ds(pl.multiple_of((2 * i + part) * wide, wide), wide)
        return pltpu.make_async_copy(hidden[2 * i + j], rows.at[:, at], sems.at[i, j])

    every = [(i, j) for i in range(2) for j in range(2)]
    for i, j in every:
        copy(i, j).start()
    for i, j in every:
        copy(i, j).wait()
    total = lax.dot_general(
        rows[...], weights_ref[...], (((1,), (1,)), ((), ())), preferred_element_type=jnp.float32
    )
    if not last:
        refs[0][...] = total
        return
    sum_ref, res_ref, dec_res_ref, out_ref, dec_ref = refs[:5]
    total = sum_ref[...] + total
    groups, block = out_ref.shape[:2]
    for r in range(groups):
        out_ref[r] = (res_ref[r].astype(jnp.float32) + total[r * block : (r + 1) * block]).astype(jnp.bfloat16)
    for step in range(dec_ref.shape[0]):
        at = groups * block + step * groups
        dec_ref[step] = (dec_res_ref[step].astype(jnp.float32) + total[at : at + groups]).astype(jnp.bfloat16)


def combine(scalars, hidden, weights, core, *rest):
    rows, columns = hidden[0].shape[0], weights.shape[0]
    half = weights.shape[1] // 2
    out_shape = [jax.ShapeDtypeStruct((rows, columns), jnp.float32)]
    if rest:
        out_shape = [jax.ShapeDtypeStruct(res.shape, jnp.bfloat16) for res in rest[1:]]
    return pl.pallas_call(
        lambda *refs: combine_kernel(bool(rest), *refs),
        grid_spec=pltpu.PrefetchScalarGridSpec(
            num_scalar_prefetch=1,
            grid=(1,),
            in_specs=[pl.BlockSpec(memory_space=pl.ANY)] * len(hidden)
            + [pl.BlockSpec((columns, half), lambda i, s: (0, core))]
            + [whole(array.shape) for array in rest],
            out_specs=[whole(out.shape) for out in out_shape],
            scratch_shapes=[pltpu.VMEM((rows, half), jnp.bfloat16), pltpu.SemaphoreType.DMA((2, 2))],
        ),
        out_shape=out_shape,
        compiler_params=params(),
        name="combine",
    )(scalars, *hidden, weights, *rest)


def local_grid(
    spikes, dec_spikes, thresholds, in_scale, qkv_weight, out_weight, head_gain, prior_state, lengths
):
    groups, block, width = spikes.shape
    steps = dec_spikes.shape[0]
    all_heads, head = head_gain.shape
    heads = all_heads // 2
    planes = lax.axis_size("rep")
    c, t, z = (lax.axis_index(name) for name in AXES)
    parity = t & 1
    y = t >> 1
    is_end = (z == 0) | (z == planes - 1)
    end = is_end.astype(jnp.int32)
    third = jnp.where(is_end, z ^ 2, z ^ 3)
    fourth = jnp.where(is_end, z ^ 3, z ^ 2)
    near_used = (z >> 1) == parity
    scalars = jnp.stack([c, end, parity, z, z ^ 1, third, fourth, near_used, c == y]).astype(jnp.int32)

    def meet(c, t, r):
        return (1 - c, t, r) if c == t // 2 else (c, t ^ 2, r)

    def corner(c, t, r):
        return None if c == t // 2 else (1 - c, t ^ 2, r)

    kept, given = split(scalars, qkv_weight, out_weight.T)
    pair_kept = move(kept, to_pair, "pair_kept")
    mid1_kept = move(kept, mid_swap, "mid1_kept")
    other = move(given, to_ctx, "pre_w")

    counts = spikes.reshape(groups * block, width)
    own_x = embed(counts, thresholds, in_scale, planes, block // 4)
    given_x = lax.dynamic_slice_in_dim(own_x, parity * block, block, 1)

    first_x = move(after(given_x, other), to_ctx, "x_ctx")

    pair_other = move(after(other, given_x), to_pair, "pair_other")
    mid1_other = move(after(other, given_x), mid_swap, "mid1_other")
    stage = (pair_kept, mid1_kept, other, given_x)
    mid2_kept = move(after(pair_kept, *stage), mid_swap, "mid2_kept")
    end1_kept = move(after(mid1_kept, pair_other, mid1_other, *stage), mid_to_end, "end1_kept")
    dec_x = embed_steps(after(dec_spikes, *stage), thresholds, in_scale, planes)

    near_blocks = jnp.stack([after(kept, *stage)[3:], pair_kept[3:]])

    stage = (mid2_kept, end1_kept, pair_other, mid1_other, first_x, near_blocks, dec_x)
    end2_kept = move(after(mid2_kept, near_blocks, dec_x), mid_to_end, "end2_kept")
    mid2_other = move(after(pair_other, *stage), mid_swap, "mid2_other")
    end1_other = move(after(mid1_other, mid2_other), mid_to_end, "end1_other")
    third_kept = jnp.where(is_end, after(end1_kept, *stage), mid1_kept)
    second_x = move(after(first_x, third_kept), to_core, "x_core")
    xs = (own_x, first_x, second_x, dec_x)
    summed = project(scalars, 0, xs, (kept, pair_kept), (other, pair_other), None)

    def carry(blocks, name):
        return blocks, move(blocks, meet, name + "_meet"), move(blocks, corner, name + "_corner")

    near = carry(after(near_blocks, third_kept), "near")

    columns = width // lax.axis_size("tp")

    def gate(rows):
        part = lax.dynamic_slice_in_dim(rows, t * columns, columns, 2)
        level = lax.dynamic_slice_in_dim(thresholds, t * columns, columns, 0)
        scale = lax.dynamic_slice_in_dim(in_scale, t * columns, columns, 0)
        return (jnp.where(part >= level, part, 0).astype(jnp.float32) * scale).astype(jnp.bfloat16)

    res, dec_res = gate(after(spikes, second_x)), gate(after(dec_spikes, second_x))
    fourth_kept = jnp.where(is_end, end2_kept, mid2_kept)
    far = carry(after(jnp.stack([third_kept[3:], fourth_kept[3:]]), near[1], near[2]), "far")
    stage = (mid2_other, end1_other, summed, res, dec_res)
    end2_other = move(after(mid2_other, fourth_kept), mid_to_end, "end2_other")
    third_other = jnp.where(is_end, after(end1_other, *stage), mid1_other)
    summed = project(scalars, 2, xs, (third_kept,), (third_other,), summed)
    gain = lax.dynamic_slice_in_dim(head_gain, c * heads, heads, 0)

    flags = jnp.stack([c, near_used, c == y, jnp.where(near_used, z & 1, z >> 1)]).astype(jnp.int32)
    dims = (groups, block, heads, head, steps)
    own_rows, far_rows, passed = attend(
        scalars, xs, (fourth_kept,), (mid2_other, end2_other), summed, prior_state, gain, lengths, near + far, dims
    )
    h_ctx = move(far_rows, to_ctx, "h_ctx")
    h_y = move(own_rows, to_y, "h_y")
    h_diag = move(far_rows, to_diagonal, "h_diag")
    mine = [own_rows, h_ctx, h_y, h_diag]
    weights = lay(flags, *near, *far, move(passed, to_core, "out_core"))
    mine = [own_rows, h_ctx, h_y, h_diag]
    sibling = [move(m, to_core, "h_core") for m in after_all(mine, weights)]
    (partial,) = combine(flags, mine, weights, 0)
    return tuple(combine(flags, sibling, weights, 1, partial, res, dec_res))


def solution(mesh):
    return jax.shard_map(
        local_grid if fits(mesh) else local_any,
        mesh=mesh,
        in_specs=(
            P("rep", "ctx", None),
            P(None, "rep", None),
            P(),
            P(),
            P(None, ("ctx", "rep"), "tp"),
            P("tp", ("ctx", "rep")),
            P("tp", None),
            P("rep", "tp", None, None),
            P("rep"),
        ),
        out_specs=(P("rep", "ctx", "tp"), P(None, "rep", "tp")),
        check_vma=False,
    )
```

```python
import jax
import jax.numpy as jnp
from jax import lax
from jax.experimental import pallas as pl
from jax.experimental.pallas import tpu as pltpu
from jax.sharding import PartitionSpec as P


def carried_in(value, axis, combine, identity):
    peers, here = (lax.axis_size(axis), lax.axis_index(axis))
    everything = lax.all_gather(value, axis)
    start = jnp.broadcast_to(jnp.asarray(identity, value.dtype), value.shape)

    def turn(k, before):
        reached = k < here
        new = combine(before, everything[k])
        return jnp.where(reached, new, before)

    return lax.fori_loop(0, peers, turn, start)


def normalize(value_rows, gain):
    mean = jnp.mean(value_rows * value_rows, axis=-1, keepdims=True)
    return (value_rows * lax.rsqrt(mean + 1e-06) * gain).astype(jnp.bfloat16)


def local_any(
    spikes,
    dec_spikes,
    thresholds,
    in_scale,
    qkv_weight,
    out_weight,
    head_gain,
    prior_state,
    lengths,
):
    groups, block, width = spikes.shape
    steps = dec_spikes.shape[0]
    heads, head = head_gain.shape
    inner = heads * head
    prompt_rows = groups * block
    topmost_precision = lax.Precision.HIGHEST
    context_position = lax.axis_index("ctx")
    tokens_x = (jnp.where(spikes >= thresholds, spikes, 0).astype(jnp.float32) * in_scale).astype(
        jnp.bfloat16
    )
    dec_x = (
        jnp.where(dec_spikes >= thresholds, dec_spikes, 0).astype(jnp.float32) * in_scale
    ).astype(jnp.bfloat16)
    rows_all = jnp.concatenate(
        [tokens_x.reshape(prompt_rows, width), dec_x.reshape(steps * groups, width)], 0
    )
    full = lax.all_gather(qkv_weight, ("ctx", "rep"), axis=1, tiled=True)
    projected = jnp.einsum("rd,cde->rce", rows_all, full, preferred_element_type=jnp.float32)
    projected = projected.astype(jnp.bfloat16)
    prompt = projected[:prompt_rows].reshape(groups, block, 3, heads, head)
    decoded = projected[prompt_rows:].reshape(steps, groups, 3, heads, head)
    query = prompt[:, :, 0]
    value_rows = prompt[:, :, 2]
    positions = context_position * block + jnp.arange(block)
    live = positions[None, :] < lengths[:, None]
    keys = jnp.where(live[:, :, None, None], prompt[:, :, 1], jnp.zeros_like(prompt[:, :, 1]))
    block_state = jnp.einsum(
        "gthk,gthv->ghkv", keys, value_rows, preferred_element_type=jnp.float32
    )
    before = carried_in(
        block_state, "ctx", lambda earlier, later: earlier + later, jnp.zeros_like(block_state)
    )
    carried = (prior_state + before).astype(jnp.bfloat16)
    inter = jnp.einsum("gthk,ghkv->gthv", query, carried, preferred_element_type=jnp.float32)
    scores = jnp.einsum("gthk,gshk->ghts", query, keys, preferred_element_type=jnp.float32)
    causal = jnp.arange(block)[:, None] >= jnp.arange(block)[None, :]
    weights = jnp.where(causal, scores, 0.0).astype(jnp.bfloat16)
    intra = jnp.einsum("ghts,gshv->gthv", weights, value_rows, preferred_element_type=jnp.float32)
    hidden = normalize(inter + intra, head_gain).reshape(prompt_rows, inner)
    dec_query = decoded[:, :, 0].astype(jnp.float32)
    dec_keys = decoded[:, :, 1].astype(jnp.float32)
    dec_values = decoded[:, :, 2].astype(jnp.float32)
    state_readouts = []
    memory_state = prior_state + lax.psum(block_state, "ctx")
    for decode_step_body in range(steps):
        memory_state = memory_state + jnp.einsum(
            "ghk,ghv->ghkv",
            dec_keys[decode_step_body],
            dec_values[decode_step_body],
            precision=topmost_precision,
        )
        state_readouts.append(
            jnp.einsum(
                "ghk,ghkv->ghv",
                dec_query[decode_step_body],
                memory_state,
                precision=topmost_precision,
            )
        )
    dec_hidden = normalize(jnp.stack(state_readouts), head_gain).reshape(steps * groups, inner)
    hidden_all = jnp.concatenate([hidden, dec_hidden], 0)
    columns = width // lax.axis_size("tp")
    residual = lax.dynamic_slice_in_dim(rows_all, lax.axis_index("tp") * columns, columns, 1)
    terms = jnp.dot(
        hidden_all,
        lax.all_gather(out_weight, ("ctx", "rep"), axis=1, tiled=True),
        preferred_element_type=jnp.float32,
    )
    summed = lax.psum_scatter(terms, "tp", scatter_dimension=1, tiled=True)
    result = (residual.astype(jnp.float32) + summed).astype(jnp.bfloat16)
    block_out = result[:prompt_rows].reshape(groups, block, columns)
    decode_out = result[prompt_rows:].reshape(steps, groups, columns)
    return (block_out, decode_out)


AXES = ("ctx", "tp", "rep")
VMEM_LIMIT = 24 * 1024 * 1024
DEC_PAD = 16


def fits(mesh):
    shape = dict(mesh.shape)
    return (shape["ctx"], shape["tp"], shape["rep"]) == (2, 4, 4)


def move(value, target, name="move"):
    sizes = [lax.axis_size(name) for name in AXES]
    pairs = []
    for c in range(sizes[0]):
        for t in range(sizes[1]):
            for r in range(sizes[2]):
                to = target(c, t, r)
                if to is not None:
                    at = (c * sizes[1] + t) * sizes[2] + r
                    pairs.append((at, (to[0] * sizes[1] + to[1]) * sizes[2] + to[2]))
    with jax.named_scope(name):
        return lax.ppermute(value, AXES, pairs)


def after(value, *earlier):
    return lax.optimization_barrier((value, *earlier))[0]


def after_all(values, *earlier):
    return lax.optimization_barrier((*values, *earlier))[: len(values)]


def to_ctx(c, t, r):
    return (1 - c, t, r)


def to_core(c, t, r):
    return (c, t ^ 1, r)


def to_y(c, t, r):
    return (c, t ^ 2, r)


def to_diagonal(c, t, r):
    return (1 - c, t ^ 2, r)


def to_pair(c, t, r):
    return (c, t, r ^ 1)


def mid_swap(c, t, r):
    return (c, t, 3 - r) if r in (1, 2) else None


def mid_to_end(c, t, r):
    return (c, t, r ^ 1) if r in (1, 2) else None


def params():
    return pltpu.CompilerParams(vmem_limit_bytes=VMEM_LIMIT)


def whole(shape):
    return pl.BlockSpec(shape, lambda *_: (0,) * len(shape))


def split_kernel(scalars, kept_in, given_in, out_in, kept_ref, given_ref):
    kinds = kept_in.shape[0]
    kept_ref[:kinds] = kept_in[...]
    given_ref[...] = given_in[...]
    wide = kept_ref.shape[2]
    for half in range(kept_ref.shape[0] - kinds):
        kept_ref[kinds + half] = out_in[:, half * wide : (half + 1) * wide]


def split(scalars, weight, out_weight):
    kinds, rows, columns = weight.shape
    wide = columns // 2
    half = (kinds, rows, wide)
    kept = (kinds + out_weight.shape[1] // wide, rows, wide)
    return pl.pallas_call(
        split_kernel,
        grid_spec=pltpu.PrefetchScalarGridSpec(
            num_scalar_prefetch=1,
            grid=(1,),
            in_specs=[
                pl.BlockSpec(half, lambda i, s: (0, 0, s[0])),
                pl.BlockSpec(half, lambda i, s: (0, 0, 1 - s[0])),
                whole(out_weight.shape),
            ],
            out_specs=[whole(kept), whole(half)],
        ),
        out_shape=[jax.ShapeDtypeStruct(kept, weight.dtype), jax.ShapeDtypeStruct(half, weight.dtype)],
        compiler_params=params(),
        name="split",
    )(scalars, weight, weight, out_weight)


def embed_kernel(parts, spikes_ref, thresholds_ref, scale_ref, out_ref):
    place(parts, spikes_ref[...], thresholds_ref, scale_ref, out_ref)


def embed_steps_kernel(parts, spikes_ref, thresholds_ref, scale_ref, out_ref):
    steps, groups, width = spikes_ref.shape
    rows = [spikes_ref[step] for step in range(steps)]
    rows.append(jnp.zeros((DEC_PAD - steps * groups, width), spikes_ref.dtype))
    place(parts, jnp.concatenate(rows, axis=0), thresholds_ref, scale_ref, out_ref)


def embed_steps(spikes, thresholds, scale, parts):
    width = spikes.shape[2]
    return pl.pallas_call(
        lambda *refs: embed_steps_kernel(parts, *refs),
        out_shape=jax.ShapeDtypeStruct((parts, DEC_PAD, width // parts), jnp.bfloat16),
        compiler_params=params(),
        name="embed_steps",
    )(spikes, thresholds, scale)


def place(parts, counts, thresholds_ref, scale_ref, out_ref):
    gated = jnp.where(counts >= thresholds_ref[...][None], counts, 0)
    x = (gated.astype(jnp.float32) * scale_ref[...][None]).astype(jnp.bfloat16)
    width = x.shape[1] // (2 * parts)
    for z in range(parts):
        first = x[:, z * width : (z + 1) * width]
        second = x[:, (parts + z) * width : (parts + z + 1) * width]
        out_ref[z] = jnp.concatenate([first, second], axis=1)


def embed(spikes, thresholds, scale, parts, tile):
    rows, width = spikes.shape
    return pl.pallas_call(
        lambda *refs: embed_kernel(parts, *refs),
        grid=(rows // tile,),
        in_specs=[
            pl.BlockSpec((tile, width), lambda i: (i, 0)),
            whole((width,)),
            whole((width,)),
        ],
        out_specs=pl.BlockSpec((parts, tile, width // parts), lambda i: (0, i, 0)),
        out_shape=jax.ShapeDtypeStruct((parts, rows, width // parts), jnp.bfloat16),
        compiler_params=params(),
        name="embed",
    )(spikes, thresholds, scale)


def weights_of(scalars, mine, other, index):
    def pick(refs):
        return refs[0][index] if len(refs) == 1 else jnp.where(scalars[1] == 1, refs[1][index], refs[0][index])

    own, far = pick(mine), pick(other)
    first = scalars[0] == 0
    return jnp.concatenate([jnp.where(first, own, far), jnp.where(first, far, own)], axis=0)


def row_blocks(x_refs):
    at = 0
    for ref in x_refs:
        rows = ref.shape[1]
        yield ref, at, rows
        at += rows


def project_kernel(steps, has_sum, scalars, *refs):
    x_refs, out_ref = refs[:4], refs[-1]
    mine, other = refs[4 : 4 + steps], refs[4 + steps : 4 + 2 * steps]
    for step in range(steps):

        @pl.when(pl.program_id(0) == step)
        def _(step=step):
            for index in range(3):
                weight = weights_of(scalars, mine[step : step + 1], other[step : step + 1], index)
                columns = slice(index * weight.shape[1], (index + 1) * weight.shape[1])
                for ref, at, rows in row_blocks(x_refs):
                    term = jnp.dot(ref[0], weight, preferred_element_type=jnp.float32)
                    if step or has_sum:
                        term = (out_ref if step else refs[-2])[at : at + rows, columns] + term
                    out_ref[at : at + rows, columns] = term


def part_spec(array, step):
    block = (1,) + array.shape[1:]
    return pl.BlockSpec(block, lambda i, scalars: (scalars[3 + step + i], 0, 0))


def project(scalars, first, xs, mine, other, summed):
    steps = len(mine)
    rows = sum(x.shape[1] for x in xs)
    columns = 3 * mine[0].shape[2]
    earlier = [] if summed is None else [summed]
    return pl.pallas_call(
        lambda *refs: project_kernel(steps, bool(earlier), *refs),
        grid_spec=pltpu.PrefetchScalarGridSpec(
            num_scalar_prefetch=1,
            grid=(steps,),
            in_specs=[part_spec(x, first) for x in xs]
            + [whole(other[0].shape) for _ in (*mine, *other)]
            + [whole(sums.shape) for sums in earlier],
            out_specs=whole((rows, columns)),
        ),
        out_shape=jax.ShapeDtypeStruct((rows, columns), jnp.float32),
        compiler_params=params(),
        name="project",
    )(scalars, *xs, *mine, *other, *earlier)


def attend_kernel(dims, scalars, *refs):
    own_x, first_x, second_x, dec_x, mine, other0, other1, sum_ref, prior_ref, gain_ref, lengths = refs[:11]
    sets, near_ref, far_ref, passed_ref, qkv, held, sems = (refs[11:14], refs[14:17]), *refs[17:]

    def copy(half, source):
        return pltpu.make_async_copy(source, held.at[half], sems.at[half])

    for near in range(2):
        for same in range(2):

            @pl.when((scalars[7] == near) & (scalars[8] == same))
            def _(near=near, same=same):
                for half in range(2):
                    copy(half, sets[near][half + 1 - same]).start()

    groups, block, heads, head, steps = dims
    for index in range(3):
        weight = weights_of(scalars, (mine,), (other0, other1), index)
        columns = slice(index * weight.shape[1], (index + 1) * weight.shape[1])
        for ref, at, rows in row_blocks((own_x, first_x, second_x, dec_x)):
            term = jnp.dot(ref[0], weight, preferred_element_type=jnp.float32)
            qkv[at : at + rows, columns] = (sum_ref[at : at + rows, columns] + term).astype(jnp.bfloat16)
    for half in range(2):
        copy(half, sets[0][0]).wait()
    give = pltpu.make_async_copy(held, passed_ref, sems.at[2])
    give.start()
    here = scalars[0]
    parity = scalars[2]
    wide = heads * head
    prompt = 2 * groups * block
    causal = lax.broadcasted_iota(jnp.int32, (block, block), 0) >= lax.broadcasted_iota(jnp.int32, (block, block), 1)
    position = lax.broadcasted_iota(jnp.int32, (block, head), 0)
    row = lax.broadcasted_iota(jnp.int32, (DEC_PAD, DEC_PAD), 0)
    column = lax.broadcasted_iota(jnp.int32, (DEC_PAD, DEC_PAD), 1)
    reach = (row % groups == column % groups) & (column <= row)
    exact = lax.Precision.HIGHEST
    inner = (((0,), (0,)), ((), ()))
    across = (((1,), (1,)), ((), ()))

    def finish(value, gain):
        mean = jnp.mean(value * value, axis=-1, keepdims=True)
        return (value * lax.rsqrt(mean + 1e-06) * gain).astype(jnp.bfloat16)

    for h in range(heads):
        cols = [slice(i * wide + h * head, i * wide + (h + 1) * head) for i in range(3)]
        gain = gain_ref[h : h + 1, :]
        dq = qkv[prompt : prompt + DEC_PAD, cols[0]]
        dk = qkv[prompt : prompt + DEC_PAD, cols[1]]
        dv = qkv[prompt : prompt + DEC_PAD, cols[2]].astype(jnp.float32)
        dq32 = dq.astype(jnp.float32)
        pairs = lax.dot_general(dq, dk, across, preferred_element_type=jnp.float32)
        read = jnp.dot(jnp.where(reach, pairs, 0.0), dv, precision=exact, preferred_element_type=jnp.float32)
        dec_group = lax.broadcasted_iota(jnp.int32, (DEC_PAD, head), 0) % groups
        for r in range(groups):
            prior = prior_ref[r, h]
            starts = (r * block, groups * block + pl.multiple_of((r ^ parity) * block, block))
            run = (here, 1 - here)
            keys, values, states = [], [], []
            for start, b in zip(starts, run):
                k = qkv[pl.ds(start, block), cols[1]]
                live = b * block + position < lengths[r]
                k = jnp.where(live, k, jnp.zeros_like(k))
                v = qkv[pl.ds(start, block), cols[2]]
                keys.append(k)
                values.append(v)
                states.append(lax.dot_general(k, v, inner, preferred_element_type=jnp.float32))
            before = (jnp.where(here == 1, states[1], 0.0), jnp.where(here == 0, states[0], 0.0))
            for side, out_ref in enumerate((near_ref, far_ref)):
                q = qkv[pl.ds(starts[side], block), cols[0]]
                carried = (prior + before[side]).astype(jnp.bfloat16)
                scores = lax.dot_general(q, keys[side], across, preferred_element_type=jnp.float32)
                weights = jnp.where(causal, scores, 0.0).astype(jnp.bfloat16)
                attended = jnp.dot(q, carried, preferred_element_type=jnp.float32) + jnp.dot(
                    weights, values[side], preferred_element_type=jnp.float32
                )
                out_ref[r * block : (r + 1) * block, h * head : (h + 1) * head] = finish(attended, gain)
            state = prior + (states[0] + states[1])
            inter = jnp.dot(dq32, state, precision=exact, preferred_element_type=jnp.float32)
            read = read + jnp.where(dec_group == r, inter, 0.0)
        done = finish(read, gain)
        near_ref[groups * block :, h * head : (h + 1) * head] = done
        far_ref[groups * block :, h * head : (h + 1) * head] = done
    give.wait()


def attend(scalars, xs, mine, other, summed, prior, gain, lengths, blocks, dims):
    groups, block, heads, head, _ = dims
    rows, columns = summed.shape
    shape = (groups * block + DEC_PAD, heads * head)
    in_specs = [part_spec(x, 3) for x in xs]
    in_specs += [whole(other[0].shape) for _ in (*mine, *other)] + [whole(summed.shape)]
    in_specs += [
        pl.BlockSpec((groups, heads, head, head), lambda i, s: (0, s[0], 0, 0)),
        whole(gain.shape),
        pl.BlockSpec(memory_space=pltpu.SMEM),
    ]
    in_specs += [pl.BlockSpec(memory_space=pl.ANY)] * len(blocks)
    passed = (2, *blocks[0].shape)
    out = jax.ShapeDtypeStruct(shape, jnp.bfloat16)
    return pl.pallas_call(
        lambda *refs: attend_kernel(dims, *refs),
        grid_spec=pltpu.PrefetchScalarGridSpec(
            num_scalar_prefetch=1,
            grid=(1,),
            in_specs=in_specs,
            out_specs=[whole(shape), whole(shape), pl.BlockSpec(memory_space=pl.ANY)],
            scratch_shapes=[
                pltpu.VMEM((rows, columns), jnp.bfloat16),
                pltpu.VMEM(passed, jnp.bfloat16),
                pltpu.SemaphoreType.DMA((3,)),
            ],
        ),
        out_shape=[out, out, jax.ShapeDtypeStruct(passed, jnp.bfloat16)],
        compiler_params=params(),
        cost_estimate=pl.CostEstimate(
            flops=2 * rows * columns * xs[0].shape[2] * 2, bytes_accessed=4 * rows * columns, transcendentals=0
        ),
        name="attend",
    )(scalars, *xs, *mine, *other, summed, prior, gain, lengths, *blocks)


def lay_kernel(scalars, *refs):
    groups, passed, out_ref, sems = (refs[:3], refs[3:6]), refs[6], refs[7], refs[8]
    depth, wide = passed.shape[3:]

    def copy(i, slot, part, source):
        at = 4 * (i % 2) + 2 * (i // 2) + part
        target = out_ref.at[pl.ds(slot * depth, depth), pl.ds(at * wide, wide)]
        return pltpu.make_async_copy(source, target, sems.at[i, slot, part])

    every = [(i, slot, part) for i in range(4) for slot in range(2) for part in range(2)]
    for near in range(2):
        for same in range(2):

            @pl.when((scalars[1] == near) & (scalars[2] == same))
            def _(near=near, same=same):
                for i, slot, part in every:
                    source = passed.at[i // 2] if i % 2 else groups[1 - near][i // 2 + 1 - same]
                    plane = jnp.bitwise_xor(scalars[3], slot)
                    copy(i, slot, part, source.at[plane, part]).start()

    for i, slot, part in every:
        copy(i, slot, part, passed.at[0, 0, 0]).wait()


def lay(scalars, *blocks):
    depth, wide = blocks[0].shape[2:]
    shape = (2 * depth, 8 * wide)
    return pl.pallas_call(
        lay_kernel,
        grid_spec=pltpu.PrefetchScalarGridSpec(
            num_scalar_prefetch=1,
            grid=(1,),
            in_specs=[pl.BlockSpec(memory_space=pl.ANY)] * len(blocks),
            out_specs=whole(shape),
            scratch_shapes=[pltpu.SemaphoreType.DMA((4, 2, 2))],
        ),
        out_shape=jax.ShapeDtypeStruct(shape, jnp.bfloat16),
        compiler_params=params(),
        name="lay",
    )(scalars, *blocks)


def combine_kernel(last, scalars, *refs):
    hidden, weights_ref, refs = refs[:4], refs[4], refs[5:]
    rows, sems = refs[-2:]
    wide = hidden[0].shape[1]

    def copy(i, j):
        part = scalars[0] if j == 0 else 1 - scalars[0]
        at = pl.ds(pl.multiple_of((2 * i + part) * wide, wide), wide)
        return pltpu.make_async_copy(hidden[2 * i + j], rows.at[:, at], sems.at[i, j])

    every = [(i, j) for i in range(2) for j in range(2)]
    for i, j in every:
        copy(i, j).start()
    for i, j in every:
        copy(i, j).wait()
    total = lax.dot_general(
        rows[...], weights_ref[...], (((1,), (1,)), ((), ())), preferred_element_type=jnp.float32
    )
    if not last:
        refs[0][...] = total
        return
    sum_ref, res_ref, dec_res_ref, out_ref, dec_ref = refs[:5]
    total = sum_ref[...] + total
    groups, block = out_ref.shape[:2]
    for r in range(groups):
        out_ref[r] = (res_ref[r].astype(jnp.float32) + total[r * block : (r + 1) * block]).astype(jnp.bfloat16)
    for step in range(dec_ref.shape[0]):
        at = groups * block + step * groups
        dec_ref[step] = (dec_res_ref[step].astype(jnp.float32) + total[at : at + groups]).astype(jnp.bfloat16)


def combine(scalars, hidden, weights, core, *rest):
    rows, columns = hidden[0].shape[0], weights.shape[0]
    half = weights.shape[1] // 2
    out_shape = [jax.ShapeDtypeStruct((rows, columns), jnp.float32)]
    if rest:
        out_shape = [jax.ShapeDtypeStruct(res.shape, jnp.bfloat16) for res in rest[1:]]
    return pl.pallas_call(
        lambda *refs: combine_kernel(bool(rest), *refs),
        grid_spec=pltpu.PrefetchScalarGridSpec(
            num_scalar_prefetch=1,
            grid=(1,),
            in_specs=[pl.BlockSpec(memory_space=pl.ANY)] * len(hidden)
            + [pl.BlockSpec((columns, half), lambda i, s: (0, core))]
            + [whole(array.shape) for array in rest],
            out_specs=[whole(out.shape) for out in out_shape],
            scratch_shapes=[pltpu.VMEM((rows, half), jnp.bfloat16), pltpu.SemaphoreType.DMA((2, 2))],
        ),
        out_shape=out_shape,
        compiler_params=params(),
        name="combine",
    )(scalars, *hidden, weights, *rest)


def local_grid(
    spikes, dec_spikes, thresholds, in_scale, qkv_weight, out_weight, head_gain, prior_state, lengths
):
    groups, block, width = spikes.shape
    steps = dec_spikes.shape[0]
    all_heads, head = head_gain.shape
    heads = all_heads // 2
    planes = lax.axis_size("rep")
    c, t, z = (lax.axis_index(name) for name in AXES)
    parity = t & 1
    y = t >> 1
    is_end = (z == 0) | (z == planes - 1)
    end = is_end.astype(jnp.int32)
    third = jnp.where(is_end, z ^ 2, z ^ 3)
    fourth = jnp.where(is_end, z ^ 3, z ^ 2)
    near_used = (z >> 1) == parity
    scalars = jnp.stack([c, end, parity, z, z ^ 1, third, fourth, near_used, c == y]).astype(jnp.int32)

    def meet(c, t, r):
        return (1 - c, t, r) if c == t // 2 else (c, t ^ 2, r)

    def corner(c, t, r):
        return None if c == t // 2 else (1 - c, t ^ 2, r)

    kept, given = split(scalars, qkv_weight, out_weight.T)
    pair_kept = move(kept, to_pair, "pair_kept")
    mid1_kept = move(kept, mid_swap, "mid1_kept")
    other = move(given, to_ctx, "pre_w")

    counts = spikes.reshape(groups * block, width)
    own_x = embed(counts, thresholds, in_scale, planes, block // 4)
    given_x = lax.dynamic_slice_in_dim(own_x, parity * block, block, 1)

    first_x = move(after(given_x, other), to_ctx, "x_ctx")

    pair_other = move(after(other, given_x), to_pair, "pair_other")
    mid1_other = move(after(other, given_x), mid_swap, "mid1_other")
    stage = (pair_kept, mid1_kept, other, given_x)
    mid2_kept = move(after(pair_kept, *stage), mid_swap, "mid2_kept")
    end1_kept = move(after(mid1_kept, pair_other, mid1_other, *stage), mid_to_end, "end1_kept")
    dec_x = embed_steps(after(dec_spikes, *stage), thresholds, in_scale, planes)

    near_blocks = jnp.stack([after(kept, *stage)[3:], pair_kept[3:]])

    stage = (mid2_kept, end1_kept, pair_other, mid1_other, first_x, near_blocks, dec_x)
    end2_kept = move(after(mid2_kept, near_blocks, dec_x), mid_to_end, "end2_kept")
    mid2_other = move(after(pair_other, *stage), mid_swap, "mid2_other")
    end1_other = move(after(mid1_other, mid2_other), mid_to_end, "end1_other")
    third_kept = jnp.where(is_end, after(end1_kept, *stage), mid1_kept)
    second_x = move(after(first_x, mid2_kept), to_core, "x_core")
    xs = (own_x, first_x, second_x, dec_x)
    summed = project(scalars, 0, xs, (kept, pair_kept), (other, pair_other), None)

    def carry(blocks, name):
        return blocks, move(blocks, meet, name + "_meet"), move(blocks, corner, name + "_corner")

    near = carry(after(near_blocks, third_kept), "near")

    columns = width // lax.axis_size("tp")

    def gate(rows):
        part = lax.dynamic_slice_in_dim(rows, t * columns, columns, 2)
        level = lax.dynamic_slice_in_dim(thresholds, t * columns, columns, 0)
        scale = lax.dynamic_slice_in_dim(in_scale, t * columns, columns, 0)
        return (jnp.where(part >= level, part, 0).astype(jnp.float32) * scale).astype(jnp.bfloat16)

    res, dec_res = gate(after(spikes, second_x)), gate(after(dec_spikes, second_x))
    fourth_kept = jnp.where(is_end, end2_kept, mid2_kept)
    far = carry(after(jnp.stack([third_kept[3:], fourth_kept[3:]]), near[1], near[2]), "far")
    stage = (mid2_other, end1_other, summed, res, dec_res)
    end2_other = move(after(mid2_other, fourth_kept), mid_to_end, "end2_other")
    third_other = jnp.where(is_end, after(end1_other, *stage), mid1_other)
    summed = project(scalars, 2, xs, (third_kept,), (third_other,), summed)
    gain = lax.dynamic_slice_in_dim(head_gain, c * heads, heads, 0)

    flags = jnp.stack([c, near_used, c == y, jnp.where(near_used, z & 1, z >> 1)]).astype(jnp.int32)
    dims = (groups, block, heads, head, steps)
    own_rows, far_rows, passed = attend(
        scalars, xs, (fourth_kept,), (mid2_other, end2_other), summed, prior_state, gain, lengths, near + far, dims
    )
    h_diag = move(far_rows, to_diagonal, "h_diag")
    h_ctx = move(far_rows, to_ctx, "h_ctx")
    h_y = move(own_rows, to_y, "h_y")
    mine = [own_rows, h_ctx, h_y, h_diag]
    weights = lay(flags, *near, *far, move(passed, to_core, "out_core"))
    mine = [own_rows, h_ctx, h_y, h_diag]
    sibling = [move(m, to_core, "h_core") for m in after_all(mine, weights)]
    (partial,) = combine(flags, mine, weights, 0)
    return tuple(combine(flags, sibling, weights, 1, partial, res, dec_res))


def solution(mesh):
    return jax.shard_map(
        local_grid if fits(mesh) else local_any,
        mesh=mesh,
        in_specs=(
            P("rep", "ctx", None),
            P(None, "rep", None),
            P(),
            P(),
            P(None, ("ctx", "rep"), "tp"),
            P("tp", ("ctx", "rep")),
            P("tp", None),
            P("rep", "tp", None, None),
            P("rep"),
        ),
        out_specs=(P("rep", "ctx", "tp"), P(None, "rep", "tp")),
        check_vma=False,
    )
```

```python
import jax
import jax.numpy as jnp
from jax import lax
from jax.experimental import pallas as pl
from jax.experimental.pallas import tpu as pltpu
from jax.sharding import PartitionSpec as P


def carried_in(value, axis, combine, identity):
    peers, here = (lax.axis_size(axis), lax.axis_index(axis))
    everything = lax.all_gather(value, axis)
    start = jnp.broadcast_to(jnp.asarray(identity, value.dtype), value.shape)

    def turn(k, before):
        reached = k < here
        new = combine(before, everything[k])
        return jnp.where(reached, new, before)

    return lax.fori_loop(0, peers, turn, start)


def normalize(value_rows, gain):
    mean = jnp.mean(value_rows * value_rows, axis=-1, keepdims=True)
    return (value_rows * lax.rsqrt(mean + 1e-06) * gain).astype(jnp.bfloat16)


def local_any(
    spikes,
    dec_spikes,
    thresholds,
    in_scale,
    qkv_weight,
    out_weight,
    head_gain,
    prior_state,
    lengths,
):
    groups, block, width = spikes.shape
    steps = dec_spikes.shape[0]
    heads, head = head_gain.shape
    inner = heads * head
    prompt_rows = groups * block
    topmost_precision = lax.Precision.HIGHEST
    context_position = lax.axis_index("ctx")
    tokens_x = (jnp.where(spikes >= thresholds, spikes, 0).astype(jnp.float32) * in_scale).astype(
        jnp.bfloat16
    )
    dec_x = (
        jnp.where(dec_spikes >= thresholds, dec_spikes, 0).astype(jnp.float32) * in_scale
    ).astype(jnp.bfloat16)
    rows_all = jnp.concatenate(
        [tokens_x.reshape(prompt_rows, width), dec_x.reshape(steps * groups, width)], 0
    )
    full = lax.all_gather(qkv_weight, ("ctx", "rep"), axis=1, tiled=True)
    projected = jnp.einsum("rd,cde->rce", rows_all, full, preferred_element_type=jnp.float32)
    projected = projected.astype(jnp.bfloat16)
    prompt = projected[:prompt_rows].reshape(groups, block, 3, heads, head)
    decoded = projected[prompt_rows:].reshape(steps, groups, 3, heads, head)
    query = prompt[:, :, 0]
    value_rows = prompt[:, :, 2]
    positions = context_position * block + jnp.arange(block)
    live = positions[None, :] < lengths[:, None]
    keys = jnp.where(live[:, :, None, None], prompt[:, :, 1], jnp.zeros_like(prompt[:, :, 1]))
    block_state = jnp.einsum(
        "gthk,gthv->ghkv", keys, value_rows, preferred_element_type=jnp.float32
    )
    before = carried_in(
        block_state, "ctx", lambda earlier, later: earlier + later, jnp.zeros_like(block_state)
    )
    carried = (prior_state + before).astype(jnp.bfloat16)
    inter = jnp.einsum("gthk,ghkv->gthv", query, carried, preferred_element_type=jnp.float32)
    scores = jnp.einsum("gthk,gshk->ghts", query, keys, preferred_element_type=jnp.float32)
    causal = jnp.arange(block)[:, None] >= jnp.arange(block)[None, :]
    weights = jnp.where(causal, scores, 0.0).astype(jnp.bfloat16)
    intra = jnp.einsum("ghts,gshv->gthv", weights, value_rows, preferred_element_type=jnp.float32)
    hidden = normalize(inter + intra, head_gain).reshape(prompt_rows, inner)
    dec_query = decoded[:, :, 0].astype(jnp.float32)
    dec_keys = decoded[:, :, 1].astype(jnp.float32)
    dec_values = decoded[:, :, 2].astype(jnp.float32)
    state_readouts = []
    memory_state = prior_state + lax.psum(block_state, "ctx")
    for decode_step_body in range(steps):
        memory_state = memory_state + jnp.einsum(
            "ghk,ghv->ghkv",
            dec_keys[decode_step_body],
            dec_values[decode_step_body],
            precision=topmost_precision,
        )
        state_readouts.append(
            jnp.einsum(
                "ghk,ghkv->ghv",
                dec_query[decode_step_body],
                memory_state,
                precision=topmost_precision,
            )
        )
    dec_hidden = normalize(jnp.stack(state_readouts), head_gain).reshape(steps * groups, inner)
    hidden_all = jnp.concatenate([hidden, dec_hidden], 0)
    columns = width // lax.axis_size("tp")
    residual = lax.dynamic_slice_in_dim(rows_all, lax.axis_index("tp") * columns, columns, 1)
    terms = jnp.dot(
        hidden_all,
        lax.all_gather(out_weight, ("ctx", "rep"), axis=1, tiled=True),
        preferred_element_type=jnp.float32,
    )
    summed = lax.psum_scatter(terms, "tp", scatter_dimension=1, tiled=True)
    result = (residual.astype(jnp.float32) + summed).astype(jnp.bfloat16)
    block_out = result[:prompt_rows].reshape(groups, block, columns)
    decode_out = result[prompt_rows:].reshape(steps, groups, columns)
    return (block_out, decode_out)


AXES = ("ctx", "tp", "rep")
VMEM_LIMIT = 24 * 1024 * 1024
DEC_PAD = 16


def fits(mesh):
    shape = dict(mesh.shape)
    return (shape["ctx"], shape["tp"], shape["rep"]) == (2, 4, 4)


def move(value, target, name="move"):
    sizes = [lax.axis_size(name) for name in AXES]
    pairs = []
    for c in range(sizes[0]):
        for t in range(sizes[1]):
            for r in range(sizes[2]):
                to = target(c, t, r)
                if to is not None:
                    at = (c * sizes[1] + t) * sizes[2] + r
                    pairs.append((at, (to[0] * sizes[1] + to[1]) * sizes[2] + to[2]))
    with jax.named_scope(name):
        return lax.ppermute(value, AXES, pairs)


def after(value, *earlier):
    return lax.optimization_barrier((value, *earlier))[0]


def after_all(values, *earlier):
    return lax.optimization_barrier((*values, *earlier))[: len(values)]


def to_ctx(c, t, r):
    return (1 - c, t, r)


def to_core(c, t, r):
    return (c, t ^ 1, r)


def to_y(c, t, r):
    return (c, t ^ 2, r)


def to_diagonal(c, t, r):
    return (1 - c, t ^ 2, r)


def to_pair(c, t, r):
    return (c, t, r ^ 1)


def mid_swap(c, t, r):
    return (c, t, 3 - r) if r in (1, 2) else None


def mid_to_end(c, t, r):
    return (c, t, r ^ 1) if r in (1, 2) else None


def params():
    return pltpu.CompilerParams(vmem_limit_bytes=VMEM_LIMIT)


def whole(shape):
    return pl.BlockSpec(shape, lambda *_: (0,) * len(shape))


def split_kernel(scalars, kept_in, given_in, out_in, kept_ref, given_ref):
    kinds = kept_in.shape[0]
    kept_ref[:kinds] = kept_in[...]
    given_ref[...] = given_in[...]
    wide = kept_ref.shape[2]
    for half in range(kept_ref.shape[0] - kinds):
        kept_ref[kinds + half] = out_in[:, half * wide : (half + 1) * wide]


def split(scalars, weight, out_weight):
    kinds, rows, columns = weight.shape
    wide = columns // 2
    half = (kinds, rows, wide)
    kept = (kinds + out_weight.shape[1] // wide, rows, wide)
    return pl.pallas_call(
        split_kernel,
        grid_spec=pltpu.PrefetchScalarGridSpec(
            num_scalar_prefetch=1,
            grid=(1,),
            in_specs=[
                pl.BlockSpec(half, lambda i, s: (0, 0, s[0])),
                pl.BlockSpec(half, lambda i, s: (0, 0, 1 - s[0])),
                whole(out_weight.shape),
            ],
            out_specs=[whole(kept), whole(half)],
        ),
        out_shape=[jax.ShapeDtypeStruct(kept, weight.dtype), jax.ShapeDtypeStruct(half, weight.dtype)],
        compiler_params=params(),
        name="split",
    )(scalars, weight, weight, out_weight)


def embed_kernel(parts, spikes_ref, thresholds_ref, scale_ref, out_ref):
    place(parts, spikes_ref[...], thresholds_ref, scale_ref, out_ref)


def embed_steps_kernel(parts, spikes_ref, thresholds_ref, scale_ref, out_ref):
    steps, groups, width = spikes_ref.shape
    rows = [spikes_ref[step] for step in range(steps)]
    rows.append(jnp.zeros((DEC_PAD - steps * groups, width), spikes_ref.dtype))
    place(parts, jnp.concatenate(rows, axis=0), thresholds_ref, scale_ref, out_ref)


def embed_steps(spikes, thresholds, scale, parts):
    width = spikes.shape[2]
    return pl.pallas_call(
        lambda *refs: embed_steps_kernel(parts, *refs),
        out_shape=jax.ShapeDtypeStruct((parts, DEC_PAD, width // parts), jnp.bfloat16),
        compiler_params=params(),
        name="embed_steps",
    )(spikes, thresholds, scale)


def place(parts, counts, thresholds_ref, scale_ref, out_ref):
    gated = jnp.where(counts >= thresholds_ref[...][None], counts, 0)
    x = (gated.astype(jnp.float32) * scale_ref[...][None]).astype(jnp.bfloat16)
    width = x.shape[1] // (2 * parts)
    for z in range(parts):
        first = x[:, z * width : (z + 1) * width]
        second = x[:, (parts + z) * width : (parts + z + 1) * width]
        out_ref[z] = jnp.concatenate([first, second], axis=1)


def embed(spikes, thresholds, scale, parts, tile):
    rows, width = spikes.shape
    return pl.pallas_call(
        lambda *refs: embed_kernel(parts, *refs),
        grid=(rows // tile,),
        in_specs=[
            pl.BlockSpec((tile, width), lambda i: (i, 0)),
            whole((width,)),
            whole((width,)),
        ],
        out_specs=pl.BlockSpec((parts, tile, width // parts), lambda i: (0, i, 0)),
        out_shape=jax.ShapeDtypeStruct((parts, rows, width // parts), jnp.bfloat16),
        compiler_params=params(),
        name="embed",
    )(spikes, thresholds, scale)


def weights_of(scalars, mine, other, index):
    def pick(refs):
        return refs[0][index] if len(refs) == 1 else jnp.where(scalars[1] == 1, refs[1][index], refs[0][index])

    own, far = pick(mine), pick(other)
    first = scalars[0] == 0
    return jnp.concatenate([jnp.where(first, own, far), jnp.where(first, far, own)], axis=0)


def row_blocks(x_refs):
    at = 0
    for ref in x_refs:
        rows = ref.shape[1]
        yield ref, at, rows
        at += rows


def project_kernel(steps, has_sum, scalars, *refs):
    x_refs, out_ref = refs[:4], refs[-1]
    mine, other = refs[4 : 4 + steps], refs[4 + steps : 4 + 2 * steps]
    for step in range(steps):

        @pl.when(pl.program_id(0) == step)
        def _(step=step):
            for index in range(3):
                weight = weights_of(scalars, mine[step : step + 1], other[step : step + 1], index)
                columns = slice(index * weight.shape[1], (index + 1) * weight.shape[1])
                for ref, at, rows in row_blocks(x_refs):
                    term = jnp.dot(ref[0], weight, preferred_element_type=jnp.float32)
                    if step or has_sum:
                        term = (out_ref if step else refs[-2])[at : at + rows, columns] + term
                    out_ref[at : at + rows, columns] = term


def part_spec(array, step):
    block = (1,) + array.shape[1:]
    return pl.BlockSpec(block, lambda i, scalars: (scalars[3 + step + i], 0, 0))


def project(scalars, first, xs, mine, other, summed):
    steps = len(mine)
    rows = sum(x.shape[1] for x in xs)
    columns = 3 * mine[0].shape[2]
    earlier = [] if summed is None else [summed]
    return pl.pallas_call(
        lambda *refs: project_kernel(steps, bool(earlier), *refs),
        grid_spec=pltpu.PrefetchScalarGridSpec(
            num_scalar_prefetch=1,
            grid=(steps,),
            in_specs=[part_spec(x, first) for x in xs]
            + [whole(other[0].shape) for _ in (*mine, *other)]
            + [whole(sums.shape) for sums in earlier],
            out_specs=whole((rows, columns)),
        ),
        out_shape=jax.ShapeDtypeStruct((rows, columns), jnp.float32),
        compiler_params=params(),
        name="project",
    )(scalars, *xs, *mine, *other, *earlier)


def attend_kernel(dims, scalars, *refs):
    own_x, first_x, second_x, dec_x, mine, other0, other1, sum_ref, prior_ref, gain_ref, lengths = refs[:11]
    sets, near_ref, far_ref, passed_ref, qkv, held, sems = (refs[11:14], refs[14:17]), *refs[17:]

    def copy(half, source):
        return pltpu.make_async_copy(source, held.at[half], sems.at[half])

    for near in range(2):
        for same in range(2):

            @pl.when((scalars[7] == near) & (scalars[8] == same))
            def _(near=near, same=same):
                for half in range(2):
                    copy(half, sets[near][half + 1 - same]).start()

    groups, block, heads, head, steps = dims
    for index in range(3):
        weight = weights_of(scalars, (mine,), (other0, other1), index)
        columns = slice(index * weight.shape[1], (index + 1) * weight.shape[1])
        for ref, at, rows in row_blocks((own_x, first_x, second_x, dec_x)):
            term = jnp.dot(ref[0], weight, preferred_element_type=jnp.float32)
            qkv[at : at + rows, columns] = (sum_ref[at : at + rows, columns] + term).astype(jnp.bfloat16)
    for half in range(2):
        copy(half, sets[0][0]).wait()
    give = pltpu.make_async_copy(held, passed_ref, sems.at[2])
    give.start()
    here = scalars[0]
    parity = scalars[2]
    wide = heads * head
    prompt = 2 * groups * block
    causal = lax.broadcasted_iota(jnp.int32, (block, block), 0) >= lax.broadcasted_iota(jnp.int32, (block, block), 1)
    position = lax.broadcasted_iota(jnp.int32, (block, head), 0)
    row = lax.broadcasted_iota(jnp.int32, (DEC_PAD, DEC_PAD), 0)
    column = lax.broadcasted_iota(jnp.int32, (DEC_PAD, DEC_PAD), 1)
    reach = (row % groups == column % groups) & (column <= row)
    exact = lax.Precision.HIGHEST
    inner = (((0,), (0,)), ((), ()))
    across = (((1,), (1,)), ((), ()))

    def finish(value, gain):
        mean = jnp.mean(value * value, axis=-1, keepdims=True)
        return (value * lax.rsqrt(mean + 1e-06) * gain).astype(jnp.bfloat16)

    for h in range(heads):
        cols = [slice(i * wide + h * head, i * wide + (h + 1) * head) for i in range(3)]
        gain = gain_ref[h : h + 1, :]
        dq = qkv[prompt : prompt + DEC_PAD, cols[0]]
        dk = qkv[prompt : prompt + DEC_PAD, cols[1]]
        dv = qkv[prompt : prompt + DEC_PAD, cols[2]].astype(jnp.float32)
        dq32 = dq.astype(jnp.float32)
        pairs = lax.dot_general(dq, dk, across, preferred_element_type=jnp.float32)
        read = jnp.dot(jnp.where(reach, pairs, 0.0), dv, precision=exact, preferred_element_type=jnp.float32)
        dec_group = lax.broadcasted_iota(jnp.int32, (DEC_PAD, head), 0) % groups
        for r in range(groups):
            prior = prior_ref[r, h]
            starts = (r * block, groups * block + pl.multiple_of((r ^ parity) * block, block))
            run = (here, 1 - here)
            keys, values, states = [], [], []
            for start, b in zip(starts, run):
                k = qkv[pl.ds(start, block), cols[1]]
                live = b * block + position < lengths[r]
                k = jnp.where(live, k, jnp.zeros_like(k))
                v = qkv[pl.ds(start, block), cols[2]]
                keys.append(k)
                values.append(v)
                states.append(lax.dot_general(k, v, inner, preferred_element_type=jnp.float32))
            before = (jnp.where(here == 1, states[1], 0.0), jnp.where(here == 0, states[0], 0.0))
            for side, out_ref in enumerate((near_ref, far_ref)):
                q = qkv[pl.ds(starts[side], block), cols[0]]
                carried = (prior + before[side]).astype(jnp.bfloat16)
                scores = lax.dot_general(q, keys[side], across, preferred_element_type=jnp.float32)
                weights = jnp.where(causal, scores, 0.0).astype(jnp.bfloat16)
                attended = jnp.dot(q, carried, preferred_element_type=jnp.float32) + jnp.dot(
                    weights, values[side], preferred_element_type=jnp.float32
                )
                out_ref[r * block : (r + 1) * block, h * head : (h + 1) * head] = finish(attended, gain)
            state = prior + (states[0] + states[1])
            inter = jnp.dot(dq32, state, precision=exact, preferred_element_type=jnp.float32)
            read = read + jnp.where(dec_group == r, inter, 0.0)
        done = finish(read, gain)
        near_ref[groups * block :, h * head : (h + 1) * head] = done
        far_ref[groups * block :, h * head : (h + 1) * head] = done
    give.wait()


def attend(scalars, xs, mine, other, summed, prior, gain, lengths, blocks, dims):
    groups, block, heads, head, _ = dims
    rows, columns = summed.shape
    shape = (groups * block + DEC_PAD, heads * head)
    in_specs = [part_spec(x, 3) for x in xs]
    in_specs += [whole(other[0].shape) for _ in (*mine, *other)] + [whole(summed.shape)]
    in_specs += [
        pl.BlockSpec((groups, heads, head, head), lambda i, s: (0, s[0], 0, 0)),
        whole(gain.shape),
        pl.BlockSpec(memory_space=pltpu.SMEM),
    ]
    in_specs += [pl.BlockSpec(memory_space=pl.ANY)] * len(blocks)
    passed = (2, *blocks[0].shape)
    out = jax.ShapeDtypeStruct(shape, jnp.bfloat16)
    return pl.pallas_call(
        lambda *refs: attend_kernel(dims, *refs),
        grid_spec=pltpu.PrefetchScalarGridSpec(
            num_scalar_prefetch=1,
            grid=(1,),
            in_specs=in_specs,
            out_specs=[whole(shape), whole(shape), pl.BlockSpec(memory_space=pl.ANY)],
            scratch_shapes=[
                pltpu.VMEM((rows, columns), jnp.bfloat16),
                pltpu.VMEM(passed, jnp.bfloat16),
                pltpu.SemaphoreType.DMA((3,)),
            ],
        ),
        out_shape=[out, out, jax.ShapeDtypeStruct(passed, jnp.bfloat16)],
        compiler_params=params(),
        cost_estimate=pl.CostEstimate(
            flops=2 * rows * columns * xs[0].shape[2] * 2, bytes_accessed=4 * rows * columns, transcendentals=0
        ),
        name="attend",
    )(scalars, *xs, *mine, *other, summed, prior, gain, lengths, *blocks)


def lay_kernel(scalars, *refs):
    groups, passed, out_ref, sems = (refs[:3], refs[3:6]), refs[6], refs[7], refs[8]
    depth, wide = passed.shape[3:]

    def copy(i, slot, part, source):
        at = 4 * (i % 2) + 2 * (i // 2) + part
        target = out_ref.at[pl.ds(slot * depth, depth), pl.ds(at * wide, wide)]
        return pltpu.make_async_copy(source, target, sems.at[i, slot, part])

    every = [(i, slot, part) for i in range(4) for slot in range(2) for part in range(2)]
    for near in range(2):
        for same in range(2):

            @pl.when((scalars[1] == near) & (scalars[2] == same))
            def _(near=near, same=same):
                for i, slot, part in every:
                    source = passed.at[i // 2] if i % 2 else groups[1 - near][i // 2 + 1 - same]
                    plane = jnp.bitwise_xor(scalars[3], slot)
                    copy(i, slot, part, source.at[plane, part]).start()

    for i, slot, part in every:
        copy(i, slot, part, passed.at[0, 0, 0]).wait()


def lay(scalars, *blocks):
    depth, wide = blocks[0].shape[2:]
    shape = (2 * depth, 8 * wide)
    return pl.pallas_call(
        lay_kernel,
        grid_spec=pltpu.PrefetchScalarGridSpec(
            num_scalar_prefetch=1,
            grid=(1,),
            in_specs=[pl.BlockSpec(memory_space=pl.ANY)] * len(blocks),
            out_specs=whole(shape),
            scratch_shapes=[pltpu.SemaphoreType.DMA((4, 2, 2))],
        ),
        out_shape=jax.ShapeDtypeStruct(shape, jnp.bfloat16),
        compiler_params=params(),
        name="lay",
    )(scalars, *blocks)


def combine_kernel(last, scalars, *refs):
    hidden, weights_ref, refs = refs[:4], refs[4], refs[5:]
    rows, sems = refs[-2:]
    wide = hidden[0].shape[1]

    def copy(i, j):
        part = scalars[0] if j == 0 else 1 - scalars[0]
        at = pl.ds(pl.multiple_of((2 * i + part) * wide, wide), wide)
        return pltpu.make_async_copy(hidden[2 * i + j], rows.at[:, at], sems.at[i, j])

    every = [(i, j) for i in range(2) for j in range(2)]
    for i, j in every:
        copy(i, j).start()
    for i, j in every:
        copy(i, j).wait()
    total = lax.dot_general(
        rows[...], weights_ref[...], (((1,), (1,)), ((), ())), preferred_element_type=jnp.float32
    )
    if not last:
        refs[0][...] = total
        return
    sum_ref, res_ref, dec_res_ref, out_ref, dec_ref = refs[:5]
    total = sum_ref[...] + total
    groups, block = out_ref.shape[:2]
    for r in range(groups):
        out_ref[r] = (res_ref[r].astype(jnp.float32) + total[r * block : (r + 1) * block]).astype(jnp.bfloat16)
    for step in range(dec_ref.shape[0]):
        at = groups * block + step * groups
        dec_ref[step] = (dec_res_ref[step].astype(jnp.float32) + total[at : at + groups]).astype(jnp.bfloat16)


def combine(scalars, hidden, weights, core, *rest):
    rows, columns = hidden[0].shape[0], weights.shape[0]
    half = weights.shape[1] // 2
    out_shape = [jax.ShapeDtypeStruct((rows, columns), jnp.float32)]
    if rest:
        out_shape = [jax.ShapeDtypeStruct(res.shape, jnp.bfloat16) for res in rest[1:]]
    return pl.pallas_call(
        lambda *refs: combine_kernel(bool(rest), *refs),
        grid_spec=pltpu.PrefetchScalarGridSpec(
            num_scalar_prefetch=1,
            grid=(1,),
            in_specs=[pl.BlockSpec(memory_space=pl.ANY)] * len(hidden)
            + [pl.BlockSpec((columns, half), lambda i, s: (0, core))]
            + [whole(array.shape) for array in rest],
            out_specs=[whole(out.shape) for out in out_shape],
            scratch_shapes=[pltpu.VMEM((rows, half), jnp.bfloat16), pltpu.SemaphoreType.DMA((2, 2))],
        ),
        out_shape=out_shape,
        compiler_params=params(),
        name="combine",
    )(scalars, *hidden, weights, *rest)


def local_grid(
    spikes, dec_spikes, thresholds, in_scale, qkv_weight, out_weight, head_gain, prior_state, lengths
):
    groups, block, width = spikes.shape
    steps = dec_spikes.shape[0]
    all_heads, head = head_gain.shape
    heads = all_heads // 2
    planes = lax.axis_size("rep")
    c, t, z = (lax.axis_index(name) for name in AXES)
    parity = t & 1
    y = t >> 1
    is_end = (z == 0) | (z == planes - 1)
    end = is_end.astype(jnp.int32)
    third = jnp.where(is_end, z ^ 2, z ^ 3)
    fourth = jnp.where(is_end, z ^ 3, z ^ 2)
    near_used = (z >> 1) == parity
    scalars = jnp.stack([c, end, parity, z, z ^ 1, third, fourth, near_used, c == y]).astype(jnp.int32)

    def meet(c, t, r):
        return (1 - c, t, r) if c == t // 2 else (c, t ^ 2, r)

    def corner(c, t, r):
        return None if c == t // 2 else (1 - c, t ^ 2, r)

    kept, given = split(scalars, qkv_weight, out_weight.T)
    pair_kept = move(kept, to_pair, "pair_kept")
    mid1_kept = move(kept, mid_swap, "mid1_kept")
    other = move(given, to_ctx, "pre_w")

    counts = spikes.reshape(groups * block, width)
    own_x = embed(counts, thresholds, in_scale, planes, block // 4)
    given_x = lax.dynamic_slice_in_dim(own_x, parity * block, block, 1)

    first_x = move(after(given_x, other), to_ctx, "x_ctx")

    pair_other = move(after(other, given_x), to_pair, "pair_other")
    mid1_other = move(after(other, given_x), mid_swap, "mid1_other")
    stage = (pair_kept, mid1_kept, other, given_x)
    mid2_kept = move(after(pair_kept, *stage), mid_swap, "mid2_kept")
    end1_kept = move(after(mid1_kept, pair_other, mid1_other, *stage), mid_to_end, "end1_kept")
    dec_x = embed_steps(after(dec_spikes, *stage), thresholds, in_scale, planes)

    near_blocks = jnp.stack([after(kept, *stage)[3:], pair_kept[3:]])

    stage = (mid2_kept, end1_kept, pair_other, mid1_other, first_x, near_blocks, dec_x)
    end2_kept = move(after(mid2_kept, near_blocks, dec_x), mid_to_end, "end2_kept")
    mid2_other = move(after(pair_other, *stage), mid_swap, "mid2_other")
    end1_other = move(after(mid1_other, mid2_other), mid_to_end, "end1_other")
    third_kept = jnp.where(is_end, after(end1_kept, *stage), mid1_kept)
    second_x = move(after(first_x, mid2_kept), to_core, "x_core")
    xs = (own_x, first_x, second_x, dec_x)
    summed = project(scalars, 0, xs, (kept, pair_kept), (other, pair_other), None)

    def carry(blocks, name):
        return blocks, move(blocks, meet, name + "_meet"), move(blocks, corner, name + "_corner")

    near = carry(after(near_blocks, first_x), "near")

    columns = width // lax.axis_size("tp")

    def gate(rows):
        part = lax.dynamic_slice_in_dim(rows, t * columns, columns, 2)
        level = lax.dynamic_slice_in_dim(thresholds, t * columns, columns, 0)
        scale = lax.dynamic_slice_in_dim(in_scale, t * columns, columns, 0)
        return (jnp.where(part >= level, part, 0).astype(jnp.float32) * scale).astype(jnp.bfloat16)

    res, dec_res = gate(after(spikes, mid2_other)), gate(after(dec_spikes, mid2_other))
    fourth_kept = jnp.where(is_end, end2_kept, mid2_kept)
    far = carry(after(jnp.stack([third_kept[3:], fourth_kept[3:]]), near[1], near[2]), "far")
    stage = (mid2_other, end1_other, summed, res, dec_res)
    end2_other = move(after(mid2_other, fourth_kept), mid_to_end, "end2_other")
    third_other = jnp.where(is_end, after(end1_other, *stage), mid1_other)
    summed = project(scalars, 2, xs, (third_kept,), (third_other,), summed)
    gain = lax.dynamic_slice_in_dim(head_gain, c * heads, heads, 0)

    flags = jnp.stack([c, near_used, c == y, jnp.where(near_used, z & 1, z >> 1)]).astype(jnp.int32)
    dims = (groups, block, heads, head, steps)
    own_rows, far_rows, passed = attend(
        scalars, xs, (fourth_kept,), (mid2_other, end2_other), summed, prior_state, gain, lengths, near + far, dims
    )
    h_diag = move(far_rows, to_diagonal, "h_diag")
    h_ctx = move(far_rows, to_ctx, "h_ctx")
    h_y = move(own_rows, to_y, "h_y")
    mine = [own_rows, h_ctx, h_y, h_diag]
    weights = lay(flags, *near, *far, move(passed, to_core, "out_core"))
    mine = [own_rows, h_ctx, h_y, h_diag]
    sibling = [move(m, to_core, "h_core") for m in after_all(mine, weights)]
    (partial,) = combine(flags, mine, weights, 0)
    return tuple(combine(flags, sibling, weights, 1, partial, res, dec_res))


def solution(mesh):
    return jax.shard_map(
        local_grid if fits(mesh) else local_any,
        mesh=mesh,
        in_specs=(
            P("rep", "ctx", None),
            P(None, "rep", None),
            P(),
            P(),
            P(None, ("ctx", "rep"), "tp"),
            P("tp", ("ctx", "rep")),
            P("tp", None),
            P("rep", "tp", None, None),
            P("rep"),
        ),
        out_specs=(P("rep", "ctx", "tp"), P(None, "rep", "tp")),
        check_vma=False,
    )
```
